128 devices in a mesh: grid: 32 (over x, y, core), basis: 4 (over z).
Axes of the slice: x: 4, y: 4, z: 4, core: 2. Of those that a mesh axis runs over, the one named last changes fastest.
Arguments:
- density: bfloat16 [64, 12, 128, 1408], P('grid', None, 'basis'), may hold values from -0.0078125 to 0.0078125
- basis_vals: bfloat16 [256, 256, 768], P('grid'), may hold values from -6 to 6
- kernel: float32 [256, 256], P('grid'), may hold values from -0.12 to -0.02
- starts: int32 [256], P('grid'), may hold values from 0 to 58, as said below
- counts: int32 [256], P('grid'), may hold values from 32 to 256
- pair_mask: int32 [64, 11], replicated, may hold values 0 or 1
Outputs:
- fock_response: float32 [64, 12, 128, 1408], P('grid', None, 'basis')
The draws below stay inside these ranges and needn't reach their ends.
Inputs may be any that keep to these rules, and one draw needn't show every extreme that they name: `starts`: the batches held by grid index g (batches g * 8 to g * 8 + 7) start between max(g * 2 - 5, 0) and min(g * 2 + 1, 58), both ends taken on every grid index.
All inputs are finite; a program needn't handle non-finite values.
Results may differ from the reference program's by a relative error of at most 0.0003.
Values may be sent and summed in bfloat16 or wider, within the bound.
A program may use at most 256 MiB of HBM per device.

```python
import jax
import jax.numpy as jnp
from jax import lax

BLOCK = 128
BLOCKS = 64
PERTS = 12
WINDOW = 6
POINTS = 256
BATCH_DEV = 8
REACH = 5
BAND = 11
BLK_DEV = 2
BATCHES = 256


def draw_starts(key, part):
    key = jax.random.fold_in(key, 11)
    batch_no = jnp.arange(BATCHES, dtype=jnp.int32)
    device = batch_no // BATCH_DEV
    slot_no = batch_no % BATCH_DEV
    lowest = jnp.maximum(device * BLK_DEV - REACH, 0)
    highest = jnp.minimum(device * BLK_DEV + BLK_DEV - 1, BLOCKS - WINDOW)
    picked = jax.random.randint(key, (BATCHES,), lowest, highest + 1)
    picked = jnp.where(slot_no == 0, lowest, jnp.where(slot_no == 1, highest, picked))
    return picked.astype(jnp.int32)


def draw_counts(key, part):
    key = jax.random.fold_in(key, 23)
    batch_no = jnp.arange(BATCHES, dtype=jnp.int32)
    slot_no = batch_no % BATCH_DEV
    picked = jax.random.randint(key, (BATCHES,), POINTS // 8, POINTS + 1)
    picked = jnp.where(slot_no == 2, POINTS, picked)
    return picked.astype(jnp.int32)


def place_ends(entries, rng, least, largest):
    longest = entries.shape.index(max(entries.shape))
    spots = []
    for shift in (0, 1):
        where = [jax.random.randint(jax.random.fold_in(rng, axis), (), 0, length) for axis, length in enumerate(entries.shape)]
        where[longest] = (where[longest] + shift) % entries.shape[longest]
        spots.append(tuple(where))
    return entries.at[spots[0]].set(least).at[spots[1]].set(largest)


def shard_levels(stream_key, extent, shards, smallest, top_value):
    loudness = 1.0
    for position, blocks in shards:
        heights = jax.random.uniform(jax.random.fold_in(jax.random.fold_in(stream_key, 6), position), (blocks,), jnp.float32, smallest / len(shards), top_value / len(shards))
        loudness = loudness * jnp.repeat(jnp.exp(heights), extent[position] // blocks).reshape((-1,) + (1,) * (len(extent) - 1 - position))
    return loudness


def centred(stream_key, dims, deviation, reach, pieces=(), kind=jnp.bfloat16):
    drawn = jax.random.normal(stream_key, dims, jnp.float32) * deviation
    if len(pieces) > 0:
        drawn = shard_levels(stream_key, dims, pieces, -0.22, 0.18) * drawn
    return jnp.clip(drawn, min=-reach, max=reach).astype(kind)


def setup_inputs(seed: int = 0) -> dict:
    splits = jax.random.split(jax.random.key(seed), 7)
    density = centred(splits[0], (BLOCKS, PERTS, BLOCK, BAND * BLOCK), (1.0 / (WINDOW * BLOCK)), 0.0078125, ((0, 32), (2, 4)))
    basis_vals = centred(splits[1], (BATCHES, POINTS, WINDOW * BLOCK), 1.0, 6.0, ((0, 32),))
    kernel = jnp.clip(-0.12 + 0.09999999776482582 * jax.random.uniform(splits[2], (BATCHES, POINTS), jnp.float32) ** shard_levels(splits[2], (BATCHES, POINTS), ((0, 32),), -0.2, 0.2), -0.12, -0.02)
    starts = draw_starts(jax.random.fold_in(splits[6], 71), 0)
    counts = draw_counts(jax.random.fold_in(splits[6], 71), 0)
    pair_mask = place_ends((jax.random.randint(splits[5], (BLOCKS, BAND), 0, 4) < 3).astype(jnp.int32), jax.random.fold_in(splits[5], 1), 0, 1)
    return dict(density=density, basis_vals=basis_vals, kernel=kernel, starts=starts, counts=counts, pair_mask=pair_mask)


def window_rows(dens_slab, mask_slab):
    column_parts = []
    for offset in range(WINDOW):
        lead_block = REACH - offset
        block_part = dens_slab[offset, :, :, lead_block * BLOCK:(lead_block + WINDOW) * BLOCK]
        keep_mask = jnp.repeat(mask_slab[offset, lead_block:lead_block + WINDOW], BLOCK)
        column_parts.append(block_part * keep_mask.astype(block_part.dtype)[None, None, :])
    stacked = jnp.stack(column_parts, axis=1)
    return stacked.reshape(PERTS, WINDOW * BLOCK, WINDOW * BLOCK)


def reference(density, basis_vals, kernel, starts, counts, pair_mask):
    positions = jnp.arange(POINTS, dtype=jnp.int32)
    highest = lax.Precision.HIGHEST

    def batch_fock(running, batch_data):
        phi_vals, start, count, kern_row = batch_data
        start = start.astype(jnp.int32)
        dens_slab = lax.dynamic_slice_in_dim(density, start, WINDOW, 0)
        mask_slab = lax.dynamic_slice_in_dim(pair_mask, start, WINDOW, 0)
        win_dens = window_rows(dens_slab, mask_slab).astype(jnp.float32)
        phi_wide = phi_vals.astype(jnp.float32)
        mixed_vals = jnp.einsum("pc,krc->kpr", phi_wide, win_dens, precision=highest)
        rho = jnp.sum(phi_wide[None] * mixed_vals, axis=2)
        live_points = (positions < count).astype(jnp.float32)
        potential = kern_row[None, :] * rho * live_points[None, :]
        weighted = potential[:, :, None] * phi_wide[None]
        fock_win = jnp.einsum("kpr,pc->krc", weighted, phi_wide, precision=highest)
        fock_win = fock_win.reshape(PERTS, WINDOW, BLOCK, WINDOW * BLOCK)
        for offset in range(WINDOW):
            lead_block = REACH - offset
            place_at = ((start + offset).astype(jnp.int32), jnp.int32(0), jnp.int32(0), jnp.int32(lead_block * BLOCK))
            present = lax.dynamic_slice(running, place_at, (1, PERTS, BLOCK, WINDOW * BLOCK))
            running = lax.dynamic_update_slice(running, present + fock_win[:, offset][None], place_at)
        return running, None

    running = jnp.zeros((BLOCKS, PERTS, BLOCK, BAND * BLOCK), jnp.float32)
    running, unused = lax.scan(batch_fock, running, (basis_vals, starts, counts, kernel))
    keep_mask = jnp.repeat(pair_mask, BLOCK, axis=1).astype(jnp.float32)
    return running * keep_mask[:, None, None, :]
```

```python
import functools

import jax
import jax.numpy as jnp
from jax import lax
from jax.experimental import pallas as pl
from jax.experimental.pallas import tpu as pltpu
from jax.sharding import PartitionSpec as P

BLOCK = 128
PERTS = 12
WINDOW = 6
POINTS = 256
REACH = 5
BAND = 11
COLS = WINDOW * BLOCK
WIDE = BAND * BLOCK
SLOTS = 6
MESH = pl.DeviceIdType.MESH
NT = (((1,), (1,)), ((), ()))


def one_hot(share, columns, first):
    rows = lax.broadcasted_iota(jnp.int32, (share, columns), 0)
    lanes = lax.broadcasted_iota(jnp.int32, (share, columns), 1)
    return jnp.where(lanes == rows + first, 1.0, 0.0).astype(jnp.bfloat16)


def density_kernel(
    chips, planes, batches, share,
    phi_ref, meta_ref, dens_ref, starts_ref, counts_ref, mask_ref, kern_ref,
    all_ref, meta_all_ref, pot_ref,
    phi_v, dens_v, far_v, left_v, left_far, meta_s, part, gathered, pot_v,
    own_sem, out_sem, core_s, core_r, y_s, y_r, z_s, z_r, c_s, c_r, m_s, m_r, f_sem, a_s, a_r, b_s, b_r,
):
    grid_pos, plane = lax.axis_index("grid"), lax.axis_index("basis")
    chip, core = grid_pos // 2, lax.rem(grid_pos, 2)
    half = batches // 2
    quarter = half // 2
    per_plane = batches // planes
    own_slot = 2 + core
    first = lax.rem(plane, 2) * half
    there = half - first
    rows_all = PERTS * share

    def device(slot, at_plane):
        return (2 * lax.rem(chip + slot // 2 - 1 + chips, chips) + lax.rem(slot, 2), at_plane)

    other = (2 * chip + 1 - core, plane)

    def remote(src, dst, send, recv, to):
        return pltpu.make_async_remote_copy(
            src_ref=src, dst_ref=dst, send_sem=send, recv_sem=recv, device_id=to, device_id_type=MESH)

    barrier = pltpu.get_barrier_semaphore()

    @pl.loop(0, SLOTS * planes)
    def _(no):
        slot, at_plane = no // planes, lax.rem(no, planes)

        @pl.when(jnp.logical_or(slot != own_slot, at_plane != plane))
        def _():
            pl.semaphore_signal(barrier, inc=1, device_id=device(slot, at_plane), device_id_type=MESH)

    pl.semaphore_wait(barrier, SLOTS * planes - 1)

    def piece(way, n):
        return n // 2 + quarter * lax.rem(n + way, 2)

    def y_copy(way, n):
        at = first + piece(way, n)
        return remote(phi_ref.at[at], phi_v.at[4 * way + core, at], y_s.at[way, n], y_r.at[way, n],
                      device(4 - 4 * way + core, plane))

    def z_copy(way, n):
        which = piece(way, n)
        where = phi_v.at[4 * way + core, first + which]
        to = lax.rem(plane + 1 - 2 * (which // quarter) + planes, planes)
        return remote(where, where, z_s.at[way, n], z_r.at[way, n], (grid_pos, to))

    def c_copy(way, m):
        at = jnp.where(m < half, first, there) + piece(way, lax.rem(m, half))
        where = phi_v.at[4 * way + core, at]
        return remote(where, where, c_s.at[way, m], c_r.at[way, m], other)

    def core_copy(no):
        return remote(phi_ref.at[no], phi_v.at[own_slot, no], core_s.at[no], core_r.at[no], other)

    def meta_copy(way, s):
        return remote(meta_ref, meta_all_ref.at[4 * way + core], m_s.at[1 + 2 * way + s], m_r.at[1 + 2 * way + core],
                      device(4 - 4 * way + s, plane))

    def out_copy(slot, no):
        return pltpu.make_async_copy(phi_v.at[slot, no], all_ref.at[slot, no], out_sem.at[slot, no])

    own_copy = pltpu.make_async_copy(phi_ref, phi_v.at[own_slot], own_sem.at[0])
    own_copy.start()
    far_copy = remote(dens_ref.at[core, :, :, pl.ds(pl.multiple_of(core * REACH * BLOCK, BLOCK), COLS)], left_far,
                      f_sem.at[0], f_sem.at[1], device(jnp.where(core == 0, 1, 4), plane))
    dens_copy = pltpu.make_async_copy(dens_ref, left_v, own_sem.at[1])
    dens_copy.start()
    core_meta = remote(meta_ref, meta_all_ref.at[own_slot], m_s.at[0], m_r.at[0], other)
    core_meta.start()
    for way in range(2):
        for s in range(2):
            meta_copy(way, s).start()
    own_meta = pltpu.make_async_copy(meta_ref, meta_all_ref.at[own_slot], own_sem.at[2])
    own_meta.start()

    @pl.loop(0, half)
    def _(n):
        for way in range(2):
            y_copy(way, n).start()

    far_copy.start()

    @pl.loop(0, batches)
    def _(no):
        core_copy(no).start()

    def masked(block, keep):
        return (block.astype(jnp.float32) * keep.astype(jnp.float32)).astype(block.dtype)

    def same(left, right):
        return (1 - jnp.minimum(jnp.abs(left - right), 1)).astype(jnp.float32)

    dens_copy.wait()
    for r in range(2):
        row = 2 * grid_pos + r
        for t in range(BAND):
            block = left_v[r, :, :, t * BLOCK:(t + 1) * BLOCK].reshape(rows_all, BLOCK)
            dens_v[r, t, :rows_all, :] = masked(block, mask_ref[row, t])
            dens_v[r, t, rows_all:, :] = one_hot(share, BLOCK, (REACH - t) * BLOCK + plane * share)
    far_v[rows_all:, :] = one_hot(share, COLS, core * REACH * BLOCK + plane * share)

    own_copy.wait()
    own_meta.wait()
    for no in range(5):
        pltpu.make_async_copy(meta_ref, meta_all_ref.at[own_slot], m_r.at[no]).wait()
    to_smem = pltpu.make_async_copy(meta_all_ref, meta_s, own_sem.at[3])
    to_smem.start()
    to_smem.wait()

    def reduced(mixed):
        picked = mixed[rows_all:rows_all + share]
        return jnp.sum(mixed[:rows_all].reshape(PERTS, share, POINTS) * picked[None], axis=1)

    def rho_part(slot, no):
        start = meta_s[slot, no, 0]
        phi = phi_v[slot, no]
        lhs, keeps = [], []
        for r in range(2):
            offset = 2 * grid_pos + r - start
            inside = jnp.clip(offset, 0, WINDOW - 1)
            keeps.append(same(offset, inside))
            lhs.append(jnp.concatenate([dens_v[r, REACH - inside + c] for c in range(WINDOW)], axis=1))
        total = None
        for r in range(2):
            mixed = lax.dot_general(lhs[r], phi, NT, preferred_element_type=jnp.float32)
            term = reduced(mixed) * keeps[r]
            total = term if total is None else total + term
        part[slot, no // per_plane, lax.rem(no, per_plane)] = total

    far_start = 4 * chip - 1

    def rho_far(slot, no):
        keep = same(meta_s[slot, no, 0], far_start)
        mixed = lax.dot_general(far_v[...], phi_v[slot, no], NT, preferred_element_type=jnp.float32)
        spot = part.at[slot, no // per_plane, lax.rem(no, per_plane)]
        spot[...] = spot[...] + reduced(mixed) * keep

    @pl.loop(0, batches)
    def _(no):
        out_copy(own_slot, no).start()
        rho_part(own_slot, no)

    @pl.loop(0, batches)
    def _(no):
        core_copy(no).wait_recv()
        out_copy(5 - own_slot, no).start()
        rho_part(5 - own_slot, no)

    def far_ready():
        far_copy.wait_recv()
        far_row = jnp.where(core == 0, jnp.maximum(2 * grid_pos - 1, 0), jnp.minimum(2 * grid_pos + 2, 2 * 2 * chips - 1))
        for t in range(WINDOW):
            block = left_far[:, :, t * BLOCK:(t + 1) * BLOCK].reshape(rows_all, BLOCK)
            far_v[:rows_all, t * BLOCK:(t + 1) * BLOCK] = masked(block, mask_ref[far_row, jnp.where(core == 0, REACH, 0) + t])

    @pl.loop(0, half + 2)
    def _(n):
        y_now = n < half
        z_now = jnp.logical_and(n >= 1, n <= half)
        cz_now = n >= 2

        @pl.when(y_now)
        def _():
            for way in range(2):
                y_copy(way, n).wait_recv()
                z_copy(way, n).start()
                c_copy(way, n).start()
                out_copy(4 * way + core, first + piece(way, n)).start()

        @pl.when(n == 0)
        def _():
            far_ready()

        @pl.when(z_now)
        def _():
            for way in range(2):
                z_copy(way, n - 1).wait_recv()
                c_copy(way, half + n - 1).start()
                out_copy(4 * way + core, there + piece(way, n - 1)).start()
            for way in range(2):
                c_copy(way, n - 1).wait_recv()
                out_copy(4 * way + 1 - core, first + piece(way, n - 1)).start()

        @pl.when(cz_now)
        def _():
            for way in range(2):
                c_copy(way, half + n - 2).wait_recv()
                out_copy(4 * way + 1 - core, there + piece(way, n - 2)).start()

        @pl.loop(0, 8)
        def _(item):
            kind, way = item // 2, lax.rem(item, 2)
            late = jnp.where(kind == 0, 0, jnp.where(kind == 3, 2, 1))
            came = n - late
            slot = 4 * way + jnp.where(kind <= 1, core, 1 - core)
            at = jnp.where(lax.rem(kind, 2) == 0, first, there) + piece(way, jnp.maximum(came, 0))

            @pl.when(jnp.logical_and(came >= 0, came < half))
            def _():
                rho_part(slot, at)

                @pl.when(jnp.logical_and(kind <= 1, way == 1 - core))
                def _():
                    rho_far(slot, at)

    def is_other(slot, at_plane):
        return jnp.logical_or(slot != own_slot, at_plane != plane)

    def part_copy(slot, at_plane):
        back = 2 * (2 - slot // 2) + core
        return remote(part.at[slot, at_plane], gathered.at[back, plane], a_s.at[slot, at_plane], a_r.at[back, plane],
                      device(slot, at_plane))

    def pot_copy(slot, at_plane):
        back = 2 * (2 - slot // 2) + core
        return remote(pot_v, pot_ref.at[back, plane], b_s.at[slot, at_plane], b_r.at[back, plane],
                      device(slot, at_plane))

    def for_others(act):
        @pl.loop(0, SLOTS * planes)
        def _(no):
            slot, at_plane = no // planes, lax.rem(no, planes)

            @pl.when(is_other(slot, at_plane))
            def _():
                act(slot, at_plane)

    for_others(lambda slot, at_plane: part_copy(slot, at_plane).start())
    gathered[own_slot, plane] = part[own_slot, plane]
    for_others(lambda slot, at_plane: pltpu.make_async_copy(
        part.at[0, 0], gathered.at[slot, at_plane], a_r.at[slot, at_plane]).wait())
    points = lax.broadcasted_iota(jnp.int32, (1, POINTS), 1)
    for no in range(per_plane):
        rho = gathered[0, 0, no]
        for slot in range(SLOTS):
            for at_plane in range(planes):
                if slot or at_plane:
                    rho = rho + gathered[slot, at_plane, no]
        mine = per_plane * plane + no
        live = jnp.clip(counts_ref[mine] - points, 0, 1).astype(jnp.float32)
        pot_v[no] = rho * (kern_ref[pl.ds(mine, 1), :] * live)
    for_others(lambda slot, at_plane: pot_copy(slot, at_plane).start())
    pot_own = pltpu.make_async_copy(pot_v, pot_ref.at[own_slot, plane], own_sem.at[0])
    pot_own.start()
    for_others(lambda slot, at_plane: pltpu.make_async_copy(
        pot_v, pot_ref.at[slot, at_plane], b_r.at[slot, at_plane]).wait())
    pot_own.wait()

    for_others(lambda slot, at_plane: part_copy(slot, at_plane).wait_send())
    for_others(lambda slot, at_plane: pot_copy(slot, at_plane).wait_send())
    far_copy.wait_send()
    core_meta.wait_send()
    for way in range(2):
        for s in range(2):
            meta_copy(way, s).wait_send()

    @pl.loop(0, batches)
    def _(no):
        core_copy(no).wait_send()
        for slot in range(SLOTS):
            out_copy(slot, no).wait()

    @pl.loop(0, half)
    def _(n):
        for way in range(2):
            y_copy(way, n).wait_send()
            z_copy(way, n).wait_send()
            c_copy(way, n).wait_send()
            c_copy(way, half + n).wait_send()


def potentials(phi, meta, density, starts, counts, pair_mask, kern, chips, planes):
    batches, points, cols = phi.shape
    share = density.shape[2]
    half, per_plane = batches // 2, batches // planes
    rows = PERTS * share + share
    far = pl.BlockSpec(memory_space=pl.ANY)
    smem = pl.BlockSpec(memory_space=pltpu.SMEM)
    vmem = pl.BlockSpec(memory_space=pltpu.VMEM)
    dma = pltpu.SemaphoreType.DMA
    f32 = jnp.float32
    small = (SLOTS, planes, per_plane, PERTS, points)
    return pl.pallas_call(
        functools.partial(density_kernel, chips, planes, batches, share),
        out_shape=(
            jax.ShapeDtypeStruct((SLOTS, batches, points, cols), phi.dtype),
            jax.ShapeDtypeStruct((SLOTS,) + meta.shape, meta.dtype),
            jax.ShapeDtypeStruct(small, f32),
        ),
        in_specs=[far, far, far, smem, smem, smem, vmem],
        out_specs=[far] * 3,
        scratch_shapes=[
            pltpu.VMEM((SLOTS, batches, points, cols), phi.dtype),
            pltpu.VMEM((2, BAND, rows, BLOCK), density.dtype),
            pltpu.VMEM((rows, COLS), density.dtype),
            pltpu.VMEM(density.shape, density.dtype),
            pltpu.VMEM((PERTS, share, COLS), density.dtype),
            pltpu.SMEM((SLOTS,) + meta.shape, meta.dtype),
            pltpu.VMEM(small, f32),
            pltpu.VMEM(small, f32),
            pltpu.VMEM((per_plane, PERTS, points), f32),
            dma((4,)), dma((SLOTS, batches)), dma((batches,)), dma((batches,)),
            dma((2, half)), dma((2, half)), dma((2, half)), dma((2, half)),
            dma((2, batches)), dma((2, batches)), dma((5,)), dma((5,)), dma((2,)),
            dma((SLOTS, planes)), dma((SLOTS, planes)), dma((SLOTS, planes)), dma((SLOTS, planes)),
        ],
        compiler_params=pltpu.CompilerParams(collective_id=0, has_side_effects=True, vmem_limit_bytes=56 << 20),
        cost_estimate=pl.CostEstimate(flops=17 * 10**9, bytes_accessed=50 * 10**6, transcendentals=0),
        name="potentials",
    )(phi, meta, density, starts, counts, pair_mask, kern)


def split_weights(pot, picked, share):
    weighted = (pot[:, None, :] * picked[None]).reshape(PERTS * share, POINTS)
    high = weighted.astype(jnp.bfloat16)
    low = (weighted - high.astype(jnp.float32)).astype(jnp.bfloat16)
    return high, low


def add_product(parts, phi, few, store):
    def product(points):
        left = jnp.concatenate(
            [jnp.concatenate([high[:, :points], low[:, :points]], axis=1) for high, low in parts], axis=0)
        right = phi[:points, :]
        store(jnp.dot(left, jnp.concatenate([right, right], axis=0), preferred_element_type=jnp.float32))

    @pl.when(few)
    def _():
        product(POINTS // 2)

    @pl.when(jnp.logical_not(few))
    def _():
        product(POINTS)


DEPTH = 4


def fock_kernel(batches, share, meta_ref, mask_ref, pot_ref, phi_ref, out_ref, chosen, buf, sems):
    grid_pos, plane = lax.axis_index("grid"), lax.axis_index("basis")
    base = 2 * grid_pos - REACH

    def note(no, count):
        lead = meta_ref[no // batches, lax.rem(no, batches), 0] - base
        near = jnp.logical_and(lead >= 0, lead <= REACH + 1)

        @pl.when(near)
        def _():
            chosen[count] = no

        return count + near.astype(jnp.int32)

    count = lax.fori_loop(0, SLOTS * batches, note, 0)

    def fetch(i):
        no = chosen[i]
        return pltpu.make_async_copy(
            phi_ref.at[no // batches, lax.rem(no, batches)], buf.at[lax.rem(i, DEPTH)], sems.at[lax.rem(i, DEPTH)])

    for i in range(DEPTH - 1):
        @pl.when(i < count)
        def _():
            fetch(i).start()

    out_ref[...] = jnp.zeros_like(out_ref)
    pick = one_hot(share, BLOCK, plane * share)

    @pl.loop(0, count)
    def _(i):
        fetch(i).wait()

        @pl.when(i + DEPTH - 1 < count)
        def _():
            fetch(i + DEPTH - 1).start()

        no = chosen[i]
        lead = meta_ref[no // batches, lax.rem(no, batches), 0] - base
        few = meta_ref[no // batches, lax.rem(no, batches), 1] <= POINTS // 2
        here = buf.at[lax.rem(i, DEPTH)]
        pot = pot_ref[no]

        def weights(offset):
            own = here[:, pl.ds(pl.multiple_of(offset * BLOCK, BLOCK), BLOCK)]
            picked = lax.dot_general(pick, own, NT, preferred_element_type=jnp.float32)
            return split_weights(pot, picked, share)

        def add(r, offset, value):
            spot = out_ref.at[r, :, :, pl.ds(pl.multiple_of((REACH - offset) * BLOCK, BLOCK), COLS)]
            spot[...] = spot[...] + value.reshape(PERTS, share, COLS)

        both = jnp.logical_and(lead >= 1, lead <= REACH)

        @pl.when(both)
        def _():
            offset = REACH - lead
            parts = [weights(offset), weights(offset + 1)]
            rows = PERTS * share

            def store(value):
                add(0, offset, value[:rows])
                add(1, offset + 1, value[rows:])

            add_product(parts, here, few, store)

        @pl.when(jnp.logical_not(both))
        def _():
            r = jnp.where(lead == 0, 0, 1)
            offset = jnp.where(lead == 0, REACH, 0)
            add_product([weights(offset)], here, few, lambda value: add(r, offset, value))

    for r in range(2):
        for t in range(BAND):
            @pl.when(mask_ref[2 * grid_pos + r, t] == 0)
            def _():
                out_ref[r, :, :, t * BLOCK:(t + 1) * BLOCK] = jnp.zeros((PERTS, share, BLOCK), jnp.float32)


def fock_own(meta_all, pair_mask, pot, phi_all, share):
    slots, batches, points, cols = phi_all.shape
    smem = pl.BlockSpec(memory_space=pltpu.SMEM)
    vmem = pl.BlockSpec(memory_space=pltpu.VMEM)
    return pl.pallas_call(
        functools.partial(fock_kernel, batches, share),
        out_shape=jax.ShapeDtypeStruct((2, PERTS, share, WIDE), jnp.float32),
        in_specs=[smem, smem, vmem, pl.BlockSpec(memory_space=pl.ANY)],
        out_specs=vmem,
        scratch_shapes=[
            pltpu.SMEM((slots * batches,), jnp.int32),
            pltpu.VMEM((DEPTH, points, cols), phi_all.dtype),
            pltpu.SemaphoreType.DMA((DEPTH,)),
        ],
        compiler_params=pltpu.CompilerParams(vmem_limit_bytes=56 << 20),
        cost_estimate=pl.CostEstimate(flops=20 * 10**9, bytes_accessed=20 * 10**6, transcendentals=0),
        name="fock_own",
    )(meta_all, pair_mask, pot, phi_all)


def far_kernel(batches, share, meta_ref, pot_ref, phi_ref, out_ref, buf, sem):
    grid_pos, plane = lax.axis_index("grid"), lax.axis_index("basis")
    core = lax.rem(grid_pos, 2)
    slot = jnp.where(core == 0, 4, 1)
    far_start = 4 * (grid_pos // 2) - 1
    out_ref[...] = jnp.zeros_like(out_ref)
    pick = one_hot(share, BLOCK, plane * share)

    @pl.loop(0, batches)
    def _(no):
        @pl.when(meta_ref[slot, no, 0] == far_start)
        def _():
            copy = pltpu.make_async_copy(phi_ref.at[slot, no], buf, sem)
            copy.start()
            copy.wait()
            own = buf[:, pl.ds(pl.multiple_of(core * REACH * BLOCK, BLOCK), BLOCK)]
            picked = lax.dot_general(pick, own, NT, preferred_element_type=jnp.float32)
            parts = [split_weights(pot_ref[slot * batches + no], picked, share)]

            def store(value):
                out_ref[...] += value.reshape(PERTS, share, COLS)

            add_product(parts, buf, meta_ref[slot, no, 1] <= POINTS // 2, store)


def fock_far(meta_all, pot, phi_all, share):
    slots, batches, points, cols = phi_all.shape
    smem = pl.BlockSpec(memory_space=pltpu.SMEM)
    vmem = pl.BlockSpec(memory_space=pltpu.VMEM)
    return pl.pallas_call(
        functools.partial(far_kernel, batches, share),
        out_shape=jax.ShapeDtypeStruct((PERTS, share, COLS), jnp.float32),
        in_specs=[smem, vmem, pl.BlockSpec(memory_space=pl.ANY)],
        out_specs=vmem,
        scratch_shapes=[pltpu.VMEM((points, cols), phi_all.dtype), pltpu.SemaphoreType.DMA],
        compiler_params=pltpu.CompilerParams(vmem_limit_bytes=56 << 20),
        cost_estimate=pl.CostEstimate(flops=10**9, bytes_accessed=2 * 10**6, transcendentals=0),
        name="fock_far",
    )(meta_all, pot, phi_all)


def shards(density, basis_vals, kernel, starts, counts, pair_mask):
    grid_size, planes = lax.axis_size("grid"), lax.axis_size("basis")
    batches, share = basis_vals.shape[0], density.shape[2]
    grid_pos = lax.axis_index("grid")
    core = lax.rem(grid_pos, 2)
    meta = jnp.pad(jnp.stack([starts, counts], axis=1), ((0, 0), (0, BLOCK - 2)))
    phi_all, meta_all, pot = potentials(
        basis_vals, meta, density, starts, counts, pair_mask, kernel, grid_size // 2, planes)
    pot = pot.reshape(SLOTS * batches, PERTS, POINTS)
    far = fock_far(meta_all, pot, phi_all, share)
    route = [(i, (i + 1) % grid_size if i % 2 else (i - 1) % grid_size) for i in range(grid_size)]
    arrived = lax.ppermute(far, "grid", route)
    own = fock_own(meta_all, pair_mask, pot, phi_all, share)
    mask_row = lax.dynamic_slice(pair_mask, (2 * grid_pos + core, core * REACH), (1, WINDOW))[0]
    keep = jnp.repeat(mask_row, BLOCK).astype(jnp.float32)
    place = (core, 0, 0, core * REACH * BLOCK)
    present = lax.dynamic_slice(own, place, (1, PERTS, share, COLS))
    return lax.dynamic_update_slice(own, present + (arrived * keep)[None], place)


def solution(mesh):
    placed = (
        P("grid", None, "basis", None),
        P("grid", None, None),
        P("grid", None),
        P("grid"),
        P("grid"),
        P(),
    )
    return jax.shard_map(
        shards,
        mesh=mesh,
        in_specs=placed,
        out_specs=P("grid", None, "basis", None),
        check_vma=False,
    )
```

```python
import functools

import jax
import jax.numpy as jnp
from jax import lax
from jax.experimental import pallas as pl
from jax.experimental.pallas import tpu as pltpu
from jax.sharding import PartitionSpec as P

BLOCK = 128
PERTS = 12
WINDOW = 6
POINTS = 256
REACH = 5
BAND = 11
COLS = WINDOW * BLOCK
WIDE = BAND * BLOCK
SLOTS = 6
MESH = pl.DeviceIdType.MESH
NT = (((1,), (1,)), ((), ()))


def one_hot(share, columns, first):
    rows = lax.broadcasted_iota(jnp.int32, (share, columns), 0)
    lanes = lax.broadcasted_iota(jnp.int32, (share, columns), 1)
    return jnp.where(lanes == rows + first, 1.0, 0.0).astype(jnp.bfloat16)


def density_kernel(
    chips, planes, batches, share,
    phi_ref, dens_ref, starts_ref, counts_ref, mask_ref, kern_ref,
    all_ref, meta_all_ref, pot_ref,
    phi_v, dens_v, far_v, left_v, left_far, meta_v, meta_all_v, meta_s, mask_s, part, gathered, pot_v,
    own_sem, out_sem, core_s, core_r, y_s, y_r, z_s, z_r, c_s, c_r, m_s, m_r, f_sem, a_s, a_r, b_s, b_r,
):
    grid_pos, plane = lax.axis_index("grid"), lax.axis_index("basis")
    chip, core = grid_pos // 2, lax.rem(grid_pos, 2)
    half = batches // 2
    quarter = half // 2
    per_plane = batches // planes
    own_slot = 2 + core
    far_slot = jnp.where(core == 0, 4, 1)
    first = lax.rem(plane, 2) * half
    there = half - first
    rows_all = PERTS * share
    cut = POINTS // 2

    def device(slot, at_plane):
        return (2 * lax.rem(chip + slot // 2 - 1 + chips, chips) + lax.rem(slot, 2), at_plane)

    other = (2 * chip + 1 - core, plane)

    def remote(src, dst, send, recv, to):
        return pltpu.make_async_remote_copy(
            src_ref=src, dst_ref=dst, send_sem=send, recv_sem=recv, device_id=to, device_id_type=MESH)

    def is_other(slot, at_plane):
        return jnp.logical_or(slot != own_slot, at_plane != plane)

    def for_others(act):
        @pl.loop(0, SLOTS * planes)
        def _(no):
            slot, at_plane = no // planes, lax.rem(no, planes)

            @pl.when(is_other(slot, at_plane))
            def _():
                act(slot, at_plane)

    own_copy = pltpu.make_async_copy(phi_ref, phi_v.at[own_slot], own_sem.at[0])
    own_copy.start()
    dens_copy = pltpu.make_async_copy(dens_ref, left_v, own_sem.at[1])
    dens_copy.start()
    mask_copy = pltpu.make_async_copy(mask_ref, mask_s, own_sem.at[2])
    mask_copy.start()

    line = lax.broadcasted_iota(jnp.int32, (2 * batches, BLOCK), 0)
    meta = jnp.zeros((2 * batches, BLOCK), jnp.int32)
    for no in range(batches):
        meta = jnp.where(line == no, starts_ref[no], meta)
        meta = jnp.where(line == batches + no, counts_ref[no], meta)
    meta_v[...] = meta
    meta_all_v[own_slot] = meta

    barrier = pltpu.get_barrier_semaphore()
    for slot in (0, 1, 4, 5):
        pl.semaphore_signal(barrier, inc=1, device_id=device(slot, plane), device_id_type=MESH)
    for partner in (other, (grid_pos, lax.rem(plane + 1, planes)), (grid_pos, lax.rem(plane + planes - 1, planes))):
        pl.semaphore_signal(barrier, inc=1, device_id=partner, device_id_type=MESH)
    pl.semaphore_wait(barrier, 7)

    def piece(way, n):
        return n // 2 + quarter * lax.rem(n + way, 2)

    def rows(h):
        return pl.ds(h * cut, cut)

    def y_copy(way, n, h):
        at = first + piece(way, n)
        return remote(phi_ref.at[at, rows(h)], phi_v.at[4 * way + core, at, rows(h)], y_s.at[way, n, h], y_r.at[way, n, h],
                      device(4 - 4 * way + core, plane))

    def z_copy(way, n, h):
        which = piece(way, n)
        where = phi_v.at[4 * way + core, first + which, rows(h)]
        to = lax.rem(plane + 1 - 2 * (which // quarter) + planes, planes)
        return remote(where, where, z_s.at[way, n, h], z_r.at[way, n, h], (grid_pos, to))

    def c_copy(way, m, h):
        at = jnp.where(m < half, first, there) + piece(way, lax.rem(m, half))
        where = phi_v.at[4 * way + core, at, rows(h)]
        return remote(where, where, c_s.at[way, m, h], c_r.at[way, m, h], other)

    def core_copy(no):
        return remote(phi_ref.at[no], phi_v.at[own_slot, no], core_s.at[no], core_r.at[no], other)

    def meta_copy(way, s):
        return remote(meta_v, meta_all_v.at[4 * way + core], m_s.at[1 + 2 * way + s], m_r.at[1 + 2 * way + core],
                      device(4 - 4 * way + s, plane))

    def out_copy(slot, no):
        return pltpu.make_async_copy(phi_v.at[slot, no], all_ref.at[slot, no], out_sem.at[slot, no])

    far_copy = remote(dens_ref.at[core, :, :, pl.ds(pl.multiple_of(core * REACH * BLOCK, BLOCK), COLS)], left_far,
                      f_sem.at[0], f_sem.at[1], device(jnp.where(core == 0, 1, 4), plane))
    core_meta = remote(meta_v, meta_all_v.at[own_slot], m_s.at[0], m_r.at[0], other)

    core_meta.start()
    for way in range(2):
        for s in range(2):
            meta_copy(way, s).start()

    @pl.loop(0, half)
    def _(n):
        for h in range(2):
            for way in range(2):
                y_copy(way, n, h).start()

    far_copy.start()

    @pl.loop(0, batches)
    def _(no):
        core_copy(no).start()

    def masked(block, keep):
        return block * keep.astype(jnp.float32).astype(block.dtype)

    def same(left, right):
        return (1 - jnp.minimum(jnp.abs(left - right), 1)).astype(jnp.float32)

    mask_copy.wait()
    dens_copy.wait()
    for r in range(2):
        row = 2 * grid_pos + r
        for t in range(BAND):
            block = left_v[r, :, :, t * BLOCK:(t + 1) * BLOCK].reshape(rows_all, BLOCK)
            dens_v[r, t, :rows_all, :] = masked(block, mask_s[row, t])
            dens_v[r, t, rows_all:, :] = one_hot(share, BLOCK, (REACH - t) * BLOCK + plane * share)
    far_v[rows_all:, :] = one_hot(share, COLS, core * REACH * BLOCK + plane * share)

    own_copy.wait()
    for no in range(5):
        pltpu.make_async_copy(meta_v, meta_all_v.at[own_slot], m_r.at[no]).wait()
    to_smem = pltpu.make_async_copy(meta_all_v, meta_s, own_sem.at[3])
    to_smem.start()
    meta_out = pltpu.make_async_copy(meta_all_v, meta_all_ref, own_sem.at[4])
    meta_out.start()
    to_smem.wait()

    def reduced(mixed):
        picked = mixed[rows_all:rows_all + share]
        sums = jnp.sum(mixed[:rows_all].reshape(PERTS, share, POINTS) * picked[None], axis=1)
        return jnp.concatenate([sums[:, :cut], sums[:, cut:]], axis=0)

    def rho_part(slot, no):
        start = meta_s[slot, no, 0]
        phi = phi_v[slot, no]
        total = None
        for r in range(2):
            offset = 2 * grid_pos + r - start
            inside = jnp.clip(offset, 0, WINDOW - 1)
            lhs = jnp.concatenate([dens_v[r, REACH - inside + c] for c in range(WINDOW)], axis=1)
            mixed = lax.dot_general(lhs, phi, NT, preferred_element_type=jnp.float32)
            term = reduced(mixed) * same(offset, inside)
            total = term if total is None else total + term
        part[slot, no] = total

    far_start = 4 * chip - 1

    def rho_far(slot, no):
        mixed = lax.dot_general(far_v[...], phi_v[slot, no], NT, preferred_element_type=jnp.float32)
        part[slot, no] = part[slot, no] + reduced(mixed) * same(meta_s[slot, no, 0], far_start)

    def part_copy(slot, no):
        back = 2 * (2 - slot // 2) + core
        keeper = no // per_plane
        which = lax.rem(no, per_plane)
        return remote(part.at[slot, no], gathered.at[back, plane, which], a_s.at[slot, no], a_r.at[back, plane, which],
                      device(slot, keeper))

    def send_part(slot, no):
        away = is_other(slot, no // per_plane)

        @pl.when(away)
        def _():
            part_copy(slot, no).start()

        @pl.when(jnp.logical_not(away))
        def _():
            gathered[own_slot, plane, lax.rem(no, per_plane)] = part[slot, no]

    def items(n, act):
        @pl.loop(0, 8)
        def _(item):
            kind, way = item // 2, lax.rem(item, 2)
            late = jnp.where(kind == 0, 0, jnp.where(kind == 3, 2, 1))
            came = n - late
            slot = 4 * way + jnp.where(kind <= 1, core, 1 - core)
            at = jnp.where(lax.rem(kind, 2) == 0, first, there) + piece(way, jnp.maximum(came, 0))

            @pl.when(jnp.logical_and(came >= 0, came < half))
            def _():
                act(slot, at)

    def send_near(slot, no):
        @pl.when(slot != far_slot)
        def _():
            send_part(slot, no)

    @pl.loop(0, batches)
    def _(no):
        out_copy(own_slot, no).start()
        rho_part(own_slot, no)

    @pl.loop(0, half + 2)
    def _(n):
        @pl.when(n < half)
        def _():
            for h in range(2):
                for way in range(2):
                    y_copy(way, n, h).wait_recv()
                    z_copy(way, n, h).start()
                    c_copy(way, n, h).start()
            for way in range(2):
                out_copy(4 * way + core, first + piece(way, n)).start()

        @pl.when(jnp.logical_and(n >= 1, n <= half))
        def _():
            for h in range(2):
                for way in range(2):
                    z_copy(way, n - 1, h).wait_recv()
                    c_copy(way, half + n - 1, h).start()
            for way in range(2):
                out_copy(4 * way + core, there + piece(way, n - 1)).start()
            for way in range(2):
                for h in range(2):
                    c_copy(way, n - 1, h).wait_recv()
                out_copy(4 * way + 1 - core, first + piece(way, n - 1)).start()

        @pl.when(n >= 2)
        def _():
            for way in range(2):
                for h in range(2):
                    c_copy(way, half + n - 2, h).wait_recv()
                out_copy(4 * way + 1 - core, there + piece(way, n - 2)).start()

        @pl.when(n == half)
        def _():
            @pl.loop(0, batches)
            def _(no):
                for slot in range(2):
                    send_part(2 + slot, no)

            @pl.loop(0, half)
            def _(m):
                items(m, send_near)

        items(n, rho_part)

        @pl.when(n >= half)
        def _():
            items(n, send_near)

        @pl.when(n == 0)
        def _():
            @pl.loop(0, batches)
            def _(no):
                core_copy(no).wait_recv()
                out_copy(5 - own_slot, no).start()
                rho_part(5 - own_slot, no)

        @pl.when(n == half)
        def _():
            far_copy.wait_recv()
            far_row = jnp.where(core == 0, jnp.maximum(2 * grid_pos - 1, 0), jnp.minimum(2 * grid_pos + 2, 4 * chips - 1))
            for t in range(WINDOW):
                block = left_far[:, :, t * BLOCK:(t + 1) * BLOCK].reshape(rows_all, BLOCK)
                keep = mask_s[far_row, jnp.where(core == 0, REACH, 0) + t]
                far_v[:rows_all, t * BLOCK:(t + 1) * BLOCK] = masked(block, keep)

            @pl.loop(0, batches)
            def _(no):
                rho_far(far_slot, no)
                send_part(far_slot, no)

    def pot_copy(slot, at_plane):
        back = 2 * (2 - slot // 2) + core
        return remote(pot_v, pot_ref.at[back, plane], b_s.at[slot, at_plane], b_r.at[back, plane],
                      device(slot, at_plane))

    def wait_parts(slot, at_plane):
        for which in range(per_plane):
            pltpu.make_async_copy(part.at[0, 0], gathered.at[slot, at_plane, which], a_r.at[slot, at_plane, which]).wait()

    for_others(wait_parts)
    points = lax.broadcasted_iota(jnp.int32, (1, POINTS), 1)
    for no in range(per_plane):
        rho = gathered[0, 0, no]
        for slot in range(SLOTS):
            for at_plane in range(planes):
                if slot or at_plane:
                    rho = rho + gathered[slot, at_plane, no]
        mine = per_plane * plane + no
        live = jnp.clip(counts_ref[mine] - points, 0, 1).astype(jnp.float32)
        factor = jnp.broadcast_to(kern_ref[pl.ds(mine, 1), :] * live, (PERTS, POINTS))
        pot_v[no] = rho * jnp.concatenate([factor[:, :cut], factor[:, cut:]], axis=0)
    for_others(lambda slot, at_plane: pot_copy(slot, at_plane).start())
    pot_own = pltpu.make_async_copy(pot_v, pot_ref.at[own_slot, plane], own_sem.at[0])
    pot_own.start()

    meta_out.wait()
    far_copy.wait_send()
    core_meta.wait_send()
    for way in range(2):
        for s in range(2):
            meta_copy(way, s).wait_send()

    @pl.loop(0, batches)
    def _(no):
        core_copy(no).wait_send()
        for slot in range(SLOTS):
            out_copy(slot, no).wait()

            @pl.when(is_other(slot, no // per_plane))
            def _():
                part_copy(slot, no).wait_send()

    @pl.loop(0, half)
    def _(n):
        for h in range(2):
            for way in range(2):
                y_copy(way, n, h).wait_send()
                z_copy(way, n, h).wait_send()
                c_copy(way, n, h).wait_send()
                c_copy(way, half + n, h).wait_send()

    for_others(lambda slot, at_plane: pltpu.make_async_copy(
        pot_v, pot_ref.at[slot, at_plane], b_r.at[slot, at_plane]).wait())
    pot_own.wait()
    for_others(lambda slot, at_plane: pot_copy(slot, at_plane).wait_send())


def potentials(phi, density, starts, counts, pair_mask, kern, chips, planes):
    batches, points, cols = phi.shape
    share = density.shape[2]
    half, per_plane = batches // 2, batches // planes
    rows = PERTS * share + share
    far = pl.BlockSpec(memory_space=pl.ANY)
    smem = pl.BlockSpec(memory_space=pltpu.SMEM)
    vmem = pl.BlockSpec(memory_space=pltpu.VMEM)
    dma = pltpu.SemaphoreType.DMA
    f32 = jnp.float32
    row_pair = (2 * PERTS, points // 2)
    meta = (2 * batches, BLOCK)
    return pl.pallas_call(
        functools.partial(density_kernel, chips, planes, batches, share),
        out_shape=(
            jax.ShapeDtypeStruct((SLOTS, batches, points, cols), phi.dtype),
            jax.ShapeDtypeStruct((SLOTS,) + meta, starts.dtype),
            jax.ShapeDtypeStruct((SLOTS, planes, per_plane) + row_pair, f32),
        ),
        in_specs=[far, far, smem, smem, far, vmem],
        out_specs=[far] * 3,
        scratch_shapes=[
            pltpu.VMEM((SLOTS, batches, points, cols), phi.dtype),
            pltpu.VMEM((2, BAND, rows, BLOCK), density.dtype),
            pltpu.VMEM((rows, COLS), density.dtype),
            pltpu.VMEM(density.shape, density.dtype),
            pltpu.VMEM((PERTS, share, COLS), density.dtype),
            pltpu.VMEM(meta, starts.dtype),
            pltpu.VMEM((SLOTS,) + meta, starts.dtype),
            pltpu.SMEM((SLOTS,) + meta, starts.dtype),
            pltpu.SMEM(pair_mask.shape, pair_mask.dtype),
            pltpu.VMEM((SLOTS, batches) + row_pair, f32),
            pltpu.VMEM((SLOTS, planes, per_plane) + row_pair, f32),
            pltpu.VMEM((per_plane,) + row_pair, f32),
            dma((5,)), dma((SLOTS, batches)), dma((batches,)), dma((batches,)),
            dma((2, half, 2)), dma((2, half, 2)), dma((2, half, 2)), dma((2, half, 2)),
            dma((2, batches, 2)), dma((2, batches, 2)), dma((5,)), dma((5,)), dma((2,)),
            dma((SLOTS, batches)), dma((SLOTS, planes, per_plane)), dma((SLOTS, planes)), dma((SLOTS, planes)),
        ],
        compiler_params=pltpu.CompilerParams(collective_id=0, has_side_effects=True, vmem_limit_bytes=56 << 20),
        cost_estimate=pl.CostEstimate(flops=17 * 10**9, bytes_accessed=50 * 10**6, transcendentals=0),
        name="potentials",
    )(phi, density, starts, counts, pair_mask, kern)


def joined(halves):
    return jnp.concatenate([halves[:PERTS], halves[PERTS:]], axis=1)


def split_weights(pot, picked, share):
    weighted = (pot[:, None, :] * picked[None]).reshape(PERTS * share, POINTS)
    high = weighted.astype(jnp.bfloat16)
    low = (weighted - high.astype(jnp.float32)).astype(jnp.bfloat16)
    return high, low


def add_product(parts, phi, few, store):
    def product(points):
        left = jnp.concatenate(
            [jnp.concatenate([high[:, :points], low[:, :points]], axis=1) for high, low in parts], axis=0)
        right = phi[:points, :]
        store(jnp.dot(left, jnp.concatenate([right, right], axis=0), preferred_element_type=jnp.float32))

    @pl.when(few)
    def _():
        product(POINTS // 2)

    @pl.when(jnp.logical_not(few))
    def _():
        product(POINTS)


DEPTH = 4


def fock_kernel(batches, share, meta_ref, mask_ref, pot_ref, phi_ref, out_ref, chosen, buf, sems):
    grid_pos, plane = lax.axis_index("grid"), lax.axis_index("basis")
    base = 2 * grid_pos - REACH

    def note(no, count):
        lead = meta_ref[no // batches, lax.rem(no, batches), 0] - base
        near = jnp.logical_and(lead >= 0, lead <= REACH + 1)

        @pl.when(near)
        def _():
            chosen[count] = no

        return count + near.astype(jnp.int32)

    count = lax.fori_loop(0, SLOTS * batches, note, 0)

    def fetch(i):
        no = chosen[i]
        return pltpu.make_async_copy(
            phi_ref.at[no // batches, lax.rem(no, batches)], buf.at[lax.rem(i, DEPTH)], sems.at[lax.rem(i, DEPTH)])

    for i in range(DEPTH - 1):
        @pl.when(i < count)
        def _():
            fetch(i).start()

    out_ref[...] = jnp.zeros_like(out_ref)
    pick = one_hot(share, BLOCK, plane * share)

    @pl.loop(0, count)
    def _(i):
        fetch(i).wait()

        @pl.when(i + DEPTH - 1 < count)
        def _():
            fetch(i + DEPTH - 1).start()

        no = chosen[i]
        lead = meta_ref[no // batches, lax.rem(no, batches), 0] - base
        few = meta_ref[no // batches, batches + lax.rem(no, batches), 0] <= POINTS // 2
        here = buf.at[lax.rem(i, DEPTH)]
        pot = joined(pot_ref[no])

        def weights(offset):
            own = here[:, pl.ds(pl.multiple_of(offset * BLOCK, BLOCK), BLOCK)]
            picked = lax.dot_general(pick, own, NT, preferred_element_type=jnp.float32)
            return split_weights(pot, picked, share)

        def add(r, offset, value):
            spot = out_ref.at[r, :, :, pl.ds(pl.multiple_of((REACH - offset) * BLOCK, BLOCK), COLS)]
            spot[...] = spot[...] + value.reshape(PERTS, share, COLS)

        both = jnp.logical_and(lead >= 1, lead <= REACH)

        @pl.when(both)
        def _():
            offset = REACH - lead
            parts = [weights(offset), weights(offset + 1)]
            rows = PERTS * share

            def store(value):
                add(0, offset, value[:rows])
                add(1, offset + 1, value[rows:])

            add_product(parts, here, few, store)

        @pl.when(jnp.logical_not(both))
        def _():
            r = jnp.where(lead == 0, 0, 1)
            offset = jnp.where(lead == 0, REACH, 0)
            add_product([weights(offset)], here, few, lambda value: add(r, offset, value))

    for r in range(2):
        for t in range(BAND):
            @pl.when(mask_ref[2 * grid_pos + r, t] == 0)
            def _():
                out_ref[r, :, :, t * BLOCK:(t + 1) * BLOCK] = jnp.zeros((PERTS, share, BLOCK), jnp.float32)


def fock_own(meta_all, pair_mask, pot, phi_all, share):
    slots, batches, points, cols = phi_all.shape
    smem = pl.BlockSpec(memory_space=pltpu.SMEM)
    vmem = pl.BlockSpec(memory_space=pltpu.VMEM)
    return pl.pallas_call(
        functools.partial(fock_kernel, batches, share),
        out_shape=jax.ShapeDtypeStruct((2, PERTS, share, WIDE), jnp.float32),
        in_specs=[smem, smem, vmem, pl.BlockSpec(memory_space=pl.ANY)],
        out_specs=vmem,
        scratch_shapes=[
            pltpu.SMEM((slots * batches,), jnp.int32),
            pltpu.VMEM((DEPTH, points, cols), phi_all.dtype),
            pltpu.SemaphoreType.DMA((DEPTH,)),
        ],
        compiler_params=pltpu.CompilerParams(vmem_limit_bytes=56 << 20),
        cost_estimate=pl.CostEstimate(flops=20 * 10**9, bytes_accessed=20 * 10**6, transcendentals=0),
        name="fock_own",
    )(meta_all, pair_mask, pot, phi_all)


def far_kernel(batches, share, meta_ref, pot_ref, phi_ref, out_ref, buf, sem):
    grid_pos, plane = lax.axis_index("grid"), lax.axis_index("basis")
    core = lax.rem(grid_pos, 2)
    slot = jnp.where(core == 0, 4, 1)
    far_start = 4 * (grid_pos // 2) - 1
    out_ref[...] = jnp.zeros_like(out_ref)
    pick = one_hot(share, BLOCK, plane * share)

    @pl.loop(0, batches)
    def _(no):
        @pl.when(meta_ref[slot, no, 0] == far_start)
        def _():
            copy = pltpu.make_async_copy(phi_ref.at[slot, no], buf, sem)
            copy.start()
            copy.wait()
            own = buf[:, pl.ds(pl.multiple_of(core * REACH * BLOCK, BLOCK), BLOCK)]
            picked = lax.dot_general(pick, own, NT, preferred_element_type=jnp.float32)
            parts = [split_weights(joined(pot_ref[slot * batches + no]), picked, share)]

            def store(value):
                out_ref[...] += value.reshape(PERTS, share, COLS)

            add_product(parts, buf, meta_ref[slot, batches + no, 0] <= POINTS // 2, store)


def fock_far(meta_all, pot, phi_all, share):
    slots, batches, points, cols = phi_all.shape
    smem = pl.BlockSpec(memory_space=pltpu.SMEM)
    vmem = pl.BlockSpec(memory_space=pltpu.VMEM)
    return pl.pallas_call(
        functools.partial(far_kernel, batches, share),
        out_shape=jax.ShapeDtypeStruct((PERTS, share, COLS), jnp.float32),
        in_specs=[smem, vmem, pl.BlockSpec(memory_space=pl.ANY)],
        out_specs=vmem,
        scratch_shapes=[pltpu.VMEM((points, cols), phi_all.dtype), pltpu.SemaphoreType.DMA],
        compiler_params=pltpu.CompilerParams(vmem_limit_bytes=56 << 20),
        cost_estimate=pl.CostEstimate(flops=10**9, bytes_accessed=2 * 10**6, transcendentals=0),
        name="fock_far",
    )(meta_all, pot, phi_all)


def shards(density, basis_vals, kernel, starts, counts, pair_mask):
    grid_size, planes = lax.axis_size("grid"), lax.axis_size("basis")
    batches, share = basis_vals.shape[0], density.shape[2]
    grid_pos = lax.axis_index("grid")
    core = lax.rem(grid_pos, 2)
    phi_all, meta_all, pot = potentials(
        basis_vals, density, starts, counts, pair_mask, kernel, grid_size // 2, planes)
    pot = pot.reshape(SLOTS * batches, 2 * PERTS, POINTS // 2)
    far = fock_far(meta_all, pot, phi_all, share)
    route = [(i, (i + 1) % grid_size if i % 2 else (i - 1) % grid_size) for i in range(grid_size)]
    arrived = lax.ppermute(far, "grid", route)
    own = fock_own(meta_all, pair_mask, pot, phi_all, share)
    mask_row = lax.dynamic_slice(pair_mask, (2 * grid_pos + core, core * REACH), (1, WINDOW))[0]
    keep = jnp.repeat(mask_row, BLOCK).astype(jnp.float32)
    place = (core, 0, 0, core * REACH * BLOCK)
    present = lax.dynamic_slice(own, place, (1, PERTS, share, COLS))
    return lax.dynamic_update_slice(own, present + (arrived * keep)[None], place)


def solution(mesh):
    placed = (
        P("grid", None, "basis", None),
        P("grid", None, None),
        P("grid", None),
        P("grid"),
        P("grid"),
        P(),
    )
    return jax.shard_map(
        shards,
        mesh=mesh,
        in_specs=placed,
        out_specs=P("grid", None, "basis", None),
        check_vma=False,
    )
```

```python
import functools

import jax
import jax.numpy as jnp
from jax import lax
from jax.experimental import pallas as pl
from jax.experimental.pallas import tpu as pltpu
from jax.sharding import PartitionSpec as P

BLOCK = 128
PERTS = 12
WINDOW = 6
POINTS = 256
REACH = 5
BAND = 11
COLS = WINDOW * BLOCK
WIDE = BAND * BLOCK
SLOTS = 6
MESH = pl.DeviceIdType.MESH
NT = (((1,), (1,)), ((), ()))


def one_hot(share, columns, first):
    rows = lax.broadcasted_iota(jnp.int32, (share, columns), 0)
    lanes = lax.broadcasted_iota(jnp.int32, (share, columns), 1)
    return jnp.where(lanes == rows + first, 1.0, 0.0).astype(jnp.bfloat16)


def density_kernel(
    chips, planes, batches, share,
    phi_ref, dens_ref, starts_ref, counts_ref, mask_ref, kern_ref,
    all_ref, facts_ref, pot_ref, picks_ref, far_picks_ref,
    phi_v, dens_v, far_v, left_v, left_far, meta_v, meta_all_v, facts_v, meta_s, mask_s, picks_v, far_picks_v, part, gathered, pot_v,
    own_sem, out_sem, core_s, core_r, y_s, y_r, z_s, z_r, c_s, c_r, m_s, m_r, f_sem, a_s, a_r, b_s, b_r,
):
    grid_pos, plane = lax.axis_index("grid"), lax.axis_index("basis")
    chip, core = grid_pos // 2, lax.rem(grid_pos, 2)
    half = batches // 2
    quarter = half // 2
    per_plane = batches // planes
    own_slot = 2 + core
    far_slot = jnp.where(core == 0, 4, 1)
    first = lax.rem(plane, 2) * half
    there = half - first
    rows_all = PERTS * share
    cut = POINTS // 2

    def device(slot, at_plane):
        return (2 * lax.rem(chip + slot // 2 - 1 + chips, chips) + lax.rem(slot, 2), at_plane)

    other = (2 * chip + 1 - core, plane)

    def remote(src, dst, send, recv, to):
        return pltpu.make_async_remote_copy(
            src_ref=src, dst_ref=dst, send_sem=send, recv_sem=recv, device_id=to, device_id_type=MESH)

    def is_other(slot, at_plane):
        return jnp.logical_or(slot != own_slot, at_plane != plane)

    def for_others(act):
        @pl.loop(0, SLOTS * planes)
        def _(no):
            slot, at_plane = no // planes, lax.rem(no, planes)

            @pl.when(is_other(slot, at_plane))
            def _():
                act(slot, at_plane)

    own_copy = pltpu.make_async_copy(phi_ref, phi_v.at[own_slot], own_sem.at[0])
    own_copy.start()
    dens_copy = pltpu.make_async_copy(dens_ref, left_v, own_sem.at[1])
    dens_copy.start()
    mask_copy = pltpu.make_async_copy(mask_ref, mask_s, own_sem.at[2])
    mask_copy.start()

    line = lax.broadcasted_iota(jnp.int32, (8, BLOCK), 0)
    lane = lax.broadcasted_iota(jnp.int32, (8, BLOCK), 1)
    meta = jnp.zeros((8, BLOCK), jnp.int32)
    for no in range(batches):
        meta = jnp.where(lane == no, starts_ref[no], meta)
        meta = jnp.where(lane == batches + no, counts_ref[no], meta)
    meta_v[...] = meta
    meta_all_v[own_slot] = meta

    barrier = pltpu.get_barrier_semaphore()
    for slot in (0, 1, 4, 5):
        pl.semaphore_signal(barrier, inc=1, device_id=device(slot, plane), device_id_type=MESH)
    for partner in (other, (grid_pos, lax.rem(plane + 1, planes)), (grid_pos, lax.rem(plane + planes - 1, planes))):
        pl.semaphore_signal(barrier, inc=1, device_id=partner, device_id_type=MESH)
    pl.semaphore_wait(barrier, 7)

    def piece(way, n):
        return n // 2 + quarter * lax.rem(n + way, 2)

    def rows(h):
        return pl.ds(h * cut, cut)

    def y_copy(way, n, h):
        at = first + piece(way, n)
        return remote(phi_ref.at[at, rows(h)], phi_v.at[4 * way + core, at, rows(h)], y_s.at[way, n, h], y_r.at[way, n, h],
                      device(4 - 4 * way + core, plane))

    def z_copy(way, n, h):
        which = piece(way, n)
        where = phi_v.at[4 * way + core, first + which, rows(h)]
        to = lax.rem(plane + 1 - 2 * (which // quarter) + planes, planes)
        return remote(where, where, z_s.at[way, n, h], z_r.at[way, n, h], (grid_pos, to))

    def c_copy(way, m, h):
        at = jnp.where(m < half, first, there) + piece(way, lax.rem(m, half))
        where = phi_v.at[4 * way + core, at, rows(h)]
        return remote(where, where, c_s.at[way, m, h], c_r.at[way, m, h], other)

    def core_copy(no):
        return remote(phi_ref.at[no], phi_v.at[own_slot, no], core_s.at[no], core_r.at[no], other)

    def meta_copy(way, s):
        return remote(meta_v, meta_all_v.at[4 * way + core], m_s.at[1 + 2 * way + s], m_r.at[1 + 2 * way + core],
                      device(4 - 4 * way + s, plane))

    def out_copy(slot, no):
        return pltpu.make_async_copy(phi_v.at[slot, no], all_ref.at[slot, no], out_sem.at[slot, no])

    far_copy = remote(dens_ref.at[core, :, :, pl.ds(pl.multiple_of(core * REACH * BLOCK, BLOCK), COLS)], left_far,
                      f_sem.at[0], f_sem.at[1], device(jnp.where(core == 0, 1, 4), plane))
    core_meta = remote(meta_v, meta_all_v.at[own_slot], m_s.at[0], m_r.at[0], other)

    core_meta.start()
    for way in range(2):
        for s in range(2):
            meta_copy(way, s).start()

    @pl.loop(0, half)
    def _(n):
        for h in range(2):
            for way in range(2):
                y_copy(way, n, h).start()

    far_copy.start()

    @pl.loop(0, batches)
    def _(no):
        core_copy(no).start()

    def masked(block, keep):
        return block * keep.astype(jnp.float32).astype(block.dtype)

    def same(left, right):
        return (1 - jnp.minimum(jnp.abs(left - right), 1)).astype(jnp.float32)

    mask_copy.wait()
    dens_copy.wait()
    for r in range(2):
        row = 2 * grid_pos + r
        for t in range(BAND):
            block = left_v[r, :, :, t * BLOCK:(t + 1) * BLOCK].reshape(rows_all, BLOCK)
            dens_v[r, t, :rows_all, :] = masked(block, mask_s[row, t])
            dens_v[r, t, rows_all:, :] = one_hot(share, BLOCK, (REACH - t) * BLOCK + plane * share)
    far_v[rows_all:, :] = one_hot(share, COLS, core * REACH * BLOCK + plane * share)

    own_copy.wait()
    for no in range(5):
        pltpu.make_async_copy(meta_v, meta_all_v.at[own_slot], m_r.at[no]).wait()
    facts = jnp.zeros((8, BLOCK), jnp.int32)
    for slot in range(SLOTS):
        facts = jnp.where(line == slot, meta_all_v[slot], facts)
    for r in range(2):
        for t in range(BAND):
            facts = jnp.where(jnp.logical_and(line == SLOTS + r, lane == t), mask_s[2 * grid_pos + r, t], facts)
    facts_v[...] = facts
    to_smem = pltpu.make_async_copy(facts_v, meta_s, own_sem.at[3])
    to_smem.start()
    facts_out = pltpu.make_async_copy(facts_v, facts_ref, own_sem.at[4])
    facts_out.start()
    to_smem.wait()

    def reduced(mixed, keep_picks):
        picked = mixed[rows_all:]
        for h in range(2):
            keep_picks(h, picked[:, h * cut:(h + 1) * cut].astype(jnp.bfloat16))
        sums = jnp.sum(mixed[:rows_all].reshape(PERTS, share, POINTS) * picked[None], axis=1)
        return jnp.concatenate([sums[:, :cut], sums[:, cut:]], axis=0)

    def rho_part(slot, no):
        start = meta_s[slot, no]
        lhs, keeps = [], []
        for r in range(2):
            offset = 2 * grid_pos + r - start
            inside = jnp.clip(offset, 0, WINDOW - 1)
            keeps.append(same(offset, inside))
            lhs.append(jnp.concatenate([dens_v[r, REACH - inside + c] for c in range(WINDOW)], axis=1))
        mixed = lax.dot_general(jnp.concatenate(lhs, axis=0), phi_v[slot, no], NT, preferred_element_type=jnp.float32)
        total = None
        for r in range(2):
            def keep_picks(h, value, r=r):
                picks_v[slot, no, h, r] = value

            term = reduced(mixed[r * (rows_all + share):(r + 1) * (rows_all + share)], keep_picks) * keeps[r]
            total = term if total is None else total + term
        part[slot, no] = total

    far_start = 4 * chip - 1

    def rho_far(slot, no):
        mixed = lax.dot_general(far_v[...], phi_v[slot, no], NT, preferred_element_type=jnp.float32)

        def keep_picks(h, value):
            far_picks_v[no, h] = value

        part[slot, no] = part[slot, no] + reduced(mixed, keep_picks) * same(meta_s[slot, no], far_start)

    def part_copy(slot, no):
        back = 2 * (2 - slot // 2) + core
        keeper = no // per_plane
        which = lax.rem(no, per_plane)
        return remote(part.at[slot, no], gathered.at[back, plane, which], a_s.at[slot, no], a_r.at[back, plane, which],
                      device(slot, keeper))

    def send_part(slot, no):
        away = is_other(slot, no // per_plane)

        @pl.when(away)
        def _():
            part_copy(slot, no).start()

        @pl.when(jnp.logical_not(away))
        def _():
            gathered[own_slot, plane, lax.rem(no, per_plane)] = part[slot, no]

    def items(n, act):
        @pl.loop(0, 8)
        def _(item):
            kind, way = item // 2, lax.rem(item, 2)
            late = jnp.where(kind == 0, 0, jnp.where(kind == 3, 2, 1))
            came = n - late
            slot = 4 * way + jnp.where(kind <= 1, core, 1 - core)
            at = jnp.where(lax.rem(kind, 2) == 0, first, there) + piece(way, jnp.maximum(came, 0))

            @pl.when(jnp.logical_and(came >= 0, came < half))
            def _():
                act(slot, at)

    def send_near(slot, no):
        @pl.when(slot != far_slot)
        def _():
            send_part(slot, no)

    @pl.loop(0, batches)
    def _(no):
        out_copy(own_slot, no).start()
        rho_part(own_slot, no)

    @pl.loop(0, half + 2)
    def _(n):
        @pl.when(n < half)
        def _():
            for h in range(2):
                for way in range(2):
                    y_copy(way, n, h).wait_recv()
                    z_copy(way, n, h).start()
                    c_copy(way, n, h).start()
            for way in range(2):
                out_copy(4 * way + core, first + piece(way, n)).start()

        @pl.when(jnp.logical_and(n >= 1, n <= half))
        def _():
            for h in range(2):
                for way in range(2):
                    z_copy(way, n - 1, h).wait_recv()
                    c_copy(way, half + n - 1, h).start()
            for way in range(2):
                out_copy(4 * way + core, there + piece(way, n - 1)).start()
            for way in range(2):
                for h in range(2):
                    c_copy(way, n - 1, h).wait_recv()
                out_copy(4 * way + 1 - core, first + piece(way, n - 1)).start()

        @pl.when(n >= 2)
        def _():
            for way in range(2):
                for h in range(2):
                    c_copy(way, half + n - 2, h).wait_recv()
                out_copy(4 * way + 1 - core, there + piece(way, n - 2)).start()

        @pl.when(n == half)
        def _():
            @pl.loop(0, batches)
            def _(no):
                for slot in range(2):
                    send_part(2 + slot, no)

            @pl.loop(0, half)
            def _(m):
                items(m, send_near)

        items(n, rho_part)

        @pl.when(n >= half)
        def _():
            items(n, send_near)

        @pl.when(n == 0)
        def _():
            @pl.loop(0, batches)
            def _(no):
                core_copy(no).wait_recv()
                out_copy(5 - own_slot, no).start()
                rho_part(5 - own_slot, no)

        @pl.when(n == half)
        def _():
            far_copy.wait_recv()
            far_row = jnp.where(core == 0, jnp.maximum(2 * grid_pos - 1, 0), jnp.minimum(2 * grid_pos + 2, 4 * chips - 1))
            for t in range(WINDOW):
                block = left_far[:, :, t * BLOCK:(t + 1) * BLOCK].reshape(rows_all, BLOCK)
                keep = mask_s[far_row, jnp.where(core == 0, REACH, 0) + t]
                far_v[:rows_all, t * BLOCK:(t + 1) * BLOCK] = masked(block, keep)

            @pl.loop(0, batches)
            def _(no):
                rho_far(far_slot, no)
                send_part(far_slot, no)

    picks_out = pltpu.make_async_copy(picks_v, picks_ref, own_sem.at[1])
    picks_out.start()
    far_picks_out = pltpu.make_async_copy(far_picks_v, far_picks_ref, own_sem.at[2])
    far_picks_out.start()

    def pot_copy(slot, at_plane):
        back = 2 * (2 - slot // 2) + core
        return remote(pot_v, pot_ref.at[back, plane], b_s.at[slot, at_plane], b_r.at[back, plane],
                      device(slot, at_plane))

    def wait_parts(slot, at_plane):
        for which in range(per_plane):
            pltpu.make_async_copy(part.at[0, 0], gathered.at[slot, at_plane, which], a_r.at[slot, at_plane, which]).wait()

    for_others(wait_parts)
    points = lax.broadcasted_iota(jnp.int32, (1, POINTS), 1)
    for no in range(per_plane):
        rho = gathered[0, 0, no]
        for slot in range(SLOTS):
            for at_plane in range(planes):
                if slot or at_plane:
                    rho = rho + gathered[slot, at_plane, no]
        mine = per_plane * plane + no
        live = jnp.clip(counts_ref[mine] - points, 0, 1).astype(jnp.float32)
        factor = jnp.broadcast_to(kern_ref[pl.ds(mine, 1), :] * live, (PERTS, POINTS))
        pot_v[no] = rho * jnp.concatenate([factor[:, :cut], factor[:, cut:]], axis=0)
    for_others(lambda slot, at_plane: pot_copy(slot, at_plane).start())
    pot_own = pltpu.make_async_copy(pot_v, pot_ref.at[own_slot, plane], own_sem.at[0])
    pot_own.start()

    facts_out.wait()
    picks_out.wait()
    far_picks_out.wait()
    far_copy.wait_send()
    core_meta.wait_send()
    for way in range(2):
        for s in range(2):
            meta_copy(way, s).wait_send()

    @pl.loop(0, batches)
    def _(no):
        core_copy(no).wait_send()
        for slot in range(SLOTS):
            out_copy(slot, no).wait()

            @pl.when(is_other(slot, no // per_plane))
            def _():
                part_copy(slot, no).wait_send()

    @pl.loop(0, half)
    def _(n):
        for h in range(2):
            for way in range(2):
                y_copy(way, n, h).wait_send()
                z_copy(way, n, h).wait_send()
                c_copy(way, n, h).wait_send()
                c_copy(way, half + n, h).wait_send()

    for_others(lambda slot, at_plane: pltpu.make_async_copy(
        pot_v, pot_ref.at[slot, at_plane], b_r.at[slot, at_plane]).wait())
    pot_own.wait()
    for_others(lambda slot, at_plane: pot_copy(slot, at_plane).wait_send())


def potentials(phi, density, starts, counts, pair_mask, kern, chips, planes):
    batches, points, cols = phi.shape
    share = density.shape[2]
    half, per_plane = batches // 2, batches // planes
    rows = PERTS * share + share
    far = pl.BlockSpec(memory_space=pl.ANY)
    smem = pl.BlockSpec(memory_space=pltpu.SMEM)
    vmem = pl.BlockSpec(memory_space=pltpu.VMEM)
    dma = pltpu.SemaphoreType.DMA
    f32 = jnp.float32
    row_pair = (2 * PERTS, points // 2)
    meta = (8, BLOCK)
    picks, far_picks = (SLOTS, batches, 2, 2, share, points // 2), (batches, 2, share, points // 2)
    return pl.pallas_call(
        functools.partial(density_kernel, chips, planes, batches, share),
        out_shape=(
            jax.ShapeDtypeStruct((SLOTS, batches, points, cols), phi.dtype),
            jax.ShapeDtypeStruct(meta, starts.dtype),
            jax.ShapeDtypeStruct((SLOTS, planes, per_plane) + row_pair, f32),
            jax.ShapeDtypeStruct(picks, phi.dtype),
            jax.ShapeDtypeStruct(far_picks, phi.dtype),
        ),
        in_specs=[far, far, smem, smem, far, vmem],
        out_specs=[far] * 5,
        scratch_shapes=[
            pltpu.VMEM((SLOTS, batches, points, cols), phi.dtype),
            pltpu.VMEM((2, BAND, rows, BLOCK), density.dtype),
            pltpu.VMEM((rows, COLS), density.dtype),
            pltpu.VMEM(density.shape, density.dtype),
            pltpu.VMEM((PERTS, share, COLS), density.dtype),
            pltpu.VMEM(meta, starts.dtype),
            pltpu.VMEM((SLOTS,) + meta, starts.dtype),
            pltpu.VMEM(meta, starts.dtype),
            pltpu.SMEM(meta, starts.dtype),
            pltpu.SMEM(pair_mask.shape, pair_mask.dtype),
            pltpu.VMEM(picks, phi.dtype),
            pltpu.VMEM(far_picks, phi.dtype),
            pltpu.VMEM((SLOTS, batches) + row_pair, f32),
            pltpu.VMEM((SLOTS, planes, per_plane) + row_pair, f32),
            pltpu.VMEM((per_plane,) + row_pair, f32),
            dma((5,)), dma((SLOTS, batches)), dma((batches,)), dma((batches,)),
            dma((2, half, 2)), dma((2, half, 2)), dma((2, half, 2)), dma((2, half, 2)),
            dma((2, batches, 2)), dma((2, batches, 2)), dma((5,)), dma((5,)), dma((2,)),
            dma((SLOTS, batches)), dma((SLOTS, planes, per_plane)), dma((SLOTS, planes)), dma((SLOTS, planes)),
        ],
        compiler_params=pltpu.CompilerParams(collective_id=0, has_side_effects=True, vmem_limit_bytes=56 << 20),
        cost_estimate=pl.CostEstimate(flops=17 * 10**9, bytes_accessed=50 * 10**6, transcendentals=0),
        name="potentials",
    )(phi, density, starts, counts, pair_mask, kern)


def joined(halves):
    return jnp.concatenate([halves[:PERTS], halves[PERTS:]], axis=1)


def split_weights(pot, picked):
    weighted = (pot[:, None, :] * picked[None]).reshape(pot.shape[0] * picked.shape[0], picked.shape[1])
    high = weighted.astype(jnp.bfloat16)
    low = (weighted - high.astype(jnp.float32)).astype(jnp.bfloat16)
    return high, low


CUT = POINTS // 2
LARGEST = 4


class Chunks:
    def __init__(self, batches, facts_ref, pot, pick, phi_ref, listed, counted, buf, sems):
        self.batches, self.facts, self.pot, self.pick, self.phi = batches, facts_ref, pot, pick, phi_ref
        self.listed, self.counted, self.buf, self.sems = listed, counted, buf, sems

    def start(self, no):
        return self.facts[no // self.batches, lax.rem(no, self.batches)]

    def note(self, which, no, wanted):
        most = self.pot.shape[0] * 2
        many = self.facts[no // self.batches, self.batches + lax.rem(no, self.batches)] > CUT

        @pl.when(wanted)
        def _():
            have = self.counted[which]
            self.listed[which * most + have] = 2 * no
            self.listed[which * most + have + 1] = 2 * no + 1
            self.counted[which] = have + 1 + many.astype(jnp.int32)

    def copy(self, chunk):
        no, h = chunk // 2, lax.rem(chunk, 2)
        return pltpu.make_async_copy(
            self.phi.at[no // self.batches, lax.rem(no, self.batches), pl.ds(pl.multiple_of(h * CUT, CUT), CUT)],
            self.buf.at[chunk], self.sems.at[chunk])

    def fetch(self, which):
        @pl.loop(0, self.counted[which])
        def _(i):
            self.copy(self.listed[which * self.pot.shape[0] * 2 + i]).start()

    def group(self, which, at, size, rows):
        rights, highs, lows = [], [[] for _ in rows], [[] for _ in rows]
        for i in range(size):
            chunk = self.listed[which * self.pot.shape[0] * 2 + at + i]
            self.copy(chunk).wait()
            pots = self.pot[chunk // 2]
            pot = jnp.where(lax.rem(chunk, 2) == 0, pots[:PERTS], pots[PERTS:])
            rights.append(self.buf[chunk])
            for no, (row, _) in enumerate(rows):
                high, low = split_weights(pot, self.pick(chunk, row).astype(jnp.float32))
                highs[no].append(high)
                lows[no].append(low)
        right = jnp.concatenate(rights + rights, axis=0)
        for no, (_, spot) in enumerate(rows):
            left = jnp.concatenate(highs[no] + lows[no], axis=1)
            total = spot[...].reshape(left.shape[0], COLS) + jnp.dot(left, right, preferred_element_type=jnp.float32)
            spot[...] = total.reshape(spot.shape)

    def add(self, which, rows):
        count = self.counted[which]
        size = LARGEST
        done = 0
        while size:
            times = (count - done) // size

            @pl.loop(0, times)
            def _(i, size=size, done=done):
                self.group(which, done + i * size, size, rows)

            done = done + times * size
            size //= 2


def fock_kernel(batches, share, facts_ref, pot_ref, picks_ref, phi_ref, out_ref,
                total, pot_v, picks_v, listed, counted, buf, sems, in_sem, out_sem):
    grid_pos = lax.axis_index("grid")
    pot_copy = pltpu.make_async_copy(pot_ref, pot_v, in_sem.at[0])
    pot_copy.start()
    picks_copy = pltpu.make_async_copy(picks_ref, picks_v, in_sem.at[1])
    picks_copy.start()
    chunks = Chunks(batches, facts_ref, pot_v, lambda chunk, row: picks_v[chunk, row], phi_ref, listed, counted, buf, sems)
    base = 2 * grid_pos - REACH
    leads = REACH + 2

    for lead in range(leads):
        counted[lead] = 0

    @pl.loop(0, SLOTS * batches)
    def _(no):
        lead = chunks.start(no) - base
        chunks.note(lead, no, jnp.logical_and(lead >= 0, lead < leads))

    chunks.fetch(0)
    chunks.fetch(1)
    total[...] = jnp.zeros_like(total)
    pot_copy.wait()
    picks_copy.wait()

    def spot(r, offset):
        return total.at[r, :, :, pl.ds(pl.multiple_of((REACH - offset) * BLOCK, BLOCK), COLS)]

    def out_copy(r, t):
        cols = pl.ds(pl.multiple_of(t * BLOCK, BLOCK), BLOCK)
        return pltpu.make_async_copy(total.at[r, :, :, cols], out_ref.at[r, :, :, cols], out_sem.at[r, t])

    def leave(r, t):
        @pl.when(facts_ref[SLOTS + r, t] == 0)
        def _():
            cols = pl.ds(pl.multiple_of(t * BLOCK, BLOCK), BLOCK)
            total[r, :, :, cols] = jnp.zeros((PERTS, share, BLOCK), jnp.float32)

        out_copy(r, t).start()

    @pl.loop(0, leads)
    def _(lead):
        @pl.when(lead + 2 < leads)
        def _():
            chunks.fetch(lead + 2)

        both = jnp.logical_and(lead >= 1, lead <= REACH)

        @pl.when(both)
        def _():
            offset = REACH - lead
            chunks.add(lead, [(0, spot(0, offset)), (1, spot(1, offset + 1))])

        @pl.when(jnp.logical_not(both))
        def _():
            r = jnp.where(lead == 0, 0, 1)
            offset = jnp.where(lead == 0, REACH, 0)
            chunks.add(lead, [(r, spot(r, offset))])

        @pl.loop(lead, jnp.where(lead == REACH, BAND, jnp.minimum(lead + 1, REACH + 1)))
        def _(t):
            leave(0, t)

        @pl.loop(jnp.maximum(lead - 1, 0), jnp.where(lead == REACH + 1, BAND, lead))
        def _(t):
            leave(1, t)

    @pl.loop(0, BAND)
    def _(t):
        for r in range(2):
            out_copy(r, t).wait()


def chunk_scratch(slots, batches, cols, lists, dtype):
    most = 2 * slots * batches
    return [
        pltpu.SMEM((lists * most,), jnp.int32),
        pltpu.SMEM((lists,), jnp.int32),
        pltpu.VMEM((most, CUT, cols), dtype),
        pltpu.SemaphoreType.DMA((most,)),
    ]


def fock_own(facts, pot, picks, phi_all, share):
    slots, batches, points, cols = phi_all.shape
    far = pl.BlockSpec(memory_space=pl.ANY)
    whole = (2, PERTS, share, WIDE)
    dma = pltpu.SemaphoreType.DMA
    return pl.pallas_call(
        functools.partial(fock_kernel, batches, share),
        out_shape=jax.ShapeDtypeStruct(whole, jnp.float32),
        in_specs=[pl.BlockSpec(memory_space=pltpu.SMEM), far, far, far],
        out_specs=far,
        scratch_shapes=[
            pltpu.VMEM(whole, jnp.float32), pltpu.VMEM(pot.shape, pot.dtype), pltpu.VMEM(picks.shape, picks.dtype),
        ]
        + chunk_scratch(slots, batches, cols, REACH + 2, phi_all.dtype)
        + [dma((2,)), dma((2, BAND))],
        compiler_params=pltpu.CompilerParams(vmem_limit_bytes=56 << 20),
        cost_estimate=pl.CostEstimate(flops=20 * 10**9, bytes_accessed=20 * 10**6, transcendentals=0),
        name="fock_own",
    )(facts, pot, picks, phi_all)


def far_kernel(batches, facts_ref, pot_ref, picks_ref, phi_ref, out_ref, listed, counted, buf, sems):
    grid_pos = lax.axis_index("grid")
    core = lax.rem(grid_pos, 2)
    slot = jnp.where(core == 0, 4, 1)
    far_start = 4 * (grid_pos // 2) - 1
    chunks = Chunks(batches, facts_ref, pot_ref, lambda chunk, row: picks_ref[chunk - 2 * batches * slot], phi_ref,
                    listed, counted, buf, sems)
    counted[0] = 0

    @pl.loop(0, batches)
    def _(no):
        chunks.note(0, slot * batches + no, chunks.start(slot * batches + no) == far_start)

    chunks.fetch(0)
    out_ref[...] = jnp.zeros_like(out_ref)
    chunks.add(0, [(0, out_ref)])


def fock_far(facts, pot, far_picks, phi_all, share):
    slots, batches, points, cols = phi_all.shape
    smem = pl.BlockSpec(memory_space=pltpu.SMEM)
    vmem = pl.BlockSpec(memory_space=pltpu.VMEM)
    return pl.pallas_call(
        functools.partial(far_kernel, batches),
        out_shape=jax.ShapeDtypeStruct((PERTS, share, COLS), jnp.float32),
        in_specs=[smem, vmem, vmem, pl.BlockSpec(memory_space=pl.ANY)],
        out_specs=vmem,
        scratch_shapes=chunk_scratch(slots, batches, cols, 1, phi_all.dtype),
        compiler_params=pltpu.CompilerParams(vmem_limit_bytes=56 << 20),
        cost_estimate=pl.CostEstimate(flops=10**9, bytes_accessed=2 * 10**6, transcendentals=0),
        name="fock_far",
    )(facts, pot, far_picks, phi_all)


def shards(density, basis_vals, kernel, starts, counts, pair_mask):
    grid_size, planes = lax.axis_size("grid"), lax.axis_size("basis")
    batches, share = basis_vals.shape[0], density.shape[2]
    grid_pos = lax.axis_index("grid")
    core = lax.rem(grid_pos, 2)
    phi_all, facts, pot, picks, far_picks = potentials(
        basis_vals, density, starts, counts, pair_mask, kernel, grid_size // 2, planes)
    pot = pot.reshape(SLOTS * batches, 2 * PERTS, POINTS // 2)
    picks = picks.reshape(2 * SLOTS * batches, 2, share, POINTS // 2)
    far_picks = far_picks.reshape(2 * batches, share, POINTS // 2)
    far = fock_far(facts, pot, far_picks, phi_all, share)
    route = [(i, (i + 1) % grid_size if i % 2 else (i - 1) % grid_size) for i in range(grid_size)]
    arrived = lax.ppermute(far, "grid", route)
    own = fock_own(facts, pot, picks, phi_all, share)
    mask_row = lax.dynamic_slice(pair_mask, (2 * grid_pos + core, core * REACH), (1, WINDOW))[0]
    keep = jnp.repeat(mask_row, BLOCK).astype(jnp.float32)
    place = (core, 0, 0, core * REACH * BLOCK)
    present = lax.dynamic_slice(own, place, (1, PERTS, share, COLS))
    return lax.dynamic_update_slice(own, present + (arrived * keep)[None], place)


def solution(mesh):
    placed = (
        P("grid", None, "basis", None),
        P("grid", None, None),
        P("grid", None),
        P("grid"),
        P("grid"),
        P(),
    )
    return jax.shard_map(
        shards,
        mesh=mesh,
        in_specs=placed,
        out_specs=P("grid", None, "basis", None),
        check_vma=False,
    )
```

```python
import functools

import jax
import jax.numpy as jnp
from jax import lax
from jax.experimental import pallas as pl
from jax.experimental.pallas import tpu as pltpu
from jax.sharding import PartitionSpec as P

BLOCK = 128
PERTS = 12
WINDOW = 6
POINTS = 256
REACH = 5
BAND = 11
COLS = WINDOW * BLOCK
WIDE = BAND * BLOCK
SLOTS = 6
MESH = pl.DeviceIdType.MESH
NT = (((1,), (1,)), ((), ()))


def one_hot(share, columns, first):
    rows = lax.broadcasted_iota(jnp.int32, (share, columns), 0)
    lanes = lax.broadcasted_iota(jnp.int32, (share, columns), 1)
    return jnp.where(lanes == rows + first, 1.0, 0.0).astype(jnp.bfloat16)


def density_kernel(
    chips, planes, batches, share,
    phi_ref, dens_ref, starts_ref, counts_ref, mask_ref, kern_ref,
    all_ref, facts_ref, pot_ref, picks_ref, far_picks_ref,
    phi_v, dens_v, far_v, left_v, left_far, meta_v, meta_all_v, facts_v, meta_s, mask_s, picks_v, far_picks_v, part, gathered, pot_v,
    own_sem, out_sem, core_s, core_r, y_s, y_r, z_s, z_r, c_s, c_r, m_s, m_r, f_sem, a_s, a_r, b_s, b_r,
):
    grid_pos, plane = lax.axis_index("grid"), lax.axis_index("basis")
    chip, core = grid_pos // 2, lax.rem(grid_pos, 2)
    half = batches // 2
    quarter = half // 2
    per_plane = batches // planes
    own_slot = 2 + core
    far_slot = jnp.where(core == 0, 4, 1)
    first = lax.rem(plane, 2) * half
    there = half - first
    rows_all = PERTS * share
    cut = POINTS // 2

    def device(slot, at_plane):
        return (2 * lax.rem(chip + slot // 2 - 1 + chips, chips) + lax.rem(slot, 2), at_plane)

    other = (2 * chip + 1 - core, plane)

    def remote(src, dst, send, recv, to):
        return pltpu.make_async_remote_copy(
            src_ref=src, dst_ref=dst, send_sem=send, recv_sem=recv, device_id=to, device_id_type=MESH)

    def is_other(slot, at_plane):
        return jnp.logical_or(slot != own_slot, at_plane != plane)

    def for_others(act):
        @pl.loop(0, SLOTS * planes)
        def _(no):
            slot, at_plane = no // planes, lax.rem(no, planes)

            @pl.when(is_other(slot, at_plane))
            def _():
                act(slot, at_plane)

    own_copy = pltpu.make_async_copy(phi_ref, phi_v.at[own_slot], own_sem.at[0])
    own_copy.start()
    dens_copy = pltpu.make_async_copy(dens_ref, left_v, own_sem.at[1])
    dens_copy.start()
    mask_copy = pltpu.make_async_copy(mask_ref, mask_s, own_sem.at[2])
    mask_copy.start()

    line = lax.broadcasted_iota(jnp.int32, (8, BLOCK), 0)
    lane = lax.broadcasted_iota(jnp.int32, (8, BLOCK), 1)
    meta = jnp.zeros((8, BLOCK), jnp.int32)
    for no in range(batches):
        meta = jnp.where(lane == no, starts_ref[no], meta)
        meta = jnp.where(lane == batches + no, counts_ref[no], meta)
    meta_v[...] = meta
    meta_all_v[own_slot] = meta

    barrier = pltpu.get_barrier_semaphore()
    for slot in (0, 1, 4, 5):
        pl.semaphore_signal(barrier, inc=1, device_id=device(slot, plane), device_id_type=MESH)
    for partner in (other, (grid_pos, lax.rem(plane + 1, planes)), (grid_pos, lax.rem(plane + planes - 1, planes))):
        pl.semaphore_signal(barrier, inc=1, device_id=partner, device_id_type=MESH)
    pl.semaphore_wait(barrier, 7)

    def piece(way, n):
        return n // 2 + quarter * lax.rem(n + way, 2)

    def rows(h):
        return pl.ds(h * cut, cut)

    def y_copy(way, n, h):
        at = first + piece(way, n)
        return remote(phi_ref.at[at, rows(h)], phi_v.at[4 * way + core, at, rows(h)], y_s.at[way, n, h], y_r.at[way, n, h],
                      device(4 - 4 * way + core, plane))

    def z_copy(way, n, h):
        which = piece(way, n)
        where = phi_v.at[4 * way + core, first + which, rows(h)]
        to = lax.rem(plane + 1 - 2 * (which // quarter) + planes, planes)
        return remote(where, where, z_s.at[way, n, h], z_r.at[way, n, h], (grid_pos, to))

    def c_copy(way, m, h):
        at = jnp.where(m < half, first, there) + piece(way, lax.rem(m, half))
        where = phi_v.at[4 * way + core, at, rows(h)]
        return remote(where, where, c_s.at[way, m, h], c_r.at[way, m, h], other)

    def core_copy(no):
        return remote(phi_ref.at[no], phi_v.at[own_slot, no], core_s.at[no], core_r.at[no], other)

    def meta_copy(way, s):
        return remote(meta_v, meta_all_v.at[4 * way + core], m_s.at[1 + 2 * way + s], m_r.at[1 + 2 * way + core],
                      device(4 - 4 * way + s, plane))

    def out_copy(slot, no):
        return pltpu.make_async_copy(phi_v.at[slot, no], all_ref.at[slot, no], out_sem.at[slot, no])

    far_copy = remote(dens_ref.at[core, :, :, pl.ds(pl.multiple_of(core * REACH * BLOCK, BLOCK), COLS)], left_far,
                      f_sem.at[0], f_sem.at[1], device(jnp.where(core == 0, 1, 4), plane))
    core_meta = remote(meta_v, meta_all_v.at[own_slot], m_s.at[0], m_r.at[0], other)

    core_meta.start()
    for way in range(2):
        for s in range(2):
            meta_copy(way, s).start()

    @pl.loop(0, half)
    def _(n):
        for h in range(2):
            for way in range(2):
                y_copy(way, n, h).start()

    far_copy.start()

    @pl.loop(0, batches)
    def _(no):
        core_copy(no).start()

    def masked(block, keep):
        return block * keep.astype(jnp.float32).astype(block.dtype)

    def same(left, right):
        return (1 - jnp.minimum(jnp.abs(left - right), 1)).astype(jnp.float32)

    mask_copy.wait()
    dens_copy.wait()
    for r in range(2):
        row = 2 * grid_pos + r
        for t in range(BAND):
            block = left_v[r, :, :, t * BLOCK:(t + 1) * BLOCK].reshape(rows_all, BLOCK)
            dens_v[r, t, :rows_all, :] = masked(block, mask_s[t, row])
            dens_v[r, t, rows_all:, :] = one_hot(share, BLOCK, (REACH - t) * BLOCK + plane * share)
    far_v[rows_all:, :] = one_hot(share, COLS, core * REACH * BLOCK + plane * share)

    own_copy.wait()
    for no in range(5):
        pltpu.make_async_copy(meta_v, meta_all_v.at[own_slot], m_r.at[no]).wait()
    facts = jnp.zeros((8, BLOCK), jnp.int32)
    for slot in range(SLOTS):
        facts = jnp.where(line == slot, meta_all_v[slot], facts)
    for r in range(2):
        for t in range(BAND):
            facts = jnp.where(jnp.logical_and(line == SLOTS + r, lane == t), mask_s[t, 2 * grid_pos + r], facts)
    facts_v[...] = facts
    to_smem = pltpu.make_async_copy(facts_v, meta_s, own_sem.at[3])
    to_smem.start()
    facts_out = pltpu.make_async_copy(facts_v, facts_ref, own_sem.at[4])
    facts_out.start()
    to_smem.wait()

    def reduced(mixed, keep_picks):
        picked = mixed[rows_all:]
        for h in range(2):
            keep_picks(h, picked[:, h * cut:(h + 1) * cut].astype(jnp.bfloat16))
        sums = jnp.sum(mixed[:rows_all].reshape(PERTS, share, POINTS) * picked[None], axis=1)
        return jnp.concatenate([sums[:, :cut], sums[:, cut:]], axis=0)

    def spread_rows(slot, no, r):
        offset = 2 * grid_pos + r - meta_s[slot, no]
        inside = jnp.clip(offset, 0, WINDOW - 1)
        lhs = jnp.concatenate([dens_v[r, REACH - inside + c] for c in range(WINDOW)], axis=1)
        return lhs, same(offset, inside)

    def rho_part(slot, no, blocks):
        out_copy(slot, no).start()
        lhs, keeps = zip(*[spread_rows(slot, no, r) for r in blocks])
        mixed = lax.dot_general(jnp.concatenate(lhs, axis=0), phi_v[slot, no], NT, preferred_element_type=jnp.float32)
        total = None
        for i, r in enumerate(blocks):
            def keep_picks(h, value, r=r):
                picks_v[slot, no, h, r] = value

            term = reduced(mixed[i * (rows_all + share):(i + 1) * (rows_all + share)], keep_picks) * keeps[i]
            total = term if total is None else total + term
        part[slot, no] = total

    far_start = 4 * chip - 1

    def rho_far(pair):
        phi = phi_v[far_slot, pl.ds(2 * pair, 2)].reshape(2 * POINTS, COLS)
        mixed = lax.dot_general(far_v[...], phi, NT, preferred_element_type=jnp.float32)
        for i in range(2):
            no = 2 * pair + i

            def keep_picks(h, value, no=no):
                far_picks_v[no, h] = value

            term = reduced(mixed[:, i * POINTS:(i + 1) * POINTS], keep_picks)
            part[far_slot, no] = part[far_slot, no] + term * same(meta_s[far_slot, no], far_start)

    def part_copy(slot, no):
        back = 2 * (2 - slot // 2) + core
        keeper = no // per_plane
        which = lax.rem(no, per_plane)
        return remote(part.at[slot, no], gathered.at[back, plane, which], a_s.at[slot, no], a_r.at[back, plane, which],
                      device(slot, keeper))

    def send_part(slot, no):
        away = is_other(slot, no // per_plane)

        @pl.when(away)
        def _():
            part_copy(slot, no).start()

        @pl.when(jnp.logical_not(away))
        def _():
            gathered[own_slot, plane, lax.rem(no, per_plane)] = part[slot, no]

    def pair(n, crossed, late):
        lead = jnp.where(crossed, core, 0)
        at = jnp.where(late, there, first)
        return tuple((4 * way + jnp.where(crossed, 1 - core, core), at + piece(way, n)) for way in (lead, 1 - lead))

    def items_before(m, act):
        odd = lax.rem(m, 2) == 1

        @pl.loop(0, 3)
        def _(item):
            mine = 2 * (m + 1) + item - 1
            slot = jnp.where(mine < half, own_slot, 5 - own_slot)
            at = 2 * lax.rem(mine, half)
            arrived = pair(jnp.maximum(m - 1, 0) // 2, False, False)
            is_own = item > 0
            chosen = tuple((jnp.where(is_own, slot, s), jnp.where(is_own, at + i, no)) for i, (s, no) in enumerate(arrived))

            @pl.when(jnp.logical_or(jnp.logical_and(is_own, m <= 2),
                                    jnp.logical_and(jnp.logical_not(is_own), jnp.logical_and(odd, m <= 2 * half - 1))))
            def _():
                act(chosen, False)

        @pl.when(m >= 2)
        def _():
            act(pair((m - 2 - lax.rem(m, 2)) // 2, True, odd), True)

    def items_after(m, act):
        @pl.when(jnp.logical_and(m >= 2, jnp.logical_and(lax.rem(m, 2) == 0, m <= 2 * half)))
        def _():
            act(pair((m - 2) // 2, False, True), False)

    def compute(batch_pair, crossed):
        rho_part(*batch_pair[0], (0, 1))
        rho_part(*batch_pair[1], (1 - core,) if crossed else (0, 1))

    def send(batch_pair, crossed):
        for slot, no in batch_pair:
            @pl.when(slot != far_slot)
            def _():
                send_part(slot, no)

    @pl.loop(0, 2 * half + 3)
    def _(step):
        m = step - 1

        @pl.when(jnp.logical_and(m >= 0, m < 2 * half))
        def _():
            n, h = m // 2, lax.rem(m, 2)
            for way in range(2):
                y_copy(way, n, h).wait_recv()
                z_copy(way, n, h).start()
                c_copy(way, n, h).start()

        @pl.when(jnp.logical_or(m == 1, m == 2))
        def _():
            for i in range(half):
                core_copy((m - 1) * half + i).wait_recv()

        @pl.when(m >= 2)
        def _():
            late = lax.rem(m, 2)
            for way in range(2):
                for h in range(2):
                    c_copy(way, late * half + (m - 2 - late) // 2, h).wait_recv()

        @pl.when(m == half + 1)
        def _():
            @pl.loop(0, half + 2)
            def _(before):
                items_before(before - 1, send)
                items_after(before - 1, send)

        items_before(m, compute)

        @pl.when(m > half)
        def _():
            items_before(m, send)

        @pl.when(jnp.logical_and(m >= 1, m <= 2 * half))
        def _():
            n, h = (m - 1) // 2, lax.rem(m - 1, 2)
            for way in range(2):
                z_copy(way, n, h).wait_recv()
                c_copy(way, half + n, h).start()

        items_after(m, compute)

        @pl.when(m > half)
        def _():
            items_after(m, send)

    far_copy.wait_recv()
    far_row = jnp.where(core == 0, jnp.maximum(2 * grid_pos - 1, 0), jnp.minimum(2 * grid_pos + 2, 4 * chips - 1))
    for t in range(WINDOW):
        block = left_far[:, :, t * BLOCK:(t + 1) * BLOCK].reshape(rows_all, BLOCK)
        keep = mask_s[jnp.where(core == 0, REACH, 0) + t, far_row]
        far_v[:rows_all, t * BLOCK:(t + 1) * BLOCK] = masked(block, keep)

    @pl.loop(0, half)
    def _(two):
        rho_far(two)
        for i in range(2):
            send_part(far_slot, 2 * two + i)

    picks_out = pltpu.make_async_copy(picks_v, picks_ref, own_sem.at[1])
    picks_out.start()
    far_picks_out = pltpu.make_async_copy(far_picks_v, far_picks_ref, own_sem.at[2])
    far_picks_out.start()

    def pot_copy(slot, at_plane):
        back = 2 * (2 - slot // 2) + core
        return remote(pot_v, pot_ref.at[back, plane], b_s.at[slot, at_plane], b_r.at[back, plane],
                      device(slot, at_plane))

    def wait_parts(slot, at_plane):
        for which in range(per_plane):
            pltpu.make_async_copy(part.at[0, 0], gathered.at[slot, at_plane, which], a_r.at[slot, at_plane, which]).wait()

    for_others(wait_parts)
    points = lax.broadcasted_iota(jnp.int32, (1, POINTS), 1)
    for no in range(per_plane):
        rho = gathered[0, 0, no]
        for slot in range(SLOTS):
            for at_plane in range(planes):
                if slot or at_plane:
                    rho = rho + gathered[slot, at_plane, no]
        mine = per_plane * plane + no
        live = jnp.clip(counts_ref[mine] - points, 0, 1).astype(jnp.float32)
        factor = jnp.broadcast_to(kern_ref[pl.ds(mine, 1), :] * live, (PERTS, POINTS))
        pot_v[no] = rho * jnp.concatenate([factor[:, :cut], factor[:, cut:]], axis=0)
    for_others(lambda slot, at_plane: pot_copy(slot, at_plane).start())
    pot_own = pltpu.make_async_copy(pot_v, pot_ref.at[own_slot, plane], own_sem.at[0])
    pot_own.start()

    facts_out.wait()
    picks_out.wait()
    far_picks_out.wait()
    far_copy.wait_send()
    core_meta.wait_send()
    for way in range(2):
        for s in range(2):
            meta_copy(way, s).wait_send()

    @pl.loop(0, batches)
    def _(no):
        core_copy(no).wait_send()
        for slot in range(SLOTS):
            out_copy(slot, no).wait()

            @pl.when(is_other(slot, no // per_plane))
            def _():
                part_copy(slot, no).wait_send()

    @pl.loop(0, half)
    def _(n):
        for h in range(2):
            for way in range(2):
                y_copy(way, n, h).wait_send()
                z_copy(way, n, h).wait_send()
                c_copy(way, n, h).wait_send()
                c_copy(way, half + n, h).wait_send()

    for_others(lambda slot, at_plane: pltpu.make_async_copy(
        pot_v, pot_ref.at[slot, at_plane], b_r.at[slot, at_plane]).wait())
    pot_own.wait()
    for_others(lambda slot, at_plane: pot_copy(slot, at_plane).wait_send())


def potentials(phi, density, starts, counts, pair_mask, kern, chips, planes):
    batches, points, cols = phi.shape
    share = density.shape[2]
    half, per_plane = batches // 2, batches // planes
    rows = PERTS * share + share
    far = pl.BlockSpec(memory_space=pl.ANY)
    smem = pl.BlockSpec(memory_space=pltpu.SMEM)
    vmem = pl.BlockSpec(memory_space=pltpu.VMEM)
    dma = pltpu.SemaphoreType.DMA
    f32 = jnp.float32
    row_pair = (2 * PERTS, points // 2)
    meta = (8, BLOCK)
    picks, far_picks = (SLOTS, batches, 2, 2, share, points // 2), (batches, 2, share, points // 2)
    return pl.pallas_call(
        functools.partial(density_kernel, chips, planes, batches, share),
        out_shape=(
            jax.ShapeDtypeStruct((SLOTS, batches, points, cols), phi.dtype),
            jax.ShapeDtypeStruct(meta, starts.dtype),
            jax.ShapeDtypeStruct((SLOTS, planes, per_plane) + row_pair, f32),
            jax.ShapeDtypeStruct(picks, phi.dtype),
            jax.ShapeDtypeStruct(far_picks, phi.dtype),
        ),
        in_specs=[far, far, smem, smem, far, vmem],
        out_specs=[far] * 5,
        scratch_shapes=[
            pltpu.VMEM((SLOTS, batches, points, cols), phi.dtype),
            pltpu.VMEM((2, BAND, rows, BLOCK), density.dtype),
            pltpu.VMEM((rows, COLS), density.dtype),
            pltpu.VMEM(density.shape, density.dtype),
            pltpu.VMEM((PERTS, share, COLS), density.dtype),
            pltpu.VMEM(meta, starts.dtype),
            pltpu.VMEM((SLOTS,) + meta, starts.dtype),
            pltpu.VMEM(meta, starts.dtype),
            pltpu.SMEM(meta, starts.dtype),
            pltpu.SMEM(pair_mask.shape, pair_mask.dtype),
            pltpu.VMEM(picks, phi.dtype),
            pltpu.VMEM(far_picks, phi.dtype),
            pltpu.VMEM((SLOTS, batches) + row_pair, f32),
            pltpu.VMEM((SLOTS, planes, per_plane) + row_pair, f32),
            pltpu.VMEM((per_plane,) + row_pair, f32),
            dma((5,)), dma((SLOTS, batches)), dma((batches,)), dma((batches,)),
            dma((2, half, 2)), dma((2, half, 2)), dma((2, half, 2)), dma((2, half, 2)),
            dma((2, batches, 2)), dma((2, batches, 2)), dma((5,)), dma((5,)), dma((2,)),
            dma((SLOTS, batches)), dma((SLOTS, planes, per_plane)), dma((SLOTS, planes)), dma((SLOTS, planes)),
        ],
        compiler_params=pltpu.CompilerParams(collective_id=0, has_side_effects=True, vmem_limit_bytes=56 << 20),
        cost_estimate=pl.CostEstimate(flops=17 * 10**9, bytes_accessed=50 * 10**6, transcendentals=0),
        name="potentials",
    )(phi, density, starts, counts, pair_mask, kern)


def joined(halves):
    return jnp.concatenate([halves[:PERTS], halves[PERTS:]], axis=1)


def split_weights(pot, picked):
    weighted = (pot[:, None, :] * picked[None]).reshape(pot.shape[0] * picked.shape[0], picked.shape[1])
    high = weighted.astype(jnp.bfloat16)
    low = (weighted - high.astype(jnp.float32)).astype(jnp.bfloat16)
    return high, low


CUT = POINTS // 2
LARGEST = 4


class Chunks:
    def __init__(self, batches, facts_ref, pot, pick, phi_ref, listed, counted, buf, sems):
        self.batches, self.facts, self.pot, self.pick, self.phi = batches, facts_ref, pot, pick, phi_ref
        self.listed, self.counted, self.buf, self.sems = listed, counted, buf, sems

    def start(self, no):
        return self.facts[no // self.batches, lax.rem(no, self.batches)]

    def note(self, which, no, wanted):
        most = self.pot.shape[0] * 2
        many = self.facts[no // self.batches, self.batches + lax.rem(no, self.batches)] > CUT

        @pl.when(wanted)
        def _():
            have = self.counted[which]
            self.listed[which * most + have] = 2 * no
            self.listed[which * most + have + 1] = 2 * no + 1
            self.counted[which] = have + 1 + many.astype(jnp.int32)

    def copy(self, chunk):
        no, h = chunk // 2, lax.rem(chunk, 2)
        return pltpu.make_async_copy(
            self.phi.at[no // self.batches, lax.rem(no, self.batches), pl.ds(pl.multiple_of(h * CUT, CUT), CUT)],
            self.buf.at[chunk], self.sems.at[chunk])

    def fetch(self, which):
        @pl.loop(0, self.counted[which])
        def _(i):
            self.copy(self.listed[which * self.pot.shape[0] * 2 + i]).start()

    def group(self, which, at, size, rows):
        rights, highs, lows = [], [[] for _ in rows], [[] for _ in rows]
        for i in range(size):
            chunk = self.listed[which * self.pot.shape[0] * 2 + at + i]
            self.copy(chunk).wait()
            pots = self.pot[chunk // 2]
            pot = jnp.where(lax.rem(chunk, 2) == 0, pots[:PERTS], pots[PERTS:])
            rights.append(self.buf[chunk])
            for no, (row, _) in enumerate(rows):
                high, low = split_weights(pot, self.pick(chunk, row).astype(jnp.float32))
                highs[no].append(high)
                lows[no].append(low)
        right = jnp.concatenate(rights + rights, axis=0)
        left = jnp.concatenate(
            [jnp.concatenate(high + low, axis=1) for high, low in zip(highs, lows)], axis=0)
        total = jnp.dot(left, right, preferred_element_type=jnp.float32)
        depth = left.shape[0] // len(rows)
        for no, (_, spot) in enumerate(rows):
            spot[...] = spot[...] + total[no * depth:(no + 1) * depth].reshape(spot.shape)

    def add(self, which, rows):
        count = self.counted[which]
        size = LARGEST
        done = 0
        while size:
            times = (count - done) // size

            @pl.loop(0, times)
            def _(i, size=size, done=done):
                self.group(which, done + i * size, size, rows)

            done = done + times * size
            size //= 2


def fock_kernel(batches, share, facts_ref, pot_ref, picks_ref, phi_ref, out_ref,
                total, pot_v, picks_v, listed, counted, buf, sems, in_sem, out_sem):
    grid_pos = lax.axis_index("grid")
    pot_copy = pltpu.make_async_copy(pot_ref, pot_v, in_sem.at[0])
    pot_copy.start()
    picks_copy = pltpu.make_async_copy(picks_ref, picks_v, in_sem.at[1])
    picks_copy.start()
    chunks = Chunks(batches, facts_ref, pot_v, lambda chunk, row: picks_v[chunk, row], phi_ref, listed, counted, buf, sems)
    base = 2 * grid_pos - REACH
    leads = REACH + 2

    for lead in range(leads):
        counted[lead] = 0

    @pl.loop(0, SLOTS * batches)
    def _(no):
        lead = chunks.start(no) - base
        chunks.note(lead, no, jnp.logical_and(lead >= 0, lead < leads))

    chunks.fetch(0)
    chunks.fetch(1)
    total[...] = jnp.zeros_like(total)
    pot_copy.wait()
    picks_copy.wait()

    def spot(r, offset):
        return total.at[r, :, :, pl.ds(pl.multiple_of((REACH - offset) * BLOCK, BLOCK), COLS)]

    def out_copy(r, t):
        cols = pl.ds(pl.multiple_of(t * BLOCK, BLOCK), BLOCK)
        return pltpu.make_async_copy(total.at[r, :, :, cols], out_ref.at[r, :, :, cols], out_sem.at[r, t])

    def leave(r, t):
        @pl.when(facts_ref[SLOTS + r, t] == 0)
        def _():
            cols = pl.ds(pl.multiple_of(t * BLOCK, BLOCK), BLOCK)
            total[r, :, :, cols] = jnp.zeros((PERTS, share, BLOCK), jnp.float32)

        out_copy(r, t).start()

    @pl.loop(0, leads)
    def _(lead):
        @pl.when(lead + 2 < leads)
        def _():
            chunks.fetch(lead + 2)

        both = jnp.logical_and(lead >= 1, lead <= REACH)

        @pl.when(both)
        def _():
            offset = REACH - lead
            chunks.add(lead, [(0, spot(0, offset)), (1, spot(1, offset + 1))])

        @pl.when(jnp.logical_not(both))
        def _():
            r = jnp.where(lead == 0, 0, 1)
            offset = jnp.where(lead == 0, REACH, 0)
            chunks.add(lead, [(r, spot(r, offset))])

        @pl.loop(lead, jnp.where(lead == REACH, BAND, jnp.minimum(lead + 1, REACH + 1)))
        def _(t):
            leave(0, t)

        @pl.loop(jnp.maximum(lead - 1, 0), jnp.where(lead == REACH + 1, BAND, lead))
        def _(t):
            leave(1, t)

    @pl.loop(0, BAND)
    def _(t):
        for r in range(2):
            out_copy(r, t).wait()


def chunk_scratch(slots, batches, cols, lists, dtype):
    most = 2 * slots * batches
    return [
        pltpu.SMEM((lists * most,), jnp.int32),
        pltpu.SMEM((lists,), jnp.int32),
        pltpu.VMEM((most, CUT, cols), dtype),
        pltpu.SemaphoreType.DMA((most,)),
    ]


def fock_own(facts, pot, picks, phi_all, share):
    slots, batches, points, cols = phi_all.shape
    far = pl.BlockSpec(memory_space=pl.ANY)
    whole = (2, PERTS, share, WIDE)
    dma = pltpu.SemaphoreType.DMA
    return pl.pallas_call(
        functools.partial(fock_kernel, batches, share),
        out_shape=jax.ShapeDtypeStruct(whole, jnp.float32),
        in_specs=[pl.BlockSpec(memory_space=pltpu.SMEM), far, far, far],
        out_specs=far,
        scratch_shapes=[
            pltpu.VMEM(whole, jnp.float32), pltpu.VMEM(pot.shape, pot.dtype), pltpu.VMEM(picks.shape, picks.dtype),
        ]
        + chunk_scratch(slots, batches, cols, REACH + 2, phi_all.dtype)
        + [dma((2,)), dma((2, BAND))],
        compiler_params=pltpu.CompilerParams(vmem_limit_bytes=56 << 20),
        cost_estimate=pl.CostEstimate(flops=20 * 10**9, bytes_accessed=20 * 10**6, transcendentals=0),
        name="fock_own",
    )(facts, pot, picks, phi_all)


def far_kernel(batches, facts_ref, pot_ref, picks_ref, phi_ref, out_ref, listed, counted, buf, sems):
    grid_pos = lax.axis_index("grid")
    core = lax.rem(grid_pos, 2)
    slot = jnp.where(core == 0, 4, 1)
    far_start = 4 * (grid_pos // 2) - 1
    chunks = Chunks(batches, facts_ref, pot_ref, lambda chunk, row: picks_ref[chunk - 2 * batches * slot], phi_ref,
                    listed, counted, buf, sems)
    counted[0] = 0

    @pl.loop(0, batches)
    def _(no):
        chunks.note(0, slot * batches + no, chunks.start(slot * batches + no) == far_start)

    chunks.fetch(0)
    out_ref[...] = jnp.zeros_like(out_ref)
    chunks.add(0, [(0, out_ref)])


def fock_far(facts, pot, far_picks, phi_all, share):
    slots, batches, points, cols = phi_all.shape
    smem = pl.BlockSpec(memory_space=pltpu.SMEM)
    vmem = pl.BlockSpec(memory_space=pltpu.VMEM)
    return pl.pallas_call(
        functools.partial(far_kernel, batches),
        out_shape=jax.ShapeDtypeStruct((PERTS, share, COLS), jnp.float32),
        in_specs=[smem, vmem, vmem, pl.BlockSpec(memory_space=pl.ANY)],
        out_specs=vmem,
        scratch_shapes=chunk_scratch(slots, batches, cols, 1, phi_all.dtype),
        compiler_params=pltpu.CompilerParams(vmem_limit_bytes=56 << 20),
        cost_estimate=pl.CostEstimate(flops=10**9, bytes_accessed=2 * 10**6, transcendentals=0),
        name="fock_far",
    )(facts, pot, far_picks, phi_all)


def shards(density, basis_vals, kernel, starts, counts, pair_mask):
    grid_size, planes = lax.axis_size("grid"), lax.axis_size("basis")
    batches, share = basis_vals.shape[0], density.shape[2]
    grid_pos = lax.axis_index("grid")
    core = lax.rem(grid_pos, 2)
    phi_all, facts, pot, picks, far_picks = potentials(
        basis_vals, density, starts, counts, pair_mask.T, kernel, grid_size // 2, planes)
    pot = pot.reshape(SLOTS * batches, 2 * PERTS, POINTS // 2)
    picks = picks.reshape(2 * SLOTS * batches, 2, share, POINTS // 2)
    far_picks = far_picks.reshape(2 * batches, share, POINTS // 2)
    far = fock_far(facts, pot, far_picks, phi_all, share)
    route = [(i, (i + 1) % grid_size if i % 2 else (i - 1) % grid_size) for i in range(grid_size)]
    arrived = lax.ppermute(far, "grid", route)
    own = fock_own(facts, pot, picks, phi_all, share)
    mask_row = lax.dynamic_slice(pair_mask, (2 * grid_pos + core, core * REACH), (1, WINDOW))[0]
    keep = jnp.repeat(mask_row, BLOCK).astype(jnp.float32)
    place = (core, 0, 0, core * REACH * BLOCK)
    present = lax.dynamic_slice(own, place, (1, PERTS, share, COLS))
    return lax.dynamic_update_slice(own, present + (arrived * keep)[None], place)


def solution(mesh):
    placed = (
        P("grid", None, "basis", None),
        P("grid", None, None),
        P("grid", None),
        P("grid"),
        P("grid"),
        P(),
    )
    return jax.shard_map(
        shards,
        mesh=mesh,
        in_specs=placed,
        out_specs=P("grid", None, "basis", None),
        check_vma=False,
    )
```

```python
import functools

import jax
import jax.numpy as jnp
from jax import lax
from jax.experimental import pallas as pl
from jax.experimental.pallas import tpu as pltpu
from jax.sharding import PartitionSpec as P

BLOCK = 128
PERTS = 12
WINDOW = 6
POINTS = 256
REACH = 5
BAND = 11
COLS = WINDOW * BLOCK
WIDE = BAND * BLOCK
SLOTS = 6
MESH = pl.DeviceIdType.MESH
NT = (((1,), (1,)), ((), ()))


def one_hot(share, columns, first):
    rows = lax.broadcasted_iota(jnp.int32, (share, columns), 0)
    lanes = lax.broadcasted_iota(jnp.int32, (share, columns), 1)
    return jnp.where(lanes == rows + first, 1.0, 0.0).astype(jnp.bfloat16)


def density_kernel(
    chips, planes, batches, share,
    phi_ref, dens_ref, starts_ref, counts_ref, mask_ref, kern_ref,
    all_ref, facts_ref, pot_ref, picks_ref, far_picks_ref,
    phi_v, dens_v, far_v, left_v, left_far, meta_v, meta_all_v, facts_v, meta_s, mask_s, picks_v, far_picks_v, part, mate, gathered, pot_v,
    own_sem, out_sem, core_s, core_r, y_s, y_r, z_s, z_r, c_s, c_r, m_s, m_r, f_sem, k_s, k_r, a_s, a_r, b_s, b_r, g_s, g_r,
):
    grid_pos, plane = lax.axis_index("grid"), lax.axis_index("basis")
    chip, core = grid_pos // 2, lax.rem(grid_pos, 2)
    half = batches // 2
    quarter = half // 2
    per_plane = batches // planes
    own_slot = 2 + core
    far_slot = jnp.where(core == 0, 4, 1)
    first = lax.rem(plane, 2) * half
    there = half - first
    rows_all = PERTS * share
    cut = POINTS // 2

    def device(slot, at_plane):
        return (2 * lax.rem(chip + slot // 2 - 1 + chips, chips) + lax.rem(slot, 2), at_plane)

    other = (2 * chip + 1 - core, plane)

    def remote(src, dst, send, recv, to):
        return pltpu.make_async_remote_copy(
            src_ref=src, dst_ref=dst, send_sem=send, recv_sem=recv, device_id=to, device_id_type=MESH)

    def is_other(d, at_plane):
        return jnp.logical_or(d != 1, at_plane != plane)

    def for_others(act, order=(0, 2, 1)):
        @pl.loop(0, 3 * planes)
        def _(no):
            turn, at_plane = no // planes, lax.rem(no, planes)
            d = jnp.where(turn == 0, order[0], jnp.where(turn == 1, order[1], order[2]))

            @pl.when(is_other(d, at_plane))
            def _():
                act(d, at_plane)

    own_copy = pltpu.make_async_copy(phi_ref, phi_v.at[own_slot], own_sem.at[0])
    own_copy.start()
    dens_copy = pltpu.make_async_copy(dens_ref, left_v, own_sem.at[1])
    dens_copy.start()
    mask_copy = pltpu.make_async_copy(mask_ref, mask_s, own_sem.at[2])
    mask_copy.start()

    line = lax.broadcasted_iota(jnp.int32, (8, BLOCK), 0)
    lane = lax.broadcasted_iota(jnp.int32, (8, BLOCK), 1)
    meta = jnp.zeros((8, BLOCK), jnp.int32)
    for no in range(batches):
        meta = jnp.where(lane == no, starts_ref[no], meta)
        meta = jnp.where(lane == batches + no, counts_ref[no], meta)
    meta_v[...] = meta
    meta_all_v[own_slot] = meta

    barrier = pltpu.get_barrier_semaphore()
    for slot in (0, 1, 4, 5):
        pl.semaphore_signal(barrier, inc=1, device_id=device(slot, plane), device_id_type=MESH)
    for partner in (other, (grid_pos, lax.rem(plane + 1, planes)), (grid_pos, lax.rem(plane + planes - 1, planes))):
        pl.semaphore_signal(barrier, inc=1, device_id=partner, device_id_type=MESH)
    pl.semaphore_wait(barrier, 7)

    def piece(way, n):
        return n // 2 + quarter * lax.rem(n + way, 2)

    def rows(h):
        return pl.ds(h * cut, cut)

    def y_copy(way, n, h):
        at = first + piece(way, n)
        return remote(phi_ref.at[at, rows(h)], phi_v.at[4 * way + core, at, rows(h)], y_s.at[way, n, h], y_r.at[way, n, h],
                      device(4 - 4 * way + core, plane))

    def z_copy(way, n, h):
        which = piece(way, n)
        where = phi_v.at[4 * way + core, first + which, rows(h)]
        to = lax.rem(plane + 1 - 2 * (which // quarter) + planes, planes)
        return remote(where, where, z_s.at[way, n, h], z_r.at[way, n, h], (grid_pos, to))

    def c_copy(way, m, h):
        at = jnp.where(m < half, first, there) + piece(way, lax.rem(m, half))
        where = phi_v.at[4 * way + core, at, rows(h)]
        return remote(where, where, c_s.at[way, m, h], c_r.at[way, m, h], other)

    def core_copy(no):
        return remote(phi_ref.at[no], phi_v.at[own_slot, no], core_s.at[no], core_r.at[no], other)

    def meta_copy(way, s):
        return remote(meta_v, meta_all_v.at[4 * way + core], m_s.at[1 + 2 * way + s], m_r.at[1 + 2 * way + core],
                      device(4 - 4 * way + s, plane))

    def out_copy(slot, no):
        return pltpu.make_async_copy(phi_v.at[slot, no], all_ref.at[slot, no], out_sem.at[slot, no])

    far_copy = remote(dens_ref.at[core, :, :, pl.ds(pl.multiple_of(core * REACH * BLOCK, BLOCK), COLS)], left_far,
                      f_sem.at[0], f_sem.at[1], device(jnp.where(core == 0, 1, 4), plane))
    core_meta = remote(meta_v, meta_all_v.at[own_slot], m_s.at[0], m_r.at[0], other)

    core_meta.start()
    for way in range(2):
        for s in range(2):
            meta_copy(way, s).start()

    @pl.loop(0, half)
    def _(n):
        for h in range(2):
            for way in range(2):
                y_copy(way, n, h).start()

    far_copy.start()

    @pl.loop(0, batches)
    def _(no):
        core_copy(no).start()

    def masked(block, keep):
        return block * keep.astype(jnp.float32).astype(block.dtype)

    def same(left, right):
        return (1 - jnp.minimum(jnp.abs(left - right), 1)).astype(jnp.float32)

    mask_copy.wait()
    dens_copy.wait()
    for r in range(2):
        row = 2 * grid_pos + r
        for t in range(BAND):
            block = left_v[r, :, :, t * BLOCK:(t + 1) * BLOCK].reshape(rows_all, BLOCK)
            dens_v[r, t, :rows_all, :] = masked(block, mask_s[t, row])
            dens_v[r, t, rows_all:, :] = one_hot(share, BLOCK, (REACH - t) * BLOCK + plane * share)
    far_v[rows_all:, :] = one_hot(share, COLS, core * REACH * BLOCK + plane * share)

    own_copy.wait()
    for no in range(5):
        pltpu.make_async_copy(meta_v, meta_all_v.at[own_slot], m_r.at[no]).wait()
    facts = jnp.zeros((8, BLOCK), jnp.int32)
    for slot in range(SLOTS):
        facts = jnp.where(line == slot, meta_all_v[slot], facts)
    for r in range(2):
        for t in range(BAND):
            facts = jnp.where(jnp.logical_and(line == SLOTS + r, lane == t), mask_s[t, 2 * grid_pos + r], facts)
    facts_v[...] = facts
    to_smem = pltpu.make_async_copy(facts_v, meta_s, own_sem.at[3])
    to_smem.start()
    facts_out = pltpu.make_async_copy(facts_v, facts_ref, own_sem.at[4])
    facts_out.start()
    to_smem.wait()

    def reduced(mixed, keep_picks):
        picked = mixed[rows_all:]
        for h in range(2):
            keep_picks(h, picked[:, h * cut:(h + 1) * cut].astype(jnp.bfloat16))
        sums = jnp.sum(mixed[:rows_all].reshape(PERTS, share, POINTS) * picked[None], axis=1)
        return jnp.concatenate([sums[:, :cut], sums[:, cut:]], axis=0)

    def spread_rows(slot, no, r):
        offset = 2 * grid_pos + r - meta_s[slot, no]
        inside = jnp.clip(offset, 0, WINDOW - 1)
        lhs = jnp.concatenate([dens_v[r, REACH - inside + c] for c in range(WINDOW)], axis=1)
        return lhs, same(offset, inside)

    def rho_part(slot, no, blocks):
        out_copy(slot, no).start()
        lhs, keeps = zip(*[spread_rows(slot, no, r) for r in blocks])
        mixed = lax.dot_general(jnp.concatenate(lhs, axis=0), phi_v[slot, no], NT, preferred_element_type=jnp.float32)
        total = None
        for i, r in enumerate(blocks):
            def keep_picks(h, value, r=r):
                picks_v[slot, no, h, r] = value

            term = reduced(mixed[i * (rows_all + share):(i + 1) * (rows_all + share)], keep_picks) * keeps[i]
            total = term if total is None else total + term
        part[slot, no] = total

    far_start = 4 * chip - 1

    def rho_far(pair):
        phi = phi_v[far_slot, pl.ds(2 * pair, 2)].reshape(2 * POINTS, COLS)
        mixed = lax.dot_general(far_v[...], phi, NT, preferred_element_type=jnp.float32)
        for i in range(2):
            no = 2 * pair + i

            def keep_picks(h, value, no=no):
                far_picks_v[no, h] = value

            term = reduced(mixed[:, i * POINTS:(i + 1) * POINTS], keep_picks)
            part[far_slot, no] = part[far_slot, no] + term * same(meta_s[far_slot, no], far_start)

    def mate_copy(d, no):
        return remote(part.at[2 * d + 1 - core, no], mate.at[d, no], k_s.at[d, no], k_r.at[d, no], other)

    def part_copy(d, no):
        keeper = no // per_plane
        which = lax.rem(no, per_plane)
        return remote(part.at[2 * d + core, no], gathered.at[2 - d, plane, which], a_s.at[d, no], a_r.at[2 - d, plane, which],
                      device(2 * d + core, keeper))

    def combine(d, no):
        slot = 2 * d + core
        pltpu.make_async_copy(part.at[slot, no], mate.at[d, no], k_r.at[d, no]).wait()
        part[slot, no] = part[slot, no] + mate[d, no]
        away = is_other(d, no // per_plane)

        @pl.when(away)
        def _():
            part_copy(d, no).start()

        @pl.when(jnp.logical_not(away))
        def _():
            gathered[1, plane, lax.rem(no, per_plane)] = part[slot, no]

    def pair(n, crossed, late):
        lead = jnp.where(crossed, core, 0)
        at = jnp.where(late, there, first)
        return tuple((4 * way + jnp.where(crossed, 1 - core, core), at + piece(way, n)) for way in (lead, 1 - lead))

    def items_before(m, act):
        odd = lax.rem(m, 2) == 1

        @pl.loop(0, 3)
        def _(item):
            mine = 2 * (m + 1) + item - 1
            slot = jnp.where(mine < half, own_slot, 5 - own_slot)
            at = 2 * lax.rem(mine, half)
            arrived = pair(jnp.maximum(m - 1, 0) // 2, False, False)
            is_own = item > 0
            chosen = tuple((jnp.where(is_own, slot, s), jnp.where(is_own, at + i, no)) for i, (s, no) in enumerate(arrived))

            @pl.when(jnp.logical_or(jnp.logical_and(is_own, m <= 2),
                                    jnp.logical_and(jnp.logical_not(is_own), jnp.logical_and(odd, m <= 2 * half - 1))))
            def _():
                act(chosen, False)

        @pl.when(m >= 2)
        def _():
            act(pair((m - 2 - lax.rem(m, 2)) // 2, True, odd), True)

    def items_after(m, act):
        @pl.when(jnp.logical_and(m >= 2, jnp.logical_and(lax.rem(m, 2) == 0, m <= 2 * half)))
        def _():
            act(pair((m - 2) // 2, False, True), False)

    def compute(batch_pair, crossed):
        rho_part(*batch_pair[0], (0, 1))
        rho_part(*batch_pair[1], (1 - core,) if crossed else (0, 1))
        for slot, no in batch_pair:
            @pl.when(lax.rem(slot, 2) != core)
            def _():
                mate_copy(slot // 2, no).start()

    def combine_pair(m):
        late = jnp.where(lax.rem(m, 2) == 0, 1, 0)
        for slot, no in pair((m - 3 - late) // 2, False, late == 1):
            @pl.when(slot != far_slot)
            def _():
                combine(slot // 2, no)

    @pl.loop(0, 2 * half + 3)
    def _(step):
        m = step - 1

        @pl.when(jnp.logical_and(m >= 0, m < 2 * half))
        def _():
            n, h = m // 2, lax.rem(m, 2)
            for way in range(2):
                y_copy(way, n, h).wait_recv()
                z_copy(way, n, h).start()
                c_copy(way, n, h).start()

        @pl.when(jnp.logical_or(m == 1, m == 2))
        def _():
            for i in range(half):
                core_copy((m - 1) * half + i).wait_recv()

        @pl.when(m >= 2)
        def _():
            late = lax.rem(m, 2)
            for way in range(2):
                for h in range(2):
                    c_copy(way, late * half + (m - 2 - late) // 2, h).wait_recv()

        @pl.when(m == half + 1)
        def _():
            @pl.loop(0, batches)
            def _(no):
                combine(1, no)

            @pl.loop(3, half + 1)
            def _(before):
                combine_pair(before)

        items_before(m, compute)

        @pl.when(jnp.logical_and(m >= 1, m <= 2 * half))
        def _():
            n, h = (m - 1) // 2, lax.rem(m - 1, 2)
            for way in range(2):
                z_copy(way, n, h).wait_recv()
                c_copy(way, half + n, h).start()

        items_after(m, compute)

        @pl.when(m > half)
        def _():
            combine_pair(m)

    combine_pair(2 * half + 2)
    far_copy.wait_recv()
    far_row = jnp.where(core == 0, jnp.maximum(2 * grid_pos - 1, 0), jnp.minimum(2 * grid_pos + 2, 4 * chips - 1))
    for t in range(WINDOW):
        block = left_far[:, :, t * BLOCK:(t + 1) * BLOCK].reshape(rows_all, BLOCK)
        keep = mask_s[jnp.where(core == 0, REACH, 0) + t, far_row]
        far_v[:rows_all, t * BLOCK:(t + 1) * BLOCK] = masked(block, keep)

    @pl.loop(0, half)
    def _(two):
        rho_far(two)
        for i in range(2):
            combine(far_slot // 2, 2 * two + i)

    picks_out = pltpu.make_async_copy(picks_v, picks_ref, own_sem.at[1])
    picks_out.start()
    far_picks_out = pltpu.make_async_copy(far_picks_v, far_picks_ref, own_sem.at[2])
    far_picks_out.start()

    def pot_copy(d, at_plane):
        return remote(pot_v, pot_ref.at[2 * (2 - d) + core, plane], b_s.at[d, at_plane], b_r.at[2 - d, plane],
                      device(2 * d + core, at_plane))

    def cross_copy(d, at_plane):
        where = pot_ref.at[2 * d + core, at_plane]
        return remote(where, where, g_s.at[d, at_plane], g_r.at[d, at_plane], other)

    own_cross = remote(pot_v, pot_ref.at[own_slot, plane], g_s.at[1, plane], g_r.at[1, plane], other)

    def wait_parts(d, at_plane):
        for which in range(per_plane):
            pltpu.make_async_copy(part.at[0, 0], gathered.at[d, at_plane, which], a_r.at[d, at_plane, which]).wait()

    for_others(wait_parts)
    points = lax.broadcasted_iota(jnp.int32, (1, POINTS), 1)
    for no in range(per_plane):
        rho = gathered[0, 0, no]
        for d in range(3):
            for at_plane in range(planes):
                if d or at_plane:
                    rho = rho + gathered[d, at_plane, no]
        mine = per_plane * plane + no
        live = jnp.clip(counts_ref[mine] - points, 0, 1).astype(jnp.float32)
        factor = jnp.broadcast_to(kern_ref[pl.ds(mine, 1), :] * live, (PERTS, POINTS))
        pot_v[no] = rho * jnp.concatenate([factor[:, :cut], factor[:, cut:]], axis=0)
    for_others(lambda d, at_plane: pot_copy(d, at_plane).start())
    own_cross.start()
    pot_own = pltpu.make_async_copy(pot_v, pot_ref.at[own_slot, plane], own_sem.at[0])
    pot_own.start()

    facts_out.wait()
    picks_out.wait()
    far_picks_out.wait()
    far_copy.wait_send()
    core_meta.wait_send()
    for way in range(2):
        for s in range(2):
            meta_copy(way, s).wait_send()

    @pl.loop(0, batches)
    def _(no):
        core_copy(no).wait_send()
        for slot in range(SLOTS):
            out_copy(slot, no).wait()
        for d in range(3):
            mate_copy(d, no).wait_send()

            @pl.when(is_other(d, no // per_plane))
            def _():
                part_copy(d, no).wait_send()

    @pl.loop(0, half)
    def _(n):
        for h in range(2):
            for way in range(2):
                y_copy(way, n, h).wait_send()
                z_copy(way, n, h).wait_send()
                c_copy(way, n, h).wait_send()
                c_copy(way, half + n, h).wait_send()

    def pass_on(d, at_plane):
        pltpu.make_async_copy(pot_v, pot_ref.at[2 * d + core, at_plane], b_r.at[d, at_plane]).wait()
        cross_copy(d, at_plane).start()

    for_others(pass_on, (1, 0, 2))

    @pl.loop(0, 3 * planes)
    def _(no):
        cross_copy(no // planes, lax.rem(no, planes)).wait_recv()

    pot_own.wait()
    own_cross.wait_send()
    for_others(lambda d, at_plane: cross_copy(d, at_plane).wait_send())
    for_others(lambda d, at_plane: pot_copy(d, at_plane).wait_send())


def potentials(phi, density, starts, counts, pair_mask, kern, chips, planes):
    batches, points, cols = phi.shape
    share = density.shape[2]
    half, per_plane = batches // 2, batches // planes
    rows = PERTS * share + share
    far = pl.BlockSpec(memory_space=pl.ANY)
    smem = pl.BlockSpec(memory_space=pltpu.SMEM)
    vmem = pl.BlockSpec(memory_space=pltpu.VMEM)
    dma = pltpu.SemaphoreType.DMA
    f32 = jnp.float32
    row_pair = (2 * PERTS, points // 2)
    meta = (8, BLOCK)
    picks, far_picks = (SLOTS, batches, 2, 2, share, points // 2), (batches, 2, share, points // 2)
    return pl.pallas_call(
        functools.partial(density_kernel, chips, planes, batches, share),
        out_shape=(
            jax.ShapeDtypeStruct((SLOTS, batches, points, cols), phi.dtype),
            jax.ShapeDtypeStruct(meta, starts.dtype),
            jax.ShapeDtypeStruct((SLOTS, planes, per_plane) + row_pair, f32),
            jax.ShapeDtypeStruct(picks, phi.dtype),
            jax.ShapeDtypeStruct(far_picks, phi.dtype),
        ),
        in_specs=[far, far, smem, smem, far, vmem],
        out_specs=[far] * 5,
        scratch_shapes=[
            pltpu.VMEM((SLOTS, batches, points, cols), phi.dtype),
            pltpu.VMEM((2, BAND, rows, BLOCK), density.dtype),
            pltpu.VMEM((rows, COLS), density.dtype),
            pltpu.VMEM(density.shape, density.dtype),
            pltpu.VMEM((PERTS, share, COLS), density.dtype),
            pltpu.VMEM(meta, starts.dtype),
            pltpu.VMEM((SLOTS,) + meta, starts.dtype),
            pltpu.VMEM(meta, starts.dtype),
            pltpu.SMEM(meta, starts.dtype),
            pltpu.SMEM(pair_mask.shape, pair_mask.dtype),
            pltpu.VMEM(picks, phi.dtype),
            pltpu.VMEM(far_picks, phi.dtype),
            pltpu.VMEM((SLOTS, batches) + row_pair, f32),
            pltpu.VMEM((3, batches) + row_pair, f32),
            pltpu.VMEM((3, planes, per_plane) + row_pair, f32),
            pltpu.VMEM((per_plane,) + row_pair, f32),
            dma((5,)), dma((SLOTS, batches)), dma((batches,)), dma((batches,)),
            dma((2, half, 2)), dma((2, half, 2)), dma((2, half, 2)), dma((2, half, 2)),
            dma((2, batches, 2)), dma((2, batches, 2)), dma((5,)), dma((5,)), dma((2,)),
            dma((3, batches)), dma((3, batches)), dma((3, batches)), dma((3, planes, per_plane)),
            dma((3, planes)), dma((3, planes)), dma((3, planes)), dma((3, planes)),
        ],
        compiler_params=pltpu.CompilerParams(collective_id=0, has_side_effects=True, vmem_limit_bytes=56 << 20),
        cost_estimate=pl.CostEstimate(flops=17 * 10**9, bytes_accessed=50 * 10**6, transcendentals=0),
        name="potentials",
    )(phi, density, starts, counts, pair_mask, kern)


def joined(halves):
    return jnp.concatenate([halves[:PERTS], halves[PERTS:]], axis=1)


def split_weights(pot, picked):
    weighted = (pot[:, None, :] * picked[None]).reshape(pot.shape[0] * picked.shape[0], picked.shape[1])
    high = weighted.astype(jnp.bfloat16)
    low = (weighted - high.astype(jnp.float32)).astype(jnp.bfloat16)
    return high, low


CUT = POINTS // 2
LARGEST = 8


class Chunks:
    def __init__(self, batches, facts_ref, pot, pick, phi_ref, listed, counted, buf, sems):
        self.batches, self.facts, self.pot, self.pick, self.phi = batches, facts_ref, pot, pick, phi_ref
        self.listed, self.counted, self.buf, self.sems = listed, counted, buf, sems

    def start(self, no):
        return self.facts[no // self.batches, lax.rem(no, self.batches)]

    def note(self, which, no, wanted):
        most = self.pot.shape[0] * 2
        many = self.facts[no // self.batches, self.batches + lax.rem(no, self.batches)] > CUT

        @pl.when(wanted)
        def _():
            have = self.counted[which]
            self.listed[which * most + have] = 2 * no
            self.listed[which * most + have + 1] = 2 * no + 1
            self.counted[which] = have + 1 + many.astype(jnp.int32)

    def copy(self, chunk):
        no, h = chunk // 2, lax.rem(chunk, 2)
        return pltpu.make_async_copy(
            self.phi.at[no // self.batches, lax.rem(no, self.batches), pl.ds(pl.multiple_of(h * CUT, CUT), CUT)],
            self.buf.at[chunk], self.sems.at[chunk])

    def fetch(self, which):
        @pl.loop(0, self.counted[which])
        def _(i):
            self.copy(self.listed[which * self.pot.shape[0] * 2 + i]).start()

    def group(self, which, at, size, rows):
        rights, highs, lows = [], [[] for _ in rows], [[] for _ in rows]
        for i in range(size):
            chunk = self.listed[which * self.pot.shape[0] * 2 + at + i]
            self.copy(chunk).wait()
            pots = self.pot[chunk // 2]
            pot = jnp.where(lax.rem(chunk, 2) == 0, pots[:PERTS], pots[PERTS:])
            rights.append(self.buf[chunk])
            for no, (row, _) in enumerate(rows):
                high, low = split_weights(pot, self.pick(chunk, row).astype(jnp.float32))
                highs[no].append(high)
                lows[no].append(low)
        right = jnp.concatenate(rights + rights, axis=0)
        left = jnp.concatenate(
            [jnp.concatenate(high + low, axis=1) for high, low in zip(highs, lows)], axis=0)
        total = jnp.dot(left, right, preferred_element_type=jnp.float32)
        depth = left.shape[0] // len(rows)
        for no, (_, spot) in enumerate(rows):
            spot[...] = spot[...] + total[no * depth:(no + 1) * depth].reshape(spot.shape)

    def add(self, which, rows):
        count = self.counted[which]
        size = LARGEST
        done = 0
        while size:
            times = (count - done) // size

            @pl.loop(0, times)
            def _(i, size=size, done=done):
                self.group(which, done + i * size, size, rows)

            done = done + times * size
            size //= 2


def fock_kernel(batches, share, facts_ref, pot_ref, picks_ref, phi_ref, out_ref,
                total, pot_v, picks_v, listed, counted, buf, sems, in_sem, out_sem):
    grid_pos = lax.axis_index("grid")
    pot_copy = pltpu.make_async_copy(pot_ref, pot_v, in_sem.at[0])
    pot_copy.start()
    picks_copy = pltpu.make_async_copy(picks_ref, picks_v, in_sem.at[1])
    picks_copy.start()
    chunks = Chunks(batches, facts_ref, pot_v, lambda chunk, row: picks_v[chunk, row], phi_ref, listed, counted, buf, sems)
    base = 2 * grid_pos - REACH
    leads = REACH + 2

    for lead in range(leads):
        counted[lead] = 0

    @pl.loop(0, SLOTS * batches)
    def _(no):
        lead = chunks.start(no) - base
        chunks.note(lead, no, jnp.logical_and(lead >= 0, lead < leads))

    chunks.fetch(0)
    chunks.fetch(1)
    total[...] = jnp.zeros_like(total)
    pot_copy.wait()
    picks_copy.wait()

    def spot(r, offset):
        return total.at[r, :, :, pl.ds(pl.multiple_of((REACH - offset) * BLOCK, BLOCK), COLS)]

    def out_copy(r, t):
        cols = pl.ds(pl.multiple_of(t * BLOCK, BLOCK), BLOCK)
        return pltpu.make_async_copy(total.at[r, :, :, cols], out_ref.at[r, :, :, cols], out_sem.at[r, t])

    def leave(r, t):
        @pl.when(facts_ref[SLOTS + r, t] == 0)
        def _():
            cols = pl.ds(pl.multiple_of(t * BLOCK, BLOCK), BLOCK)
            total[r, :, :, cols] = jnp.zeros((PERTS, share, BLOCK), jnp.float32)

        out_copy(r, t).start()

    @pl.loop(0, leads)
    def _(lead):
        @pl.when(lead + 2 < leads)
        def _():
            chunks.fetch(lead + 2)

        both = jnp.logical_and(lead >= 1, lead <= REACH)

        @pl.when(both)
        def _():
            offset = REACH - lead
            chunks.add(lead, [(0, spot(0, offset)), (1, spot(1, offset + 1))])

        @pl.when(jnp.logical_not(both))
        def _():
            r = jnp.where(lead == 0, 0, 1)
            offset = jnp.where(lead == 0, REACH, 0)
            chunks.add(lead, [(r, spot(r, offset))])

        @pl.loop(lead, jnp.where(lead == REACH, BAND, jnp.minimum(lead + 1, REACH + 1)))
        def _(t):
            leave(0, t)

        @pl.loop(jnp.maximum(lead - 1, 0), jnp.where(lead == REACH + 1, BAND, lead))
        def _(t):
            leave(1, t)

    @pl.loop(0, BAND)
    def _(t):
        for r in range(2):
            out_copy(r, t).wait()


def chunk_scratch(slots, batches, cols, lists, dtype):
    most = 2 * slots * batches
    return [
        pltpu.SMEM((lists * most,), jnp.int32),
        pltpu.SMEM((lists,), jnp.int32),
        pltpu.VMEM((most, CUT, cols), dtype),
        pltpu.SemaphoreType.DMA((most,)),
    ]


def fock_own(facts, pot, picks, phi_all, share):
    slots, batches, points, cols = phi_all.shape
    far = pl.BlockSpec(memory_space=pl.ANY)
    whole = (2, PERTS, share, WIDE)
    dma = pltpu.SemaphoreType.DMA
    return pl.pallas_call(
        functools.partial(fock_kernel, batches, share),
        out_shape=jax.ShapeDtypeStruct(whole, jnp.float32),
        in_specs=[pl.BlockSpec(memory_space=pltpu.SMEM), far, far, far],
        out_specs=far,
        scratch_shapes=[
            pltpu.VMEM(whole, jnp.float32), pltpu.VMEM(pot.shape, pot.dtype), pltpu.VMEM(picks.shape, picks.dtype),
        ]
        + chunk_scratch(slots, batches, cols, REACH + 2, phi_all.dtype)
        + [dma((2,)), dma((2, BAND))],
        compiler_params=pltpu.CompilerParams(vmem_limit_bytes=56 << 20),
        cost_estimate=pl.CostEstimate(flops=20 * 10**9, bytes_accessed=20 * 10**6, transcendentals=0),
        name="fock_own",
    )(facts, pot, picks, phi_all)


def far_kernel(batches, facts_ref, pot_ref, picks_ref, phi_ref, out_ref, pot_v, picks_v, listed, counted, buf, sems, in_sem):
    grid_pos = lax.axis_index("grid")
    core = lax.rem(grid_pos, 2)
    slot = jnp.where(core == 0, 4, 1)
    far_start = 4 * (grid_pos // 2) - 1
    own = pl.ds(slot * batches, batches)
    pot_copy = pltpu.make_async_copy(pot_ref.at[own], pot_v.at[own], in_sem.at[0])
    pot_copy.start()
    picks_copy = pltpu.make_async_copy(picks_ref, picks_v, in_sem.at[1])
    picks_copy.start()
    chunks = Chunks(batches, facts_ref, pot_v, lambda chunk, row: picks_v[chunk - 2 * batches * slot], phi_ref,
                    listed, counted, buf, sems)
    counted[0] = 0

    @pl.loop(0, batches)
    def _(no):
        chunks.note(0, slot * batches + no, chunks.start(slot * batches + no) == far_start)

    chunks.fetch(0)
    out_ref[...] = jnp.zeros_like(out_ref)
    pot_copy.wait()
    picks_copy.wait()
    chunks.add(0, [(0, out_ref)])


def fock_far(facts, pot, far_picks, phi_all, share):
    slots, batches, points, cols = phi_all.shape
    smem = pl.BlockSpec(memory_space=pltpu.SMEM)
    far = pl.BlockSpec(memory_space=pl.ANY)
    vmem = pl.BlockSpec(memory_space=pltpu.VMEM)
    return pl.pallas_call(
        functools.partial(far_kernel, batches),
        out_shape=jax.ShapeDtypeStruct((PERTS, share, COLS), jnp.float32),
        in_specs=[smem, far, far, far],
        out_specs=vmem,
        scratch_shapes=[pltpu.VMEM(pot.shape, pot.dtype), pltpu.VMEM(far_picks.shape, far_picks.dtype)]
        + chunk_scratch(slots, batches, cols, 1, phi_all.dtype)
        + [pltpu.SemaphoreType.DMA((2,))],
        compiler_params=pltpu.CompilerParams(vmem_limit_bytes=56 << 20),
        cost_estimate=pl.CostEstimate(flops=10**9, bytes_accessed=2 * 10**6, transcendentals=0),
        name="fock_far",
    )(facts, pot, far_picks, phi_all)


def shards(density, basis_vals, kernel, starts, counts, pair_mask):
    grid_size, planes = lax.axis_size("grid"), lax.axis_size("basis")
    batches, share = basis_vals.shape[0], density.shape[2]
    grid_pos = lax.axis_index("grid")
    core = lax.rem(grid_pos, 2)
    phi_all, facts, pot, picks, far_picks = potentials(
        basis_vals, density, starts, counts, pair_mask.T, kernel, grid_size // 2, planes)
    pot = pot.reshape(SLOTS * batches, 2 * PERTS, POINTS // 2)
    picks = picks.reshape(2 * SLOTS * batches, 2, share, POINTS // 2)
    far_picks = far_picks.reshape(2 * batches, share, POINTS // 2)
    far = fock_far(facts, pot, far_picks, phi_all, share)
    route = [(i, (i + 1) % grid_size if i % 2 else (i - 1) % grid_size) for i in range(grid_size)]
    arrived = lax.ppermute(far, "grid", route)
    own = fock_own(facts, pot, picks, phi_all, share)
    mask_row = lax.dynamic_slice(pair_mask, (2 * grid_pos + core, core * REACH), (1, WINDOW))[0]
    keep = jnp.repeat(mask_row, BLOCK).astype(jnp.float32)
    place = (core, 0, 0, core * REACH * BLOCK)
    present = lax.dynamic_slice(own, place, (1, PERTS, share, COLS))
    return lax.dynamic_update_slice(own, present + (arrived * keep)[None], place)


def solution(mesh):
    placed = (
        P("grid", None, "basis", None),
        P("grid", None, None),
        P("grid", None),
        P("grid"),
        P("grid"),
        P(),
    )
    return jax.shard_map(
        shards,
        mesh=mesh,
        in_specs=placed,
        out_specs=P("grid", None, "basis", None),
        check_vma=False,
    )
```

```python
import functools

import jax
import jax.numpy as jnp
from jax import lax
from jax.experimental import pallas as pl
from jax.experimental.pallas import tpu as pltpu
from jax.sharding import PartitionSpec as P

BLOCK = 128
PERTS = 12
WINDOW = 6
POINTS = 256
REACH = 5
BAND = 11
COLS = WINDOW * BLOCK
WIDE = BAND * BLOCK
SLOTS = 6
MESH = pl.DeviceIdType.MESH
NT = (((1,), (1,)), ((), ()))


def one_hot(share, columns, first):
    rows = lax.broadcasted_iota(jnp.int32, (share, columns), 0)
    lanes = lax.broadcasted_iota(jnp.int32, (share, columns), 1)
    return jnp.where(lanes == rows + first, 1.0, 0.0).astype(jnp.bfloat16)


def density_kernel(
    chips, planes, batches, share,
    phi_ref, dens_ref, starts_ref, counts_ref, mask_ref, kern_ref,
    all_ref, facts_ref, pot_ref, picks_ref, far_picks_ref,
    phi_v, dens_v, far_v, left_v, left_far, meta_v, meta_all_v, facts_v, meta_s, mask_s, picks_v, far_picks_v, part, mate, gathered, pot_v,
    own_sem, out_sem, core_s, core_r, y_s, y_r, z_s, z_r, c_s, c_r, m_s, m_r, f_sem, k_s, k_r, a_s, a_r, b_s, b_r, g_s, g_r,
):
    grid_pos, plane = lax.axis_index("grid"), lax.axis_index("basis")
    chip, core = grid_pos // 2, lax.rem(grid_pos, 2)
    half = batches // 2
    quarter = half // 2
    per_plane = batches // planes
    own_slot = 2 + core
    far_slot = jnp.where(core == 0, 4, 1)
    first = lax.rem(plane, 2) * half
    there = half - first
    rows_all = PERTS * share
    cut = POINTS // 2

    def device(slot, at_plane):
        return (2 * lax.rem(chip + slot // 2 - 1 + chips, chips) + lax.rem(slot, 2), at_plane)

    other = (2 * chip + 1 - core, plane)

    def remote(src, dst, send, recv, to):
        return pltpu.make_async_remote_copy(
            src_ref=src, dst_ref=dst, send_sem=send, recv_sem=recv, device_id=to, device_id_type=MESH)

    def is_other(d, at_plane):
        return jnp.logical_or(d != 1, at_plane != plane)

    def for_others(act, order=(0, 2, 1)):
        @pl.loop(0, 3 * planes)
        def _(no):
            turn, at_plane = no // planes, lax.rem(no, planes)
            d = jnp.where(turn == 0, order[0], jnp.where(turn == 1, order[1], order[2]))

            @pl.when(is_other(d, at_plane))
            def _():
                act(d, at_plane)

    own_copy = pltpu.make_async_copy(phi_ref, phi_v.at[own_slot], own_sem.at[0])
    own_copy.start()
    dens_copy = pltpu.make_async_copy(dens_ref, left_v, own_sem.at[1])
    dens_copy.start()
    mask_copy = pltpu.make_async_copy(mask_ref, mask_s, own_sem.at[2])
    mask_copy.start()

    line = lax.broadcasted_iota(jnp.int32, (8, BLOCK), 0)
    lane = lax.broadcasted_iota(jnp.int32, (8, BLOCK), 1)
    meta = jnp.zeros((8, BLOCK), jnp.int32)
    for no in range(batches):
        meta = jnp.where(lane == no, starts_ref[no], meta)
        meta = jnp.where(lane == batches + no, counts_ref[no], meta)
    meta_v[...] = meta
    meta_all_v[own_slot] = meta

    barrier = pltpu.get_barrier_semaphore()
    for slot in (0, 1, 4, 5):
        pl.semaphore_signal(barrier, inc=1, device_id=device(slot, plane), device_id_type=MESH)
    for partner in (other, (grid_pos, lax.rem(plane + 1, planes)), (grid_pos, lax.rem(plane + planes - 1, planes))):
        pl.semaphore_signal(barrier, inc=1, device_id=partner, device_id_type=MESH)
    pl.semaphore_wait(barrier, 7)

    def piece(way, n):
        return n // 2 + quarter * lax.rem(n + way, 2)

    def rows(h):
        return pl.ds(h * cut, cut)

    def y_copy(way, n, h):
        at = first + piece(way, n)
        return remote(phi_ref.at[at, rows(h)], phi_v.at[4 * way + core, at, rows(h)], y_s.at[way, n, h], y_r.at[way, n, h],
                      device(4 - 4 * way + core, plane))

    def z_copy(way, n, h):
        which = piece(way, n)
        where = phi_v.at[4 * way + core, first + which, rows(h)]
        to = lax.rem(plane + 1 - 2 * (which // quarter) + planes, planes)
        return remote(where, where, z_s.at[way, n, h], z_r.at[way, n, h], (grid_pos, to))

    def c_copy(way, m, h):
        at = jnp.where(m < half, first, there) + piece(way, lax.rem(m, half))
        where = phi_v.at[4 * way + core, at, rows(h)]
        return remote(where, where, c_s.at[way, m, h], c_r.at[way, m, h], other)

    def core_copy(no):
        return remote(phi_ref.at[no], phi_v.at[own_slot, no], core_s.at[no], core_r.at[no], other)

    def meta_copy(way, s):
        return remote(meta_v, meta_all_v.at[4 * way + core], m_s.at[1 + 2 * way + s], m_r.at[1 + 2 * way + core],
                      device(4 - 4 * way + s, plane))

    def out_copy(slot, no):
        return pltpu.make_async_copy(phi_v.at[slot, no], all_ref.at[slot, no], out_sem.at[slot, no])

    far_copy = remote(dens_ref.at[core, :, :, pl.ds(pl.multiple_of(core * REACH * BLOCK, BLOCK), COLS)], left_far,
                      f_sem.at[0], f_sem.at[1], device(jnp.where(core == 0, 1, 4), plane))
    core_meta = remote(meta_v, meta_all_v.at[own_slot], m_s.at[0], m_r.at[0], other)

    core_meta.start()
    for way in range(2):
        for s in range(2):
            meta_copy(way, s).start()

    @pl.loop(0, half)
    def _(n):
        for h in range(2):
            for way in range(2):
                y_copy(way, n, h).start()

    far_copy.start()

    @pl.loop(0, batches)
    def _(no):
        core_copy(no).start()

    def masked(block, keep):
        return block * keep.astype(jnp.float32).astype(block.dtype)

    def same(left, right):
        return (1 - jnp.minimum(jnp.abs(left - right), 1)).astype(jnp.float32)

    mask_copy.wait()
    dens_copy.wait()
    for r in range(2):
        row = 2 * grid_pos + r
        for t in range(BAND):
            block = left_v[r, :, :, t * BLOCK:(t + 1) * BLOCK].reshape(rows_all, BLOCK)
            dens_v[r, t, :rows_all, :] = masked(block, mask_s[t, row])
            dens_v[r, t, rows_all:, :] = one_hot(share, BLOCK, (REACH - t) * BLOCK + plane * share)
    far_v[rows_all:, :] = one_hot(share, COLS, core * REACH * BLOCK + plane * share)

    own_copy.wait()
    for no in range(5):
        pltpu.make_async_copy(meta_v, meta_all_v.at[own_slot], m_r.at[no]).wait()
    facts = jnp.zeros((8, BLOCK), jnp.int32)
    for slot in range(SLOTS):
        facts = jnp.where(line == slot, meta_all_v[slot], facts)
    for r in range(2):
        for t in range(BAND):
            facts = jnp.where(jnp.logical_and(line == SLOTS + r, lane == t), mask_s[t, 2 * grid_pos + r], facts)
    facts_v[...] = facts
    to_smem = pltpu.make_async_copy(facts_v, meta_s, own_sem.at[3])
    to_smem.start()
    facts_out = pltpu.make_async_copy(facts_v, facts_ref, own_sem.at[4])
    facts_out.start()
    to_smem.wait()

    def reduced(mixed, keep_picks):
        picked = mixed[rows_all:]
        for h in range(2):
            keep_picks(h, picked[:, h * cut:(h + 1) * cut].astype(jnp.bfloat16))
        sums = jnp.sum(mixed[:rows_all].reshape(PERTS, share, POINTS) * picked[None], axis=1)
        return jnp.concatenate([sums[:, :cut], sums[:, cut:]], axis=0)

    def spread_rows(slot, no, r):
        offset = 2 * grid_pos + r - meta_s[slot, no]
        inside = jnp.clip(offset, 0, WINDOW - 1)
        lhs = jnp.concatenate([dens_v[r, REACH - inside + c] for c in range(WINDOW)], axis=1)
        return lhs, same(offset, inside)

    def rho_part(slot, no, blocks):
        out_copy(slot, no).start()
        lhs, keeps = zip(*[spread_rows(slot, no, r) for r in blocks])
        mixed = lax.dot_general(jnp.concatenate(lhs, axis=0), phi_v[slot, no], NT, preferred_element_type=jnp.float32)
        total = None
        for i, r in enumerate(blocks):
            def keep_picks(h, value, r=r):
                picks_v[slot, no, h, r] = value

            term = reduced(mixed[i * (rows_all + share):(i + 1) * (rows_all + share)], keep_picks) * keeps[i]
            total = term if total is None else total + term
        part[slot, no] = total

    far_start = 4 * chip - 1

    def rho_far(pair):
        phi = phi_v[far_slot, pl.ds(2 * pair, 2)].reshape(2 * POINTS, COLS)
        mixed = lax.dot_general(far_v[...], phi, NT, preferred_element_type=jnp.float32)
        for i in range(2):
            no = 2 * pair + i

            def keep_picks(h, value, no=no):
                far_picks_v[no, h] = value

            term = reduced(mixed[:, i * POINTS:(i + 1) * POINTS], keep_picks)
            part[far_slot, no] = part[far_slot, no] + term * same(meta_s[far_slot, no], far_start)

    def mate_copy(d, no):
        return remote(part.at[2 * d + 1 - core, no], mate.at[d, no], k_s.at[d, no], k_r.at[d, no], other)

    def part_copy(d, no):
        keeper = no // per_plane
        which = lax.rem(no, per_plane)
        return remote(part.at[2 * d + core, no], gathered.at[2 - d, plane, which], a_s.at[d, no], a_r.at[2 - d, plane, which],
                      device(2 * d + core, keeper))

    def combine(d, no):
        slot = 2 * d + core
        pltpu.make_async_copy(part.at[slot, no], mate.at[d, no], k_r.at[d, no]).wait()
        part[slot, no] = part[slot, no] + mate[d, no]
        away = is_other(d, no // per_plane)

        @pl.when(away)
        def _():
            part_copy(d, no).start()

        @pl.when(jnp.logical_not(away))
        def _():
            gathered[1, plane, lax.rem(no, per_plane)] = part[slot, no]

    def pair(n, crossed, late):
        lead = jnp.where(crossed, core, 0)
        at = jnp.where(late, there, first)
        return tuple((4 * way + jnp.where(crossed, 1 - core, core), at + piece(way, n)) for way in (lead, 1 - lead))

    def items_before(m, act):
        odd = lax.rem(m, 2) == 1

        @pl.loop(0, 3)
        def _(item):
            mine = 2 * (m + 1) + item - 1
            slot = jnp.where(mine < half, own_slot, 5 - own_slot)
            at = 2 * lax.rem(mine, half)
            arrived = pair(jnp.maximum(m - 1, 0) // 2, False, False)
            is_own = item > 0
            chosen = tuple((jnp.where(is_own, slot, s), jnp.where(is_own, at + i, no)) for i, (s, no) in enumerate(arrived))

            @pl.when(jnp.logical_or(jnp.logical_and(is_own, m <= 2),
                                    jnp.logical_and(jnp.logical_not(is_own), jnp.logical_and(odd, m <= 2 * half - 1))))
            def _():
                act(chosen, False)

        @pl.when(m >= 2)
        def _():
            act(pair((m - 2 - lax.rem(m, 2)) // 2, True, odd), True)

    def items_after(m, act):
        @pl.when(jnp.logical_and(m >= 2, jnp.logical_and(lax.rem(m, 2) == 0, m <= 2 * half)))
        def _():
            act(pair((m - 2) // 2, False, True), False)

    def compute(batch_pair, crossed):
        rho_part(*batch_pair[0], (0, 1))
        rho_part(*batch_pair[1], (1 - core,) if crossed else (0, 1))
        for slot, no in batch_pair:
            @pl.when(lax.rem(slot, 2) != core)
            def _():
                mate_copy(slot // 2, no).start()

    def combine_pair(m):
        late = jnp.where(lax.rem(m, 2) == 0, 1, 0)
        for slot, no in pair((m - 3 - late) // 2, False, late == 1):
            @pl.when(slot != far_slot)
            def _():
                combine(slot // 2, no)

    @pl.loop(0, 2 * half + 3)
    def _(step):
        m = step - 1

        @pl.when(jnp.logical_and(m >= 0, m < 2 * half))
        def _():
            n, h = m // 2, lax.rem(m, 2)
            for way in range(2):
                y_copy(way, n, h).wait_recv()
                z_copy(way, n, h).start()
                c_copy(way, n, h).start()

        @pl.when(jnp.logical_or(m == 1, m == 2))
        def _():
            for i in range(half):
                core_copy((m - 1) * half + i).wait_recv()

        @pl.when(m >= 2)
        def _():
            late = lax.rem(m, 2)
            for way in range(2):
                for h in range(2):
                    c_copy(way, late * half + (m - 2 - late) // 2, h).wait_recv()

        @pl.when(m == half + 1)
        def _():
            @pl.loop(0, batches)
            def _(no):
                combine(1, no)

            @pl.loop(3, half + 1)
            def _(before):
                combine_pair(before)

        items_before(m, compute)

        @pl.when(jnp.logical_and(m >= 1, m <= 2 * half))
        def _():
            n, h = (m - 1) // 2, lax.rem(m - 1, 2)
            for way in range(2):
                z_copy(way, n, h).wait_recv()
                c_copy(way, half + n, h).start()

        items_after(m, compute)

        @pl.when(m > half)
        def _():
            combine_pair(m)

    combine_pair(2 * half + 2)
    far_copy.wait_recv()
    far_row = jnp.where(core == 0, jnp.maximum(2 * grid_pos - 1, 0), jnp.minimum(2 * grid_pos + 2, 4 * chips - 1))
    for t in range(WINDOW):
        block = left_far[:, :, t * BLOCK:(t + 1) * BLOCK].reshape(rows_all, BLOCK)
        keep = mask_s[jnp.where(core == 0, REACH, 0) + t, far_row]
        far_v[:rows_all, t * BLOCK:(t + 1) * BLOCK] = masked(block, keep)

    @pl.loop(0, half)
    def _(two):
        rho_far(two)
        for i in range(2):
            combine(far_slot // 2, 2 * two + i)

    picks_out = pltpu.make_async_copy(picks_v, picks_ref, own_sem.at[1])
    picks_out.start()
    far_picks_out = pltpu.make_async_copy(far_picks_v, far_picks_ref, own_sem.at[2])
    far_picks_out.start()

    def pot_copy(d, at_plane):
        return remote(pot_v, pot_ref.at[2 * (2 - d) + core, plane], b_s.at[d, at_plane], b_r.at[2 - d, plane],
                      device(2 * d + core, at_plane))

    def cross_copy(d, at_plane):
        where = pot_ref.at[2 * d + core, at_plane]
        return remote(where, where, g_s.at[d, at_plane], g_r.at[d, at_plane], other)

    own_cross = remote(pot_v, pot_ref.at[own_slot, plane], g_s.at[1, plane], g_r.at[1, plane], other)

    def wait_parts(d, at_plane):
        for which in range(per_plane):
            pltpu.make_async_copy(part.at[0, 0], gathered.at[d, at_plane, which], a_r.at[d, at_plane, which]).wait()

    for_others(wait_parts)
    points = lax.broadcasted_iota(jnp.int32, (1, POINTS), 1)
    for no in range(per_plane):
        rho = gathered[0, 0, no]
        for d in range(3):
            for at_plane in range(planes):
                if d or at_plane:
                    rho = rho + gathered[d, at_plane, no]
        mine = per_plane * plane + no
        live = jnp.clip(counts_ref[mine] - points, 0, 1).astype(jnp.float32)
        factor = jnp.broadcast_to(kern_ref[pl.ds(mine, 1), :] * live, (PERTS, POINTS))
        pot_v[no] = rho * jnp.concatenate([factor[:, :cut], factor[:, cut:]], axis=0)
    for_others(lambda d, at_plane: pot_copy(d, at_plane).start())
    own_cross.start()
    pot_own = pltpu.make_async_copy(pot_v, pot_ref.at[own_slot, plane], own_sem.at[0])
    pot_own.start()

    facts_out.wait()
    picks_out.wait()
    far_picks_out.wait()
    far_copy.wait_send()
    core_meta.wait_send()
    for way in range(2):
        for s in range(2):
            meta_copy(way, s).wait_send()

    @pl.loop(0, batches)
    def _(no):
        core_copy(no).wait_send()
        for slot in range(SLOTS):
            out_copy(slot, no).wait()
        for d in range(3):
            mate_copy(d, no).wait_send()

            @pl.when(is_other(d, no // per_plane))
            def _():
                part_copy(d, no).wait_send()

    @pl.loop(0, half)
    def _(n):
        for h in range(2):
            for way in range(2):
                y_copy(way, n, h).wait_send()
                z_copy(way, n, h).wait_send()
                c_copy(way, n, h).wait_send()
                c_copy(way, half + n, h).wait_send()

    def pass_on(d, at_plane):
        pltpu.make_async_copy(pot_v, pot_ref.at[2 * d + core, at_plane], b_r.at[d, at_plane]).wait()
        cross_copy(d, at_plane).start()

    for_others(pass_on, (1, 0, 2))

    @pl.loop(0, 3 * planes)
    def _(no):
        cross_copy(no // planes, lax.rem(no, planes)).wait_recv()

    pot_own.wait()
    own_cross.wait_send()
    for_others(lambda d, at_plane: cross_copy(d, at_plane).wait_send())
    for_others(lambda d, at_plane: pot_copy(d, at_plane).wait_send())


def potentials(phi, density, starts, counts, pair_mask, kern, chips, planes):
    batches, points, cols = phi.shape
    share = density.shape[2]
    half, per_plane = batches // 2, batches // planes
    rows = PERTS * share + share
    far = pl.BlockSpec(memory_space=pl.ANY)
    smem = pl.BlockSpec(memory_space=pltpu.SMEM)
    vmem = pl.BlockSpec(memory_space=pltpu.VMEM)
    dma = pltpu.SemaphoreType.DMA
    f32 = jnp.float32
    row_pair = (2 * PERTS, points // 2)
    meta = (8, BLOCK)
    picks, far_picks = (SLOTS, batches, 2, 2, share, points // 2), (batches, 2, share, points // 2)
    return pl.pallas_call(
        functools.partial(density_kernel, chips, planes, batches, share),
        out_shape=(
            jax.ShapeDtypeStruct((SLOTS, batches, points, cols), phi.dtype),
            jax.ShapeDtypeStruct(meta, starts.dtype),
            jax.ShapeDtypeStruct((SLOTS, planes, per_plane) + row_pair, f32),
            jax.ShapeDtypeStruct(picks, phi.dtype),
            jax.ShapeDtypeStruct(far_picks, phi.dtype),
        ),
        in_specs=[far, far, smem, smem, far, vmem],
        out_specs=[far] * 5,
        scratch_shapes=[
            pltpu.VMEM((SLOTS, batches, points, cols), phi.dtype),
            pltpu.VMEM((2, BAND, rows, BLOCK), density.dtype),
            pltpu.VMEM((rows, COLS), density.dtype),
            pltpu.VMEM(density.shape, density.dtype),
            pltpu.VMEM((PERTS, share, COLS), density.dtype),
            pltpu.VMEM(meta, starts.dtype),
            pltpu.VMEM((SLOTS,) + meta, starts.dtype),
            pltpu.VMEM(meta, starts.dtype),
            pltpu.SMEM(meta, starts.dtype),
            pltpu.SMEM(pair_mask.shape, pair_mask.dtype),
            pltpu.VMEM(picks, phi.dtype),
            pltpu.VMEM(far_picks, phi.dtype),
            pltpu.VMEM((SLOTS, batches) + row_pair, f32),
            pltpu.VMEM((3, batches) + row_pair, f32),
            pltpu.VMEM((3, planes, per_plane) + row_pair, f32),
            pltpu.VMEM((per_plane,) + row_pair, f32),
            dma((5,)), dma((SLOTS, batches)), dma((batches,)), dma((batches,)),
            dma((2, half, 2)), dma((2, half, 2)), dma((2, half, 2)), dma((2, half, 2)),
            dma((2, batches, 2)), dma((2, batches, 2)), dma((5,)), dma((5,)), dma((2,)),
            dma((3, batches)), dma((3, batches)), dma((3, batches)), dma((3, planes, per_plane)),
            dma((3, planes)), dma((3, planes)), dma((3, planes)), dma((3, planes)),
        ],
        compiler_params=pltpu.CompilerParams(collective_id=0, has_side_effects=True, vmem_limit_bytes=56 << 20),
        cost_estimate=pl.CostEstimate(flops=17 * 10**9, bytes_accessed=50 * 10**6, transcendentals=0),
        name="potentials",
    )(phi, density, starts, counts, pair_mask, kern)


def joined(halves):
    return jnp.concatenate([halves[:PERTS], halves[PERTS:]], axis=1)


def split_weights(pot, picked, scale):
    weighted = (pot[:, None, :] * picked[None]).reshape(pot.shape[0] * picked.shape[0], picked.shape[1])
    high = weighted.astype(jnp.bfloat16)
    low = ((weighted - high.astype(jnp.float32)) * scale).astype(EIGHT)
    return high, low


CUT = POINTS // 2
LARGEST = 8
EIGHT = jnp.float8_e4m3fn
ROOM = 448.0 / (6.0 * 2.0**-8)


class Chunks:
    def __init__(self, batches, facts_ref, pot, pick, phi_ref, listed, counted, buf, sems, scale):
        self.batches, self.facts, self.pot, self.pick, self.phi = batches, facts_ref, pot, pick, phi_ref
        self.listed, self.counted, self.buf, self.sems, self.scale = listed, counted, buf, sems, scale

    def set_scale(self, pots):
        most = jnp.maximum(jnp.max(jnp.abs(pots)), 1e-30)
        self.scale[0] = ROOM / most
        self.scale[1] = most * (1.0 / ROOM)

    def start(self, no):
        return self.facts[no // self.batches, lax.rem(no, self.batches)]

    def note(self, which, no, wanted):
        most = self.pot.shape[0] * 2
        many = self.facts[no // self.batches, self.batches + lax.rem(no, self.batches)] > CUT

        @pl.when(wanted)
        def _():
            have = self.counted[which]
            self.listed[which * most + have] = 2 * no
            self.listed[which * most + have + 1] = 2 * no + 1
            self.counted[which] = have + 1 + many.astype(jnp.int32)

    def copy(self, chunk):
        no, h = chunk // 2, lax.rem(chunk, 2)
        return pltpu.make_async_copy(
            self.phi.at[no // self.batches, lax.rem(no, self.batches), pl.ds(pl.multiple_of(h * CUT, CUT), CUT)],
            self.buf.at[chunk], self.sems.at[chunk])

    def fetch(self, which):
        @pl.loop(0, self.counted[which])
        def _(i):
            self.copy(self.listed[which * self.pot.shape[0] * 2 + i]).start()

    def group(self, which, at, size, rows):
        rights, highs, lows = [], [[] for _ in rows], [[] for _ in rows]
        scale = self.scale[0]
        for i in range(size):
            chunk = self.listed[which * self.pot.shape[0] * 2 + at + i]
            self.copy(chunk).wait()
            pots = self.pot[chunk // 2]
            pot = jnp.where(lax.rem(chunk, 2) == 0, pots[:PERTS], pots[PERTS:])
            rights.append(self.buf[chunk])
            for no, (row, _) in enumerate(rows):
                high, low = split_weights(pot, self.pick(chunk, row).astype(jnp.float32), scale)
                highs[no].append(high)
                lows[no].append(low)
        right = jnp.concatenate(rights, axis=0)
        left = jnp.concatenate([jnp.concatenate(high, axis=1) for high in highs], axis=0)
        total = jnp.dot(left, right, preferred_element_type=jnp.float32)
        low = jnp.concatenate([jnp.concatenate(low, axis=1) for low in lows], axis=0)
        rest = jnp.dot(low, right.astype(EIGHT), preferred_element_type=jnp.float32)
        total = total + rest * self.scale[1]
        depth = left.shape[0] // len(rows)
        for no, (_, spot) in enumerate(rows):
            spot[...] = spot[...] + total[no * depth:(no + 1) * depth].reshape(spot.shape)

    def add(self, which, rows):
        count = self.counted[which]
        size = LARGEST
        done = 0
        while size:
            times = (count - done) // size

            @pl.loop(0, times)
            def _(i, size=size, done=done):
                self.group(which, done + i * size, size, rows)

            done = done + times * size
            size //= 2


def fock_kernel(batches, share, facts_ref, pot_ref, picks_ref, phi_ref, out_ref,
                total, pot_v, picks_v, listed, counted, buf, sems, scale, in_sem, out_sem):
    grid_pos = lax.axis_index("grid")
    pot_copy = pltpu.make_async_copy(pot_ref, pot_v, in_sem.at[0])
    pot_copy.start()
    picks_copy = pltpu.make_async_copy(picks_ref, picks_v, in_sem.at[1])
    picks_copy.start()
    chunks = Chunks(batches, facts_ref, pot_v, lambda chunk, row: picks_v[chunk, row], phi_ref, listed, counted, buf, sems,
                    scale)
    base = 2 * grid_pos - REACH
    leads = REACH + 2

    for lead in range(leads):
        counted[lead] = 0

    @pl.loop(0, SLOTS * batches)
    def _(no):
        lead = chunks.start(no) - base
        chunks.note(lead, no, jnp.logical_and(lead >= 0, lead < leads))

    chunks.fetch(0)
    chunks.fetch(1)
    total[...] = jnp.zeros_like(total)
    pot_copy.wait()
    chunks.set_scale(pot_v[...])
    picks_copy.wait()

    def spot(r, offset):
        return total.at[r, :, :, pl.ds(pl.multiple_of((REACH - offset) * BLOCK, BLOCK), COLS)]

    def out_copy(r, t):
        cols = pl.ds(pl.multiple_of(t * BLOCK, BLOCK), BLOCK)
        return pltpu.make_async_copy(total.at[r, :, :, cols], out_ref.at[r, :, :, cols], out_sem.at[r, t])

    def leave(r, t):
        @pl.when(facts_ref[SLOTS + r, t] == 0)
        def _():
            cols = pl.ds(pl.multiple_of(t * BLOCK, BLOCK), BLOCK)
            total[r, :, :, cols] = jnp.zeros((PERTS, share, BLOCK), jnp.float32)

        out_copy(r, t).start()

    @pl.loop(0, leads)
    def _(lead):
        @pl.when(lead + 2 < leads)
        def _():
            chunks.fetch(lead + 2)

        both = jnp.logical_and(lead >= 1, lead <= REACH)

        @pl.when(both)
        def _():
            offset = REACH - lead
            chunks.add(lead, [(0, spot(0, offset)), (1, spot(1, offset + 1))])

        @pl.when(jnp.logical_not(both))
        def _():
            r = jnp.where(lead == 0, 0, 1)
            offset = jnp.where(lead == 0, REACH, 0)
            chunks.add(lead, [(r, spot(r, offset))])

        @pl.loop(lead, jnp.where(lead == REACH, BAND, jnp.minimum(lead + 1, REACH + 1)))
        def _(t):
            leave(0, t)

        @pl.loop(jnp.maximum(lead - 1, 0), jnp.where(lead == REACH + 1, BAND, lead))
        def _(t):
            leave(1, t)

    @pl.loop(0, BAND)
    def _(t):
        for r in range(2):
            out_copy(r, t).wait()


def chunk_scratch(slots, batches, cols, lists, dtype):
    most = 2 * slots * batches
    return [
        pltpu.SMEM((lists * most,), jnp.int32),
        pltpu.SMEM((lists,), jnp.int32),
        pltpu.VMEM((most, CUT, cols), dtype),
        pltpu.SemaphoreType.DMA((most,)),
        pltpu.SMEM((2,), jnp.float32),
    ]


def fock_own(facts, pot, picks, phi_all, share):
    slots, batches, points, cols = phi_all.shape
    far = pl.BlockSpec(memory_space=pl.ANY)
    whole = (2, PERTS, share, WIDE)
    dma = pltpu.SemaphoreType.DMA
    return pl.pallas_call(
        functools.partial(fock_kernel, batches, share),
        out_shape=jax.ShapeDtypeStruct(whole, jnp.float32),
        in_specs=[pl.BlockSpec(memory_space=pltpu.SMEM), far, far, far],
        out_specs=far,
        scratch_shapes=[
            pltpu.VMEM(whole, jnp.float32), pltpu.VMEM(pot.shape, pot.dtype), pltpu.VMEM(picks.shape, picks.dtype),
        ]
        + chunk_scratch(slots, batches, cols, REACH + 2, phi_all.dtype)
        + [dma((2,)), dma((2, BAND))],
        compiler_params=pltpu.CompilerParams(vmem_limit_bytes=56 << 20),
        cost_estimate=pl.CostEstimate(flops=20 * 10**9, bytes_accessed=20 * 10**6, transcendentals=0),
        name="fock_own",
    )(facts, pot, picks, phi_all)


def far_kernel(batches, facts_ref, pot_ref, picks_ref, phi_ref, out_ref, pot_v, picks_v, listed, counted, buf, sems, scale, in_sem):
    grid_pos = lax.axis_index("grid")
    core = lax.rem(grid_pos, 2)
    slot = jnp.where(core == 0, 4, 1)
    far_start = 4 * (grid_pos // 2) - 1
    own = pl.ds(slot * batches, batches)
    pot_copy = pltpu.make_async_copy(pot_ref.at[own], pot_v.at[own], in_sem.at[0])
    pot_copy.start()
    picks_copy = pltpu.make_async_copy(picks_ref, picks_v, in_sem.at[1])
    picks_copy.start()
    chunks = Chunks(batches, facts_ref, pot_v, lambda chunk, row: picks_v[chunk - 2 * batches * slot], phi_ref,
                    listed, counted, buf, sems, scale)
    counted[0] = 0

    @pl.loop(0, batches)
    def _(no):
        chunks.note(0, slot * batches + no, chunks.start(slot * batches + no) == far_start)

    chunks.fetch(0)
    out_ref[...] = jnp.zeros_like(out_ref)
    pot_copy.wait()
    chunks.set_scale(pot_v[own])
    picks_copy.wait()
    chunks.add(0, [(0, out_ref)])


def fock_far(facts, pot, far_picks, phi_all, share):
    slots, batches, points, cols = phi_all.shape
    smem = pl.BlockSpec(memory_space=pltpu.SMEM)
    far = pl.BlockSpec(memory_space=pl.ANY)
    vmem = pl.BlockSpec(memory_space=pltpu.VMEM)
    return pl.pallas_call(
        functools.partial(far_kernel, batches),
        out_shape=jax.ShapeDtypeStruct((PERTS, share, COLS), jnp.float32),
        in_specs=[smem, far, far, far],
        out_specs=vmem,
        scratch_shapes=[pltpu.VMEM(pot.shape, pot.dtype), pltpu.VMEM(far_picks.shape, far_picks.dtype)]
        + chunk_scratch(slots, batches, cols, 1, phi_all.dtype)
        + [pltpu.SemaphoreType.DMA((2,))],
        compiler_params=pltpu.CompilerParams(vmem_limit_bytes=56 << 20),
        cost_estimate=pl.CostEstimate(flops=10**9, bytes_accessed=2 * 10**6, transcendentals=0),
        name="fock_far",
    )(facts, pot, far_picks, phi_all)


def shards(density, basis_vals, kernel, starts, counts, pair_mask):
    grid_size, planes = lax.axis_size("grid"), lax.axis_size("basis")
    batches, share = basis_vals.shape[0], density.shape[2]
    grid_pos = lax.axis_index("grid")
    core = lax.rem(grid_pos, 2)
    phi_all, facts, pot, picks, far_picks = potentials(
        basis_vals, density, starts, counts, pair_mask.T, kernel, grid_size // 2, planes)
    pot = pot.reshape(SLOTS * batches, 2 * PERTS, POINTS // 2)
    picks = picks.reshape(2 * SLOTS * batches, 2, share, POINTS // 2)
    far_picks = far_picks.reshape(2 * batches, share, POINTS // 2)
    far = fock_far(facts, pot, far_picks, phi_all, share)
    route = [(i, (i + 1) % grid_size if i % 2 else (i - 1) % grid_size) for i in range(grid_size)]
    arrived = lax.ppermute(far, "grid", route)
    own = fock_own(facts, pot, picks, phi_all, share)
    mask_row = lax.dynamic_slice(pair_mask, (2 * grid_pos + core, core * REACH), (1, WINDOW))[0]
    keep = jnp.repeat(mask_row, BLOCK).astype(jnp.float32)
    place = (core, 0, 0, core * REACH * BLOCK)
    present = lax.dynamic_slice(own, place, (1, PERTS, share, COLS))
    return lax.dynamic_update_slice(own, present + (arrived * keep)[None], place)


def solution(mesh):
    placed = (
        P("grid", None, "basis", None),
        P("grid", None, None),
        P("grid", None),
        P("grid"),
        P("grid"),
        P(),
    )
    return jax.shard_map(
        shards,
        mesh=mesh,
        in_specs=placed,
        out_specs=P("grid", None, "basis", None),
        check_vma=False,
    )
```

```python
import functools

import jax
import jax.numpy as jnp
from jax import lax
from jax.experimental import pallas as pl
from jax.experimental.pallas import tpu as pltpu
from jax.sharding import PartitionSpec as P

BLOCK = 128
PERTS = 12
WINDOW = 6
POINTS = 256
REACH = 5
BAND = 11
COLS = WINDOW * BLOCK
WIDE = BAND * BLOCK
SLOTS = 6
MESH = pl.DeviceIdType.MESH
NT = (((1,), (1,)), ((), ()))


def one_hot(share, columns, first):
    rows = lax.broadcasted_iota(jnp.int32, (share, columns), 0)
    lanes = lax.broadcasted_iota(jnp.int32, (share, columns), 1)
    return jnp.where(lanes == rows + first, 1.0, 0.0).astype(jnp.bfloat16)


def density_kernel(
    chips, planes, batches, share,
    phi_ref, dens_ref, starts_ref, counts_ref, mask_ref, kern_ref,
    all_ref, facts_ref, pot_ref, picks_ref, far_picks_ref,
    phi_v, dens_v, far_v, left_v, left_far, meta_v, meta_all_v, facts_v, meta_s, mask_s, picks_v, far_picks_v, part, mate, gathered, pot_v,
    own_sem, out_sem, core_s, core_r, y_s, y_r, z_s, z_r, c_s, c_r, m_s, m_r, f_sem, k_s, k_r, a_s, a_r, b_s, b_r, g_s, g_r,
):
    grid_pos, plane = lax.axis_index("grid"), lax.axis_index("basis")
    chip, core = grid_pos // 2, lax.rem(grid_pos, 2)
    half = batches // 2
    quarter = half // 2
    per_plane = batches // planes
    own_slot = 2 + core
    far_slot = jnp.where(core == 0, 4, 1)
    first = lax.rem(plane, 2) * half
    there = half - first
    rows_all = PERTS * share
    cut = POINTS // 2
    has_down, has_up = chip > 0, chip < chips - 1
    sends, comes = (has_up, has_down), (has_down, has_up)
    far_exists = jnp.where(core == 0, chip, chips - 1 - chip) > 0

    def exists(d):
        return jnp.where(d == 0, chip, jnp.where(d == 2, chips - 1 - chip, 1)) > 0

    def device(slot, at_plane):
        return (2 * lax.rem(chip + slot // 2 - 1 + chips, chips) + lax.rem(slot, 2), at_plane)

    other = (2 * chip + 1 - core, plane)

    def remote(src, dst, send, recv, to):
        return pltpu.make_async_remote_copy(
            src_ref=src, dst_ref=dst, send_sem=send, recv_sem=recv, device_id=to, device_id_type=MESH)

    def is_other(d, at_plane):
        return jnp.logical_or(d != 1, at_plane != plane)

    def for_others(act, order=(0, 2, 1)):
        @pl.loop(0, 3 * planes)
        def _(no):
            turn, at_plane = no // planes, lax.rem(no, planes)
            d = jnp.where(turn == 0, order[0], jnp.where(turn == 1, order[1], order[2]))

            @pl.when(jnp.logical_and(is_other(d, at_plane), exists(d)))
            def _():
                act(d, at_plane)

    own_copy = pltpu.make_async_copy(phi_ref, phi_v.at[own_slot], own_sem.at[0])
    own_copy.start()
    dens_copy = pltpu.make_async_copy(dens_ref, left_v, own_sem.at[1])
    dens_copy.start()
    mask_copy = pltpu.make_async_copy(mask_ref, mask_s, own_sem.at[2])
    mask_copy.start()

    line = lax.broadcasted_iota(jnp.int32, (8, BLOCK), 0)
    lane = lax.broadcasted_iota(jnp.int32, (8, BLOCK), 1)
    meta = jnp.zeros((8, BLOCK), jnp.int32)
    for no in range(batches):
        meta = jnp.where(lane == no, starts_ref[no], meta)
        meta = jnp.where(lane == batches + no, counts_ref[no], meta)
    meta_v[...] = meta
    meta_all_v[own_slot] = meta

    barrier = pltpu.get_barrier_semaphore()
    for there_is, slots in ((has_down, (0, 1)), (has_up, (4, 5))):
        @pl.when(there_is)
        def _(slots=slots):
            for slot in slots:
                pl.semaphore_signal(barrier, inc=1, device_id=device(slot, plane), device_id_type=MESH)

    for partner in (other, (grid_pos, lax.rem(plane + 1, planes)), (grid_pos, lax.rem(plane + planes - 1, planes))):
        pl.semaphore_signal(barrier, inc=1, device_id=partner, device_id_type=MESH)
    pl.semaphore_wait(barrier, 3 + 2 * has_down.astype(jnp.int32) + 2 * has_up.astype(jnp.int32))

    def piece(way, n):
        return n // 2 + quarter * lax.rem(n + way, 2)

    def rows(h):
        return pl.ds(h * cut, cut)

    def y_copy(way, n, h):
        at = first + piece(way, n)
        return remote(phi_ref.at[at, rows(h)], phi_v.at[4 * way + core, at, rows(h)], y_s.at[way, n, h], y_r.at[way, n, h],
                      device(4 - 4 * way + core, plane))

    def z_copy(way, n, h):
        which = piece(way, n)
        where = phi_v.at[4 * way + core, first + which, rows(h)]
        to = lax.rem(plane + 1 - 2 * (which // quarter) + planes, planes)
        return remote(where, where, z_s.at[way, n, h], z_r.at[way, n, h], (grid_pos, to))

    def c_copy(way, m, h):
        at = jnp.where(m < half, first, there) + piece(way, lax.rem(m, half))
        where = phi_v.at[4 * way + core, at, rows(h)]
        return remote(where, where, c_s.at[way, m, h], c_r.at[way, m, h], other)

    def core_copy(no):
        return remote(phi_ref.at[no], phi_v.at[own_slot, no], core_s.at[no], core_r.at[no], other)

    def meta_copy(way, s):
        return remote(meta_v, meta_all_v.at[4 * way + core], m_s.at[1 + 2 * way + s], m_r.at[1 + 2 * way + core],
                      device(4 - 4 * way + s, plane))

    def out_copy(slot, no):
        return pltpu.make_async_copy(phi_v.at[slot, no], all_ref.at[slot, no], out_sem.at[slot, no])

    far_copy = remote(dens_ref.at[core, :, :, pl.ds(pl.multiple_of(core * REACH * BLOCK, BLOCK), COLS)], left_far,
                      f_sem.at[0], f_sem.at[1], device(jnp.where(core == 0, 1, 4), plane))
    core_meta = remote(meta_v, meta_all_v.at[own_slot], m_s.at[0], m_r.at[0], other)

    core_meta.start()
    for way in range(2):
        @pl.when(sends[way])
        def _(way=way):
            for s in range(2):
                meta_copy(way, s).start()

        @pl.when(jnp.logical_not(comes[way]))
        def _(way=way):
            for s in range(2):
                meta_all_v[4 * way + s] = jnp.full((8, BLOCK), -1000, jnp.int32)

    @pl.loop(0, half)
    def _(n):
        for h in range(2):
            for way in range(2):
                @pl.when(sends[way])
                def _(way=way, h=h):
                    y_copy(way, n, h).start()

    @pl.when(far_exists)
    def _():
        far_copy.start()

    @pl.loop(0, batches)
    def _(no):
        core_copy(no).start()

    def masked(block, keep):
        return block * keep.astype(jnp.float32).astype(block.dtype)

    def same(left, right):
        return (1 - jnp.minimum(jnp.abs(left - right), 1)).astype(jnp.float32)

    mask_copy.wait()
    dens_copy.wait()
    for r in range(2):
        row = 2 * grid_pos + r
        for t in range(BAND):
            block = left_v[r, :, :, t * BLOCK:(t + 1) * BLOCK].reshape(rows_all, BLOCK)
            dens_v[r, t, :rows_all, :] = masked(block, mask_s[t, row])
            dens_v[r, t, rows_all:, :] = one_hot(share, BLOCK, (REACH - t) * BLOCK + plane * share)
    far_v[rows_all:, :] = one_hot(share, COLS, core * REACH * BLOCK + plane * share)

    own_copy.wait()
    pltpu.make_async_copy(meta_v, meta_all_v.at[own_slot], m_r.at[0]).wait()
    for way in range(2):
        @pl.when(comes[way])
        def _(way=way):
            for s in range(2):
                pltpu.make_async_copy(meta_v, meta_all_v.at[own_slot], m_r.at[1 + 2 * way + s]).wait()

    facts = jnp.zeros((8, BLOCK), jnp.int32)
    for slot in range(SLOTS):
        facts = jnp.where(line == slot, meta_all_v[slot], facts)
    for r in range(2):
        for t in range(BAND):
            facts = jnp.where(jnp.logical_and(line == SLOTS + r, lane == t), mask_s[t, 2 * grid_pos + r], facts)
    facts_v[...] = facts
    to_smem = pltpu.make_async_copy(facts_v, meta_s, own_sem.at[3])
    to_smem.start()
    facts_out = pltpu.make_async_copy(facts_v, facts_ref, own_sem.at[4])
    facts_out.start()
    to_smem.wait()

    def reduced(mixed, keep_picks):
        picked = mixed[rows_all:]
        for h in range(2):
            keep_picks(h, picked[:, h * cut:(h + 1) * cut].astype(jnp.bfloat16))
        sums = jnp.sum(mixed[:rows_all].reshape(PERTS, share, POINTS) * picked[None], axis=1)
        return jnp.concatenate([sums[:, :cut], sums[:, cut:]], axis=0)

    def spread_rows(slot, no, r):
        offset = 2 * grid_pos + r - meta_s[slot, no]
        inside = jnp.clip(offset, 0, WINDOW - 1)
        lhs = jnp.concatenate([dens_v[r, REACH - inside + c] for c in range(WINDOW)], axis=1)
        return lhs, same(offset, inside)

    def rho_part(slot, no, blocks):
        out_copy(slot, no).start()
        lhs, keeps = zip(*[spread_rows(slot, no, r) for r in blocks])
        mixed = lax.dot_general(jnp.concatenate(lhs, axis=0), phi_v[slot, no], NT, preferred_element_type=jnp.float32)
        total = None
        for i, r in enumerate(blocks):
            def keep_picks(h, value, r=r):
                picks_v[slot, no, h, r] = value

            term = reduced(mixed[i * (rows_all + share):(i + 1) * (rows_all + share)], keep_picks) * keeps[i]
            total = term if total is None else total + term
        part[slot, no] = total

    far_start = 4 * chip - 1

    def rho_far(pair):
        phi = phi_v[far_slot, pl.ds(2 * pair, 2)].reshape(2 * POINTS, COLS)
        mixed = lax.dot_general(far_v[...], phi, NT, preferred_element_type=jnp.float32)
        for i in range(2):
            no = 2 * pair + i

            def keep_picks(h, value, no=no):
                far_picks_v[no, h] = value

            term = reduced(mixed[:, i * POINTS:(i + 1) * POINTS], keep_picks)
            part[far_slot, no] = part[far_slot, no] + term * same(meta_s[far_slot, no], far_start)

    def mate_copy(d, no):
        return remote(part.at[2 * d + 1 - core, no], mate.at[d, no], k_s.at[d, no], k_r.at[d, no], other)

    def part_copy(d, no):
        keeper = no // per_plane
        which = lax.rem(no, per_plane)
        return remote(part.at[2 * d + core, no], gathered.at[2 - d, plane, which], a_s.at[d, no], a_r.at[2 - d, plane, which],
                      device(2 * d + core, keeper))

    def combine(d, no):
        slot = 2 * d + core
        pltpu.make_async_copy(part.at[slot, no], mate.at[d, no], k_r.at[d, no]).wait()
        part[slot, no] = part[slot, no] + mate[d, no]
        away = is_other(d, no // per_plane)

        @pl.when(away)
        def _():
            part_copy(d, no).start()

        @pl.when(jnp.logical_not(away))
        def _():
            gathered[1, plane, lax.rem(no, per_plane)] = part[slot, no]

    def pair(n, crossed, late):
        lead = jnp.where(crossed, core, 0)
        at = jnp.where(late, there, first)
        return tuple((4 * way + jnp.where(crossed, 1 - core, core), at + piece(way, n)) for way in (lead, 1 - lead))

    def items_before(m, act):
        odd = lax.rem(m, 2) == 1

        @pl.loop(0, 3)
        def _(item):
            mine = 2 * (m + 1) + item - 1
            slot = jnp.where(mine < half, own_slot, 5 - own_slot)
            at = 2 * lax.rem(mine, half)
            arrived = pair(jnp.maximum(m - 1, 0) // 2, False, False)
            is_own = item > 0
            chosen = tuple((jnp.where(is_own, slot, s), jnp.where(is_own, at + i, no)) for i, (s, no) in enumerate(arrived))

            @pl.when(jnp.logical_or(jnp.logical_and(is_own, m <= 2),
                                    jnp.logical_and(jnp.logical_not(is_own), jnp.logical_and(odd, m <= 2 * half - 1))))
            def _():
                act(chosen, False)

        @pl.when(m >= 2)
        def _():
            act(pair((m - 2 - lax.rem(m, 2)) // 2, True, odd), True)

    def items_after(m, act):
        @pl.when(jnp.logical_and(m >= 2, jnp.logical_and(lax.rem(m, 2) == 0, m <= 2 * half)))
        def _():
            act(pair((m - 2) // 2, False, True), False)

    def compute(batch_pair, crossed):
        rho_part(*batch_pair[0], (0, 1))
        rho_part(*batch_pair[1], (1 - core,) if crossed else (0, 1))
        for slot, no in batch_pair:
            @pl.when(jnp.logical_and(lax.rem(slot, 2) != core, exists(slot // 2)))
            def _():
                mate_copy(slot // 2, no).start()

    def combine_pair(m):
        late = jnp.where(lax.rem(m, 2) == 0, 1, 0)
        for slot, no in pair((m - 3 - late) // 2, False, late == 1):
            @pl.when(jnp.logical_and(slot != far_slot, exists(slot // 2)))
            def _():
                combine(slot // 2, no)

    @pl.loop(0, 2 * half + 3)
    def _(step):
        m = step - 1

        @pl.when(jnp.logical_and(m >= 0, m < 2 * half))
        def _():
            n, h = m // 2, lax.rem(m, 2)
            for way in range(2):
                @pl.when(comes[way])
                def _(way=way):
                    y_copy(way, n, h).wait_recv()
                    z_copy(way, n, h).start()
                    c_copy(way, n, h).start()

        @pl.when(jnp.logical_or(m == 1, m == 2))
        def _():
            for i in range(half):
                core_copy((m - 1) * half + i).wait_recv()

        @pl.when(m >= 2)
        def _():
            late = lax.rem(m, 2)
            for way in range(2):
                @pl.when(comes[way])
                def _(way=way):
                    for h in range(2):
                        c_copy(way, late * half + (m - 2 - late) // 2, h).wait_recv()

        @pl.when(m == half + 1)
        def _():
            @pl.loop(0, batches)
            def _(no):
                combine(1, no)

            @pl.loop(3, half + 1)
            def _(before):
                combine_pair(before)

        items_before(m, compute)

        @pl.when(jnp.logical_and(m >= 1, m <= 2 * half))
        def _():
            n, h = (m - 1) // 2, lax.rem(m - 1, 2)
            for way in range(2):
                @pl.when(comes[way])
                def _(way=way):
                    z_copy(way, n, h).wait_recv()
                    c_copy(way, half + n, h).start()

        items_after(m, compute)

        @pl.when(m > half)
        def _():
            combine_pair(m)

    combine_pair(2 * half + 2)
    @pl.when(far_exists)
    def _():
        far_copy.wait_recv()
        far_row = jnp.where(core == 0, jnp.maximum(2 * grid_pos - 1, 0), jnp.minimum(2 * grid_pos + 2, 4 * chips - 1))
        for t in range(WINDOW):
            block = left_far[:, :, t * BLOCK:(t + 1) * BLOCK].reshape(rows_all, BLOCK)
            keep = mask_s[jnp.where(core == 0, REACH, 0) + t, far_row]
            far_v[:rows_all, t * BLOCK:(t + 1) * BLOCK] = masked(block, keep)

    @pl.loop(0, half)
    def _(two):
        @pl.when(far_exists)
        def _():
            rho_far(two)

        @pl.when(exists(far_slot // 2))
        def _():
            for i in range(2):
                combine(far_slot // 2, 2 * two + i)

    picks_out = pltpu.make_async_copy(picks_v, picks_ref, own_sem.at[1])
    picks_out.start()
    far_picks_out = pltpu.make_async_copy(far_picks_v, far_picks_ref, own_sem.at[2])
    far_picks_out.start()

    def pot_copy(d, at_plane):
        return remote(pot_v, pot_ref.at[2 * (2 - d) + core, plane], b_s.at[d, at_plane], b_r.at[2 - d, plane],
                      device(2 * d + core, at_plane))

    def cross_copy(d, at_plane):
        where = pot_ref.at[2 * d + core, at_plane]
        return remote(where, where, g_s.at[d, at_plane], g_r.at[d, at_plane], other)

    own_cross = remote(pot_v, pot_ref.at[own_slot, plane], g_s.at[1, plane], g_r.at[1, plane], other)

    def wait_parts(d, at_plane):
        for which in range(per_plane):
            pltpu.make_async_copy(part.at[0, 0], gathered.at[d, at_plane, which], a_r.at[d, at_plane, which]).wait()

    def no_pot_copy(way, s):
        return pltpu.make_async_copy(gathered.at[2 * way], pot_ref.at[4 * way + s], own_sem.at[5 + 2 * way + s])

    for way in range(2):
        @pl.when(jnp.logical_not(comes[way]))
        def _(way=way):
            gathered[2 * way] = jnp.zeros((planes, per_plane, 2 * PERTS, cut), jnp.float32)
            for s in range(2):
                no_pot_copy(way, s).start()

    for_others(wait_parts)
    points = lax.broadcasted_iota(jnp.int32, (1, POINTS), 1)
    for no in range(per_plane):
        rho = gathered[0, 0, no]
        for d in range(3):
            for at_plane in range(planes):
                if d or at_plane:
                    rho = rho + gathered[d, at_plane, no]
        mine = per_plane * plane + no
        live = jnp.clip(counts_ref[mine] - points, 0, 1).astype(jnp.float32)
        factor = jnp.broadcast_to(kern_ref[pl.ds(mine, 1), :] * live, (PERTS, POINTS))
        pot_v[no] = rho * jnp.concatenate([factor[:, :cut], factor[:, cut:]], axis=0)
    for_others(lambda d, at_plane: pot_copy(d, at_plane).start())
    own_cross.start()
    pot_own = pltpu.make_async_copy(pot_v, pot_ref.at[own_slot, plane], own_sem.at[0])
    pot_own.start()

    facts_out.wait()
    picks_out.wait()
    far_picks_out.wait()

    @pl.when(far_exists)
    def _():
        far_copy.wait_send()

    core_meta.wait_send()
    for way in range(2):
        @pl.when(sends[way])
        def _(way=way):
            for s in range(2):
                meta_copy(way, s).wait_send()

        @pl.when(jnp.logical_not(comes[way]))
        def _(way=way):
            for s in range(2):
                no_pot_copy(way, s).wait()

    @pl.loop(0, batches)
    def _(no):
        core_copy(no).wait_send()
        for slot in range(SLOTS):
            out_copy(slot, no).wait()
        for d in range(3):
            @pl.when(exists(d))
            def _(d=d):
                mate_copy(d, no).wait_send()

            @pl.when(jnp.logical_and(is_other(d, no // per_plane), exists(d)))
            def _(d=d):
                part_copy(d, no).wait_send()

    @pl.loop(0, half)
    def _(n):
        for h in range(2):
            for way in range(2):
                @pl.when(sends[way])
                def _(way=way, h=h):
                    y_copy(way, n, h).wait_send()

                @pl.when(comes[way])
                def _(way=way, h=h):
                    z_copy(way, n, h).wait_send()
                    c_copy(way, n, h).wait_send()
                    c_copy(way, half + n, h).wait_send()

    def pass_on(d, at_plane):
        pltpu.make_async_copy(pot_v, pot_ref.at[2 * d + core, at_plane], b_r.at[d, at_plane]).wait()
        cross_copy(d, at_plane).start()

    for_others(pass_on, (1, 0, 2))

    @pl.loop(0, 3 * planes)
    def _(no):
        @pl.when(exists(no // planes))
        def _():
            cross_copy(no // planes, lax.rem(no, planes)).wait_recv()

    pot_own.wait()
    own_cross.wait_send()
    for_others(lambda d, at_plane: cross_copy(d, at_plane).wait_send())
    for_others(lambda d, at_plane: pot_copy(d, at_plane).wait_send())


def potentials(phi, density, starts, counts, pair_mask, kern, chips, planes):
    batches, points, cols = phi.shape
    share = density.shape[2]
    half, per_plane = batches // 2, batches // planes
    rows = PERTS * share + share
    far = pl.BlockSpec(memory_space=pl.ANY)
    smem = pl.BlockSpec(memory_space=pltpu.SMEM)
    vmem = pl.BlockSpec(memory_space=pltpu.VMEM)
    dma = pltpu.SemaphoreType.DMA
    f32 = jnp.float32
    row_pair = (2 * PERTS, points // 2)
    meta = (8, BLOCK)
    picks, far_picks = (SLOTS, batches, 2, 2, share, points // 2), (batches, 2, share, points // 2)
    return pl.pallas_call(
        functools.partial(density_kernel, chips, planes, batches, share),
        out_shape=(
            jax.ShapeDtypeStruct((SLOTS, batches, points, cols), phi.dtype),
            jax.ShapeDtypeStruct(meta, starts.dtype),
            jax.ShapeDtypeStruct((SLOTS, planes, per_plane) + row_pair, f32),
            jax.ShapeDtypeStruct(picks, phi.dtype),
            jax.ShapeDtypeStruct(far_picks, phi.dtype),
        ),
        in_specs=[far, far, smem, smem, far, vmem],
        out_specs=[far] * 5,
        scratch_shapes=[
            pltpu.VMEM((SLOTS, batches, points, cols), phi.dtype),
            pltpu.VMEM((2, BAND, rows, BLOCK), density.dtype),
            pltpu.VMEM((rows, COLS), density.dtype),
            pltpu.VMEM(density.shape, density.dtype),
            pltpu.VMEM((PERTS, share, COLS), density.dtype),
            pltpu.VMEM(meta, starts.dtype),
            pltpu.VMEM((SLOTS,) + meta, starts.dtype),
            pltpu.VMEM(meta, starts.dtype),
            pltpu.SMEM(meta, starts.dtype),
            pltpu.SMEM(pair_mask.shape, pair_mask.dtype),
            pltpu.VMEM(picks, phi.dtype),
            pltpu.VMEM(far_picks, phi.dtype),
            pltpu.VMEM((SLOTS, batches) + row_pair, f32),
            pltpu.VMEM((3, batches) + row_pair, f32),
            pltpu.VMEM((3, planes, per_plane) + row_pair, f32),
            pltpu.VMEM((per_plane,) + row_pair, f32),
            dma((9,)), dma((SLOTS, batches)), dma((batches,)), dma((batches,)),
            dma((2, half, 2)), dma((2, half, 2)), dma((2, half, 2)), dma((2, half, 2)),
            dma((2, batches, 2)), dma((2, batches, 2)), dma((5,)), dma((5,)), dma((2,)),
            dma((3, batches)), dma((3, batches)), dma((3, batches)), dma((3, planes, per_plane)),
            dma((3, planes)), dma((3, planes)), dma((3, planes)), dma((3, planes)),
        ],
        compiler_params=pltpu.CompilerParams(collective_id=0, has_side_effects=True, vmem_limit_bytes=56 << 20),
        cost_estimate=pl.CostEstimate(flops=17 * 10**9, bytes_accessed=50 * 10**6, transcendentals=0),
        name="potentials",
    )(phi, density, starts, counts, pair_mask, kern)


def joined(halves):
    return jnp.concatenate([halves[:PERTS], halves[PERTS:]], axis=1)


def split_weights(pot, picked, scale):
    weighted = (pot[:, None, :] * picked[None]).reshape(pot.shape[0] * picked.shape[0], picked.shape[1])
    high = weighted.astype(jnp.bfloat16)
    low = ((weighted - high.astype(jnp.float32)) * scale).astype(EIGHT)
    return high, low


CUT = POINTS // 2
LARGEST = 8
EIGHT = jnp.float8_e4m3fn
ROOM = 448.0 / (6.0 * 2.0**-8)


class Chunks:
    def __init__(self, batches, facts_ref, pot, pick, phi_ref, listed, counted, buf, sems, scale):
        self.batches, self.facts, self.pot, self.pick, self.phi = batches, facts_ref, pot, pick, phi_ref
        self.listed, self.counted, self.buf, self.sems, self.scale = listed, counted, buf, sems, scale

    def set_scale(self, pots):
        most = jnp.maximum(jnp.max(jnp.abs(pots)), 1e-30)
        self.scale[0] = ROOM / most
        self.scale[1] = most * (1.0 / ROOM)

    def start(self, no):
        return self.facts[no // self.batches, lax.rem(no, self.batches)]

    def note(self, which, no, wanted):
        most = self.pot.shape[0] * 2
        many = self.facts[no // self.batches, self.batches + lax.rem(no, self.batches)] > CUT

        @pl.when(wanted)
        def _():
            have = self.counted[which]
            self.listed[which * most + have] = 2 * no
            self.listed[which * most + have + 1] = 2 * no + 1
            self.counted[which] = have + 1 + many.astype(jnp.int32)

    def copy(self, chunk):
        no, h = chunk // 2, lax.rem(chunk, 2)
        return pltpu.make_async_copy(
            self.phi.at[no // self.batches, lax.rem(no, self.batches), pl.ds(pl.multiple_of(h * CUT, CUT), CUT)],
            self.buf.at[chunk], self.sems.at[chunk])

    def fetch(self, which):
        @pl.loop(0, self.counted[which])
        def _(i):
            self.copy(self.listed[which * self.pot.shape[0] * 2 + i]).start()

    def group(self, which, at, size, rows):
        rights, highs, lows = [], [[] for _ in rows], [[] for _ in rows]
        scale = self.scale[0]
        for i in range(size):
            chunk = self.listed[which * self.pot.shape[0] * 2 + at + i]
            self.copy(chunk).wait()
            pots = self.pot[chunk // 2]
            pot = jnp.where(lax.rem(chunk, 2) == 0, pots[:PERTS], pots[PERTS:])
            rights.append(self.buf[chunk])
            for no, (row, _) in enumerate(rows):
                high, low = split_weights(pot, self.pick(chunk, row).astype(jnp.float32), scale)
                highs[no].append(high)
                lows[no].append(low)
        right = jnp.concatenate(rights, axis=0)
        left = jnp.concatenate([jnp.concatenate(high, axis=1) for high in highs], axis=0)
        total = jnp.dot(left, right, preferred_element_type=jnp.float32)
        low = jnp.concatenate([jnp.concatenate(low, axis=1) for low in lows], axis=0)
        rest = jnp.dot(low, right.astype(EIGHT), preferred_element_type=jnp.float32)
        total = total + rest * self.scale[1]
        depth = left.shape[0] // len(rows)
        for no, (_, spot) in enumerate(rows):
            spot[...] = spot[...] + total[no * depth:(no + 1) * depth].reshape(spot.shape)

    def add(self, which, rows):
        count = self.counted[which]
        size = LARGEST
        done = 0
        while size:
            times = (count - done) // size

            @pl.loop(0, times)
            def _(i, size=size, done=done):
                self.group(which, done + i * size, size, rows)

            done = done + times * size
            size //= 2


def fock_kernel(batches, share, facts_ref, pot_ref, picks_ref, phi_ref, out_ref,
                total, pot_v, picks_v, listed, counted, buf, sems, scale, in_sem, out_sem):
    grid_pos = lax.axis_index("grid")
    pot_copy = pltpu.make_async_copy(pot_ref, pot_v, in_sem.at[0])
    pot_copy.start()
    picks_copy = pltpu.make_async_copy(picks_ref, picks_v, in_sem.at[1])
    picks_copy.start()
    chunks = Chunks(batches, facts_ref, pot_v, lambda chunk, row: picks_v[chunk, row], phi_ref, listed, counted, buf, sems,
                    scale)
    base = 2 * grid_pos - REACH
    leads = REACH + 2

    for lead in range(leads):
        counted[lead] = 0

    @pl.loop(0, SLOTS * batches)
    def _(no):
        lead = chunks.start(no) - base
        chunks.note(lead, no, jnp.logical_and(lead >= 0, lead < leads))

    chunks.fetch(0)
    chunks.fetch(1)
    total[...] = jnp.zeros_like(total)
    pot_copy.wait()
    chunks.set_scale(pot_v[...])
    picks_copy.wait()

    def spot(r, offset):
        return total.at[r, :, :, pl.ds(pl.multiple_of((REACH - offset) * BLOCK, BLOCK), COLS)]

    def out_copy(r, t):
        cols = pl.ds(pl.multiple_of(t * BLOCK, BLOCK), BLOCK)
        return pltpu.make_async_copy(total.at[r, :, :, cols], out_ref.at[r, :, :, cols], out_sem.at[r, t])

    def leave(r, t):
        @pl.when(facts_ref[SLOTS + r, t] == 0)
        def _():
            cols = pl.ds(pl.multiple_of(t * BLOCK, BLOCK), BLOCK)
            total[r, :, :, cols] = jnp.zeros((PERTS, share, BLOCK), jnp.float32)

        out_copy(r, t).start()

    @pl.loop(0, leads)
    def _(lead):
        @pl.when(lead + 2 < leads)
        def _():
            chunks.fetch(lead + 2)

        both = jnp.logical_and(lead >= 1, lead <= REACH)

        @pl.when(both)
        def _():
            offset = REACH - lead
            chunks.add(lead, [(0, spot(0, offset)), (1, spot(1, offset + 1))])

        @pl.when(jnp.logical_not(both))
        def _():
            r = jnp.where(lead == 0, 0, 1)
            offset = jnp.where(lead == 0, REACH, 0)
            chunks.add(lead, [(r, spot(r, offset))])

        @pl.loop(lead, jnp.where(lead == REACH, BAND, jnp.minimum(lead + 1, REACH + 1)))
        def _(t):
            leave(0, t)

        @pl.loop(jnp.maximum(lead - 1, 0), jnp.where(lead == REACH + 1, BAND, lead))
        def _(t):
            leave(1, t)

    @pl.loop(0, BAND)
    def _(t):
        for r in range(2):
            out_copy(r, t).wait()


def chunk_scratch(slots, batches, cols, lists, dtype):
    most = 2 * slots * batches
    return [
        pltpu.SMEM((lists * most,), jnp.int32),
        pltpu.SMEM((lists,), jnp.int32),
        pltpu.VMEM((most, CUT, cols), dtype),
        pltpu.SemaphoreType.DMA((most,)),
        pltpu.SMEM((2,), jnp.float32),
    ]


def fock_own(facts, pot, picks, phi_all, share):
    slots, batches, points, cols = phi_all.shape
    far = pl.BlockSpec(memory_space=pl.ANY)
    whole = (2, PERTS, share, WIDE)
    dma = pltpu.SemaphoreType.DMA
    return pl.pallas_call(
        functools.partial(fock_kernel, batches, share),
        out_shape=jax.ShapeDtypeStruct(whole, jnp.float32),
        in_specs=[pl.BlockSpec(memory_space=pltpu.SMEM), far, far, far],
        out_specs=far,
        scratch_shapes=[
            pltpu.VMEM(whole, jnp.float32), pltpu.VMEM(pot.shape, pot.dtype), pltpu.VMEM(picks.shape, picks.dtype),
        ]
        + chunk_scratch(slots, batches, cols, REACH + 2, phi_all.dtype)
        + [dma((2,)), dma((2, BAND))],
        compiler_params=pltpu.CompilerParams(vmem_limit_bytes=56 << 20),
        cost_estimate=pl.CostEstimate(flops=20 * 10**9, bytes_accessed=20 * 10**6, transcendentals=0),
        name="fock_own",
    )(facts, pot, picks, phi_all)


def far_kernel(batches, facts_ref, pot_ref, picks_ref, phi_ref, out_ref, pot_v, picks_v, listed, counted, buf, sems, scale, in_sem):
    grid_pos = lax.axis_index("grid")
    core = lax.rem(grid_pos, 2)
    slot = jnp.where(core == 0, 4, 1)
    far_start = 4 * (grid_pos // 2) - 1
    own = pl.ds(slot * batches, batches)
    pot_copy = pltpu.make_async_copy(pot_ref.at[own], pot_v.at[own], in_sem.at[0])
    pot_copy.start()
    picks_copy = pltpu.make_async_copy(picks_ref, picks_v, in_sem.at[1])
    picks_copy.start()
    chunks = Chunks(batches, facts_ref, pot_v, lambda chunk, row: picks_v[chunk - 2 * batches * slot], phi_ref,
                    listed, counted, buf, sems, scale)
    counted[0] = 0

    @pl.loop(0, batches)
    def _(no):
        chunks.note(0, slot * batches + no, chunks.start(slot * batches + no) == far_start)

    chunks.fetch(0)
    out_ref[...] = jnp.zeros_like(out_ref)
    pot_copy.wait()
    chunks.set_scale(pot_v[own])
    picks_copy.wait()
    chunks.add(0, [(0, out_ref)])


def fock_far(facts, pot, far_picks, phi_all, share):
    slots, batches, points, cols = phi_all.shape
    smem = pl.BlockSpec(memory_space=pltpu.SMEM)
    far = pl.BlockSpec(memory_space=pl.ANY)
    vmem = pl.BlockSpec(memory_space=pltpu.VMEM)
    return pl.pallas_call(
        functools.partial(far_kernel, batches),
        out_shape=jax.ShapeDtypeStruct((PERTS, share, COLS), jnp.float32),
        in_specs=[smem, far, far, far],
        out_specs=vmem,
        scratch_shapes=[pltpu.VMEM(pot.shape, pot.dtype), pltpu.VMEM(far_picks.shape, far_picks.dtype)]
        + chunk_scratch(slots, batches, cols, 1, phi_all.dtype)
        + [pltpu.SemaphoreType.DMA((2,))],
        compiler_params=pltpu.CompilerParams(vmem_limit_bytes=56 << 20),
        cost_estimate=pl.CostEstimate(flops=10**9, bytes_accessed=2 * 10**6, transcendentals=0),
        name="fock_far",
    )(facts, pot, far_picks, phi_all)


def shards(density, basis_vals, kernel, starts, counts, pair_mask):
    grid_size, planes = lax.axis_size("grid"), lax.axis_size("basis")
    batches, share = basis_vals.shape[0], density.shape[2]
    grid_pos = lax.axis_index("grid")
    core = lax.rem(grid_pos, 2)
    phi_all, facts, pot, picks, far_picks = potentials(
        basis_vals, density, starts, counts, pair_mask.T, kernel, grid_size // 2, planes)
    pot = pot.reshape(SLOTS * batches, 2 * PERTS, POINTS // 2)
    picks = picks.reshape(2 * SLOTS * batches, 2, share, POINTS // 2)
    far_picks = far_picks.reshape(2 * batches, share, POINTS // 2)
    far = fock_far(facts, pot, far_picks, phi_all, share)
    route = [(i, i + 1 if i % 2 else i - 1) for i in range(1, grid_size - 1)]
    arrived = lax.ppermute(far, "grid", route)
    own = fock_own(facts, pot, picks, phi_all, share)
    mask_row = lax.dynamic_slice(pair_mask, (2 * grid_pos + core, core * REACH), (1, WINDOW))[0]
    keep = jnp.repeat(mask_row, BLOCK).astype(jnp.float32)
    place = (core, 0, 0, core * REACH * BLOCK)
    present = lax.dynamic_slice(own, place, (1, PERTS, share, COLS))
    return lax.dynamic_update_slice(own, present + (arrived * keep)[None], place)


def solution(mesh):
    placed = (
        P("grid", None, "basis", None),
        P("grid", None, None),
        P("grid", None),
        P("grid"),
        P("grid"),
        P(),
    )
    return jax.shard_map(
        shards,
        mesh=mesh,
        in_specs=placed,
        out_specs=P("grid", None, "basis", None),
        check_vma=False,
    )
```

```python
import functools

import jax
import jax.numpy as jnp
from jax import lax
from jax.experimental import pallas as pl
from jax.experimental.pallas import tpu as pltpu
from jax.sharding import PartitionSpec as P

BLOCK = 128
PERTS = 12
WINDOW = 6
POINTS = 256
REACH = 5
BAND = 11
COLS = WINDOW * BLOCK
WIDE = BAND * BLOCK
SLOTS = 6
MESH = pl.DeviceIdType.MESH
NT = (((1,), (1,)), ((), ()))


def one_hot(share, columns, first):
    rows = lax.broadcasted_iota(jnp.int32, (share, columns), 0)
    lanes = lax.broadcasted_iota(jnp.int32, (share, columns), 1)
    return jnp.where(lanes == rows + first, 1.0, 0.0).astype(jnp.bfloat16)


def density_kernel(
    chips, planes, batches, share,
    phi_ref, dens_ref, starts_ref, counts_ref, mask_ref, kern_ref,
    all_ref, facts_ref, pot_ref, picks_ref, far_picks_ref,
    phi_v, dens_v, far_v, left_v, left_far, meta_v, meta_all_v, facts_v, meta_s, mask_s, picks_v, far_picks_v, part, mate, gathered, pot_v,
    own_sem, out_sem, core_s, core_r, y_s, y_r, z_s, z_r, c_s, c_r, m_s, m_r, f_sem, k_s, k_r, a_s, a_r, b_s, b_r, g_s, g_r,
):
    grid_pos, plane = lax.axis_index("grid"), lax.axis_index("basis")
    chip, core = grid_pos // 2, lax.rem(grid_pos, 2)
    half = batches // 2
    quarter = half // 2
    per_plane = batches // planes
    own_slot = 2 + core
    far_slot = jnp.where(core == 0, 4, 1)
    first = lax.rem(plane, 2) * half
    there = half - first
    rows_all = PERTS * share
    cut = POINTS // 2
    has_down, has_up = chip > 0, chip < chips - 1
    sends, comes = (has_up, has_down), (has_down, has_up)
    far_exists = jnp.where(core == 0, chip, chips - 1 - chip) > 0

    def exists(d):
        return jnp.where(d == 0, chip, jnp.where(d == 2, chips - 1 - chip, 1)) > 0

    def device(slot, at_plane):
        return (2 * lax.rem(chip + slot // 2 - 1 + chips, chips) + lax.rem(slot, 2), at_plane)

    other = (2 * chip + 1 - core, plane)

    def remote(src, dst, send, recv, to):
        return pltpu.make_async_remote_copy(
            src_ref=src, dst_ref=dst, send_sem=send, recv_sem=recv, device_id=to, device_id_type=MESH)

    def is_other(d, at_plane):
        return jnp.logical_or(d != 1, at_plane != plane)

    def for_others(act, order=(0, 2, 1)):
        @pl.loop(0, 3 * planes)
        def _(no):
            turn, at_plane = no // planes, lax.rem(no, planes)
            d = jnp.where(turn == 0, order[0], jnp.where(turn == 1, order[1], order[2]))

            @pl.when(jnp.logical_and(is_other(d, at_plane), exists(d)))
            def _():
                act(d, at_plane)

    own_copy = pltpu.make_async_copy(phi_ref, phi_v.at[own_slot], own_sem.at[0])
    own_copy.start()
    dens_copy = pltpu.make_async_copy(dens_ref, left_v, own_sem.at[1])
    dens_copy.start()
    mask_copy = pltpu.make_async_copy(mask_ref, mask_s, own_sem.at[2])
    mask_copy.start()

    line = lax.broadcasted_iota(jnp.int32, (8, BLOCK), 0)
    lane = lax.broadcasted_iota(jnp.int32, (8, BLOCK), 1)
    meta = jnp.zeros((8, BLOCK), jnp.int32)
    for no in range(batches):
        meta = jnp.where(lane == no, starts_ref[no], meta)
        meta = jnp.where(lane == batches + no, counts_ref[no], meta)
    meta_v[...] = meta
    meta_all_v[own_slot] = meta

    barrier = pltpu.get_barrier_semaphore()
    for there_is, slots in ((has_down, (0, 1)), (has_up, (4, 5))):
        @pl.when(there_is)
        def _(slots=slots):
            for slot in slots:
                pl.semaphore_signal(barrier, inc=1, device_id=device(slot, plane), device_id_type=MESH)

    for partner in (other, (grid_pos, lax.rem(plane + 1, planes)), (grid_pos, lax.rem(plane + planes - 1, planes))):
        pl.semaphore_signal(barrier, inc=1, device_id=partner, device_id_type=MESH)
    pl.semaphore_wait(barrier, 3 + 2 * has_down.astype(jnp.int32) + 2 * has_up.astype(jnp.int32))

    def piece(way, n):
        return n // 2 + quarter * lax.rem(n + way, 2)

    def rows(h):
        return pl.ds(h * cut, cut)

    def y_copy(way, n, h):
        at = first + piece(way, n)
        return remote(phi_ref.at[at, rows(h)], phi_v.at[4 * way + core, at, rows(h)], y_s.at[way, n, h], y_r.at[way, n, h],
                      device(4 - 4 * way + core, plane))

    def z_copy(way, n, h):
        which = piece(way, n)
        where = phi_v.at[4 * way + core, first + which, rows(h)]
        to = lax.rem(plane + 1 - 2 * (which // quarter) + planes, planes)
        return remote(where, where, z_s.at[way, n, h], z_r.at[way, n, h], (grid_pos, to))

    def c_copy(way, m, h):
        at = jnp.where(m < half, first, there) + piece(way, lax.rem(m, half))
        where = phi_v.at[4 * way + core, at, rows(h)]
        return remote(where, where, c_s.at[way, m, h], c_r.at[way, m, h], other)

    def core_copy(no):
        return remote(phi_ref.at[no], phi_v.at[own_slot, no], core_s.at[no], core_r.at[no], other)

    def meta_copy(way, s):
        return remote(meta_v, meta_all_v.at[4 * way + core], m_s.at[1 + 2 * way + s], m_r.at[1 + 2 * way + core],
                      device(4 - 4 * way + s, plane))

    def out_copy(slot, no):
        return pltpu.make_async_copy(phi_v.at[slot, no], all_ref.at[slot, no], out_sem.at[slot, no])

    far_copy = remote(dens_ref.at[core, :, :, pl.ds(pl.multiple_of(core * REACH * BLOCK, BLOCK), COLS)], left_far,
                      f_sem.at[0], f_sem.at[1], device(jnp.where(core == 0, 1, 4), plane))
    core_meta = remote(meta_v, meta_all_v.at[own_slot], m_s.at[0], m_r.at[0], other)

    core_meta.start()
    for way in range(2):
        @pl.when(sends[way])
        def _(way=way):
            for s in range(2):
                meta_copy(way, s).start()

        @pl.when(jnp.logical_not(comes[way]))
        def _(way=way):
            for s in range(2):
                meta_all_v[4 * way + s] = jnp.full((8, BLOCK), -1000, jnp.int32)

    @pl.loop(0, half)
    def _(n):
        for h in range(2):
            for way in range(2):
                @pl.when(sends[way])
                def _(way=way, h=h):
                    y_copy(way, n, h).start()

    @pl.when(far_exists)
    def _():
        far_copy.start()

    @pl.loop(0, batches)
    def _(no):
        core_copy(no).start()

    def masked(block, keep):
        return block * keep.astype(jnp.float32).astype(block.dtype)

    def same(left, right):
        return (1 - jnp.minimum(jnp.abs(left - right), 1)).astype(jnp.float32)

    mask_copy.wait()
    dens_copy.wait()
    for r in range(2):
        row = 2 * grid_pos + r
        for t in range(BAND):
            block = left_v[r, :, :, t * BLOCK:(t + 1) * BLOCK].reshape(rows_all, BLOCK)
            dens_v[r, t, :rows_all, :] = masked(block, mask_s[t, row])
            dens_v[r, t, rows_all:, :] = one_hot(share, BLOCK, (REACH - t) * BLOCK + plane * share)
    far_v[rows_all:, :] = one_hot(share, COLS, core * REACH * BLOCK + plane * share)

    own_copy.wait()
    pltpu.make_async_copy(meta_v, meta_all_v.at[own_slot], m_r.at[0]).wait()
    for way in range(2):
        @pl.when(comes[way])
        def _(way=way):
            for s in range(2):
                pltpu.make_async_copy(meta_v, meta_all_v.at[own_slot], m_r.at[1 + 2 * way + s]).wait()

    facts = jnp.zeros((8, BLOCK), jnp.int32)
    for slot in range(SLOTS):
        facts = jnp.where(line == slot, meta_all_v[slot], facts)
    for r in range(2):
        for t in range(BAND):
            facts = jnp.where(jnp.logical_and(line == SLOTS + r, lane == t), mask_s[t, 2 * grid_pos + r], facts)
    facts_v[...] = facts
    to_smem = pltpu.make_async_copy(facts_v, meta_s, own_sem.at[3])
    to_smem.start()
    facts_out = pltpu.make_async_copy(facts_v, facts_ref, own_sem.at[4])
    facts_out.start()
    to_smem.wait()

    def reduced(mixed, keep_picks):
        picked = mixed[rows_all:]
        for h in range(2):
            keep_picks(h, picked[:, h * cut:(h + 1) * cut].astype(jnp.bfloat16))
        sums = jnp.sum(mixed[:rows_all].reshape(PERTS, share, POINTS) * picked[None], axis=1)
        return jnp.concatenate([sums[:, :cut], sums[:, cut:]], axis=0)

    def spread_rows(slot, no, r):
        offset = 2 * grid_pos + r - meta_s[slot, no]
        inside = jnp.clip(offset, 0, WINDOW - 1)
        lhs = jnp.concatenate([dens_v[r, REACH - inside + c] for c in range(WINDOW)], axis=1)
        return lhs, same(offset, inside)

    def rho_part(slot, no, blocks):
        out_copy(slot, no).start()
        lhs, keeps = zip(*[spread_rows(slot, no, r) for r in blocks])
        mixed = lax.dot_general(jnp.concatenate(lhs, axis=0), phi_v[slot, no], NT, preferred_element_type=jnp.float32)
        total = None
        for i, r in enumerate(blocks):
            def keep_picks(h, value, r=r):
                picks_v[slot, no, h, r] = value

            term = reduced(mixed[i * (rows_all + share):(i + 1) * (rows_all + share)], keep_picks) * keeps[i]
            total = term if total is None else total + term
        part[slot, no] = total

    far_start = 4 * chip - 1

    def rho_far(pair):
        phi = phi_v[far_slot, pl.ds(2 * pair, 2)].reshape(2 * POINTS, COLS)
        mixed = lax.dot_general(far_v[...], phi, NT, preferred_element_type=jnp.float32)
        for i in range(2):
            no = 2 * pair + i

            def keep_picks(h, value, no=no):
                far_picks_v[no, h] = value

            term = reduced(mixed[:, i * POINTS:(i + 1) * POINTS], keep_picks)
            part[far_slot, no] = part[far_slot, no] + term * same(meta_s[far_slot, no], far_start)

    def mate_copy(d, no):
        return remote(part.at[2 * d + 1 - core, no], mate.at[d, no], k_s.at[d, no], k_r.at[d, no], other)

    def part_copy(d, no):
        keeper = no // per_plane
        which = lax.rem(no, per_plane)
        return remote(part.at[2 * d + core, no], gathered.at[2 - d, plane, which], a_s.at[d, no], a_r.at[2 - d, plane, which],
                      device(2 * d + core, keeper))

    def combine(d, no):
        slot = 2 * d + core
        pltpu.make_async_copy(part.at[slot, no], mate.at[d, no], k_r.at[d, no]).wait()
        part[slot, no] = part[slot, no] + mate[d, no]
        away = is_other(d, no // per_plane)

        @pl.when(away)
        def _():
            part_copy(d, no).start()

        @pl.when(jnp.logical_not(away))
        def _():
            gathered[1, plane, lax.rem(no, per_plane)] = part[slot, no]

    def pair(n, crossed, late):
        lead = jnp.where(crossed, core, 0)
        at = jnp.where(late, there, first)
        return tuple((4 * way + jnp.where(crossed, 1 - core, core), at + piece(way, n)) for way in (lead, 1 - lead))

    def items_before(m, act):
        odd = lax.rem(m, 2) == 1

        @pl.loop(0, 3)
        def _(item):
            mine = 2 * (m + 1) + item - 1
            slot = jnp.where(mine < half, own_slot, 5 - own_slot)
            at = 2 * lax.rem(mine, half)
            arrived = pair(jnp.maximum(m - 1, 0) // 2, False, False)
            is_own = item > 0
            chosen = tuple((jnp.where(is_own, slot, s), jnp.where(is_own, at + i, no)) for i, (s, no) in enumerate(arrived))

            @pl.when(jnp.logical_or(jnp.logical_and(is_own, m <= 2),
                                    jnp.logical_and(jnp.logical_not(is_own), jnp.logical_and(odd, m <= 2 * half - 1))))
            def _():
                act(chosen, False)

        @pl.when(m >= 2)
        def _():
            act(pair((m - 2 - lax.rem(m, 2)) // 2, True, odd), True)

    def items_after(m, act):
        @pl.when(jnp.logical_and(m >= 2, jnp.logical_and(lax.rem(m, 2) == 0, m <= 2 * half)))
        def _():
            act(pair((m - 2) // 2, False, True), False)

    def compute(batch_pair, crossed):
        rho_part(*batch_pair[0], (0, 1))
        rho_part(*batch_pair[1], (1 - core,) if crossed else (0, 1))
        for slot, no in batch_pair:
            @pl.when(jnp.logical_and(lax.rem(slot, 2) != core, exists(slot // 2)))
            def _():
                mate_copy(slot // 2, no).start()

    def combine_pair(m):
        late = jnp.where(lax.rem(m, 2) == 0, 1, 0)
        for slot, no in pair((m - 3 - late) // 2, False, late == 1):
            @pl.when(jnp.logical_and(slot != far_slot, exists(slot // 2)))
            def _():
                combine(slot // 2, no)

    @pl.loop(0, 2 * half + 3)
    def _(step):
        m = step - 1

        @pl.when(jnp.logical_and(m >= 0, m < 2 * half))
        def _():
            n, h = m // 2, lax.rem(m, 2)
            for way in range(2):
                @pl.when(comes[way])
                def _(way=way):
                    y_copy(way, n, h).wait_recv()
                    z_copy(way, n, h).start()
                    c_copy(way, n, h).start()

        @pl.when(jnp.logical_or(m == 1, m == 2))
        def _():
            for i in range(half):
                core_copy((m - 1) * half + i).wait_recv()

        @pl.when(m >= 2)
        def _():
            late = lax.rem(m, 2)
            for way in range(2):
                @pl.when(comes[way])
                def _(way=way):
                    for h in range(2):
                        c_copy(way, late * half + (m - 2 - late) // 2, h).wait_recv()

        @pl.when(m == half + 1)
        def _():
            @pl.loop(0, batches)
            def _(no):
                combine(1, no)

            @pl.loop(3, half + 1)
            def _(before):
                combine_pair(before)

        items_before(m, compute)

        @pl.when(jnp.logical_and(m >= 1, m <= 2 * half))
        def _():
            n, h = (m - 1) // 2, lax.rem(m - 1, 2)
            for way in range(2):
                @pl.when(comes[way])
                def _(way=way):
                    z_copy(way, n, h).wait_recv()
                    c_copy(way, half + n, h).start()

        items_after(m, compute)

        @pl.when(m > half)
        def _():
            combine_pair(m)

    combine_pair(2 * half + 2)
    @pl.when(far_exists)
    def _():
        far_copy.wait_recv()
        far_row = jnp.where(core == 0, jnp.maximum(2 * grid_pos - 1, 0), jnp.minimum(2 * grid_pos + 2, 4 * chips - 1))
        for t in range(WINDOW):
            block = left_far[:, :, t * BLOCK:(t + 1) * BLOCK].reshape(rows_all, BLOCK)
            keep = mask_s[jnp.where(core == 0, REACH, 0) + t, far_row]
            far_v[:rows_all, t * BLOCK:(t + 1) * BLOCK] = masked(block, keep)

    @pl.loop(0, half)
    def _(two):
        @pl.when(far_exists)
        def _():
            rho_far(two)

        @pl.when(exists(far_slot // 2))
        def _():
            for i in range(2):
                combine(far_slot // 2, 2 * two + i)

    picks_out = pltpu.make_async_copy(picks_v, picks_ref, own_sem.at[1])
    picks_out.start()
    far_picks_out = pltpu.make_async_copy(far_picks_v, far_picks_ref, own_sem.at[2])
    far_picks_out.start()

    def pot_copy(d, at_plane):
        return remote(pot_v, pot_ref.at[2 * (2 - d) + core, plane], b_s.at[d, at_plane], b_r.at[2 - d, plane],
                      device(2 * d + core, at_plane))

    def cross_copy(d, at_plane):
        where = pot_ref.at[2 * d + core, at_plane]
        return remote(where, where, g_s.at[d, at_plane], g_r.at[d, at_plane], other)

    own_cross = remote(pot_v, pot_ref.at[own_slot, plane], g_s.at[1, plane], g_r.at[1, plane], other)

    def wait_parts(d, at_plane):
        for which in range(per_plane):
            pltpu.make_async_copy(part.at[0, 0], gathered.at[d, at_plane, which], a_r.at[d, at_plane, which]).wait()

    def no_pot_copy(way, s):
        return pltpu.make_async_copy(gathered.at[2 * way], pot_ref.at[4 * way + s], own_sem.at[5 + 2 * way + s])

    for way in range(2):
        @pl.when(jnp.logical_not(comes[way]))
        def _(way=way):
            gathered[2 * way] = jnp.zeros((planes, per_plane, 2 * PERTS, cut), jnp.float32)
            for s in range(2):
                no_pot_copy(way, s).start()

    for_others(wait_parts)
    points = lax.broadcasted_iota(jnp.int32, (1, POINTS), 1)
    for no in range(per_plane):
        rho = gathered[0, 0, no]
        for d in range(3):
            for at_plane in range(planes):
                if d or at_plane:
                    rho = rho + gathered[d, at_plane, no]
        mine = per_plane * plane + no
        live = jnp.clip(counts_ref[mine] - points, 0, 1).astype(jnp.float32)
        factor = jnp.broadcast_to(kern_ref[pl.ds(mine, 1), :] * live, (PERTS, POINTS))
        pot_v[no] = rho * jnp.concatenate([factor[:, :cut], factor[:, cut:]], axis=0)
    for_others(lambda d, at_plane: pot_copy(d, at_plane).start())
    own_cross.start()
    pot_own = pltpu.make_async_copy(pot_v, pot_ref.at[own_slot, plane], own_sem.at[0])
    pot_own.start()

    facts_out.wait()
    picks_out.wait()
    far_picks_out.wait()

    @pl.when(far_exists)
    def _():
        far_copy.wait_send()

    core_meta.wait_send()
    for way in range(2):
        @pl.when(sends[way])
        def _(way=way):
            for s in range(2):
                meta_copy(way, s).wait_send()

        @pl.when(jnp.logical_not(comes[way]))
        def _(way=way):
            for s in range(2):
                no_pot_copy(way, s).wait()

    @pl.loop(0, batches)
    def _(no):
        core_copy(no).wait_send()
        for slot in range(SLOTS):
            out_copy(slot, no).wait()
        for d in range(3):
            @pl.when(exists(d))
            def _(d=d):
                mate_copy(d, no).wait_send()

            @pl.when(jnp.logical_and(is_other(d, no // per_plane), exists(d)))
            def _(d=d):
                part_copy(d, no).wait_send()

    @pl.loop(0, half)
    def _(n):
        for h in range(2):
            for way in range(2):
                @pl.when(sends[way])
                def _(way=way, h=h):
                    y_copy(way, n, h).wait_send()

                @pl.when(comes[way])
                def _(way=way, h=h):
                    z_copy(way, n, h).wait_send()
                    c_copy(way, n, h).wait_send()
                    c_copy(way, half + n, h).wait_send()

    def pass_on(d, at_plane):
        pltpu.make_async_copy(pot_v, pot_ref.at[2 * d + core, at_plane], b_r.at[d, at_plane]).wait()
        cross_copy(d, at_plane).start()

    for_others(pass_on, (1, 0, 2))

    @pl.loop(0, 3 * planes)
    def _(no):
        @pl.when(exists(no // planes))
        def _():
            cross_copy(no // planes, lax.rem(no, planes)).wait_recv()

    pot_own.wait()
    own_cross.wait_send()
    for_others(lambda d, at_plane: cross_copy(d, at_plane).wait_send())
    for_others(lambda d, at_plane: pot_copy(d, at_plane).wait_send())


def potentials(phi, density, starts, counts, pair_mask, kern, chips, planes):
    batches, points, cols = phi.shape
    share = density.shape[2]
    half, per_plane = batches // 2, batches // planes
    rows = PERTS * share + share
    far = pl.BlockSpec(memory_space=pl.ANY)
    smem = pl.BlockSpec(memory_space=pltpu.SMEM)
    vmem = pl.BlockSpec(memory_space=pltpu.VMEM)
    dma = pltpu.SemaphoreType.DMA
    f32 = jnp.float32
    row_pair = (2 * PERTS, points // 2)
    meta = (8, BLOCK)
    picks, far_picks = (SLOTS, batches, 2, 2, share, points // 2), (batches, 2, share, points // 2)
    return pl.pallas_call(
        functools.partial(density_kernel, chips, planes, batches, share),
        out_shape=(
            jax.ShapeDtypeStruct((SLOTS, batches, points, cols), phi.dtype),
            jax.ShapeDtypeStruct(meta, starts.dtype),
            jax.ShapeDtypeStruct((SLOTS, planes, per_plane) + row_pair, f32),
            jax.ShapeDtypeStruct(picks, phi.dtype),
            jax.ShapeDtypeStruct(far_picks, phi.dtype),
        ),
        in_specs=[far, far, smem, smem, far, vmem],
        out_specs=[far] * 5,
        scratch_shapes=[
            pltpu.VMEM((SLOTS, batches, points, cols), phi.dtype),
            pltpu.VMEM((2, BAND, rows, BLOCK), density.dtype),
            pltpu.VMEM((rows, COLS), density.dtype),
            pltpu.VMEM(density.shape, density.dtype),
            pltpu.VMEM((PERTS, share, COLS), density.dtype),
            pltpu.VMEM(meta, starts.dtype),
            pltpu.VMEM((SLOTS,) + meta, starts.dtype),
            pltpu.VMEM(meta, starts.dtype),
            pltpu.SMEM(meta, starts.dtype),
            pltpu.SMEM(pair_mask.shape, pair_mask.dtype),
            pltpu.VMEM(picks, phi.dtype),
            pltpu.VMEM(far_picks, phi.dtype),
            pltpu.VMEM((SLOTS, batches) + row_pair, f32),
            pltpu.VMEM((3, batches) + row_pair, f32),
            pltpu.VMEM((3, planes, per_plane) + row_pair, f32),
            pltpu.VMEM((per_plane,) + row_pair, f32),
            dma((9,)), dma((SLOTS, batches)), dma((batches,)), dma((batches,)),
            dma((2, half, 2)), dma((2, half, 2)), dma((2, half, 2)), dma((2, half, 2)),
            dma((2, batches, 2)), dma((2, batches, 2)), dma((5,)), dma((5,)), dma((2,)),
            dma((3, batches)), dma((3, batches)), dma((3, batches)), dma((3, planes, per_plane)),
            dma((3, planes)), dma((3, planes)), dma((3, planes)), dma((3, planes)),
        ],
        compiler_params=pltpu.CompilerParams(collective_id=0, has_side_effects=True, vmem_limit_bytes=56 << 20),
        cost_estimate=pl.CostEstimate(flops=17 * 10**9, bytes_accessed=50 * 10**6, transcendentals=0),
        name="potentials",
    )(phi, density, starts, counts, pair_mask, kern)


def joined(halves):
    return jnp.concatenate([halves[:PERTS], halves[PERTS:]], axis=1)


def split_weights(pot, picked, scale):
    weighted = (pot[:, None, :] * picked[None]).reshape(pot.shape[0] * picked.shape[0], picked.shape[1])
    high = weighted.astype(jnp.bfloat16)
    low = ((weighted - high.astype(jnp.float32)) * scale).astype(EIGHT)
    return high, low


CUT = POINTS // 2
LARGEST = 8
EIGHT = jnp.float8_e4m3fn
ROOM = 448.0 / (6.0 * 2.0**-8)


class Chunks:
    def __init__(self, batches, facts_ref, pot, pick, phi_ref, listed, counted, buf, sems, scale):
        self.batches, self.facts, self.pot, self.pick, self.phi = batches, facts_ref, pot, pick, phi_ref
        self.listed, self.counted, self.buf, self.sems, self.scale = listed, counted, buf, sems, scale

    def set_scale(self, pots):
        most = jnp.maximum(jnp.max(jnp.abs(pots)), 1e-30)
        self.scale[0] = ROOM / most
        self.scale[1] = most * (1.0 / ROOM)

    def start(self, no):
        return self.facts[no // self.batches, lax.rem(no, self.batches)]

    def note(self, which, no, wanted):
        most = self.pot.shape[0] * 2
        many = self.facts[no // self.batches, self.batches + lax.rem(no, self.batches)] > CUT

        @pl.when(wanted)
        def _():
            have = self.counted[which]
            self.listed[which * most + have] = 2 * no
            self.listed[which * most + have + 1] = 2 * no + 1
            self.counted[which] = have + 1 + many.astype(jnp.int32)

    def copy(self, chunk):
        no, h = chunk // 2, lax.rem(chunk, 2)
        return pltpu.make_async_copy(
            self.phi.at[no // self.batches, lax.rem(no, self.batches), pl.ds(pl.multiple_of(h * CUT, CUT), CUT)],
            self.buf.at[chunk], self.sems.at[chunk])

    def fetch(self, which):
        @pl.loop(0, self.counted[which])
        def _(i):
            self.copy(self.listed[which * self.pot.shape[0] * 2 + i]).start()

    def group(self, which, at, size, rows):
        rights, highs, lows = [], [[] for _ in rows], [[] for _ in rows]
        scale = self.scale[0]
        for i in range(size):
            chunk = self.listed[which * self.pot.shape[0] * 2 + at + i]
            self.copy(chunk).wait()
            pots = self.pot[chunk // 2]
            pot = jnp.where(lax.rem(chunk, 2) == 0, pots[:PERTS], pots[PERTS:])
            rights.append(self.buf[chunk])
            for no, (row, _) in enumerate(rows):
                high, low = split_weights(pot, self.pick(chunk, row).astype(jnp.float32), scale)
                highs[no].append(high)
                lows[no].append(low)
        right = jnp.concatenate(rights, axis=0)
        left = jnp.concatenate([jnp.concatenate(high, axis=1) for high in highs], axis=0)
        total = jnp.dot(left, right, preferred_element_type=jnp.float32)
        low = jnp.concatenate([jnp.concatenate(low, axis=1) for low in lows], axis=0)
        rest = jnp.dot(low, right.astype(EIGHT), preferred_element_type=jnp.float32)
        total = total + rest * self.scale[1]
        depth = left.shape[0] // len(rows)
        for no, (_, spot) in enumerate(rows):
            spot[...] = spot[...] + total[no * depth:(no + 1) * depth].reshape(spot.shape)

    def add(self, which, rows):
        count = self.counted[which]
        size = LARGEST
        done = 0
        while size:
            times = (count - done) // size

            @pl.loop(0, times)
            def _(i, size=size, done=done):
                self.group(which, done + i * size, size, rows)

            done = done + times * size
            size //= 2


def fock_kernel(batches, share, facts_ref, pot_ref, picks_ref, phi_ref, out_ref,
                total, pot_v, picks_v, listed, counted, buf, sems, scale, in_sem, out_sem):
    grid_pos = lax.axis_index("grid")
    pot_copy = pltpu.make_async_copy(pot_ref, pot_v, in_sem.at[0])
    pot_copy.start()
    picks_copy = pltpu.make_async_copy(picks_ref, picks_v, in_sem.at[1])
    picks_copy.start()
    chunks = Chunks(batches, facts_ref, pot_v, lambda chunk, row: picks_v[chunk, row], phi_ref, listed, counted, buf, sems,
                    scale)
    base = 2 * grid_pos - REACH
    leads = REACH + 2

    for lead in range(leads):
        counted[lead] = 0

    @pl.loop(0, SLOTS * batches)
    def _(no):
        lead = chunks.start(no) - base
        chunks.note(lead, no, jnp.logical_and(lead >= 0, lead < leads))

    chunks.fetch(0)
    chunks.fetch(1)
    total[...] = jnp.zeros_like(total)
    pot_copy.wait()
    chunks.set_scale(pot_v[...])
    picks_copy.wait()

    def spot(r, offset):
        return total.at[r, :, :, pl.ds(pl.multiple_of((REACH - offset) * BLOCK, BLOCK), COLS)]

    def out_copy(r, t):
        cols = pl.ds(pl.multiple_of(t * BLOCK, BLOCK), BLOCK)
        return pltpu.make_async_copy(total.at[r, :, :, cols], out_ref.at[r, :, :, cols], out_sem.at[r, t])

    def leave(r, t):
        @pl.when(facts_ref[SLOTS + r, t] == 0)
        def _():
            cols = pl.ds(pl.multiple_of(t * BLOCK, BLOCK), BLOCK)
            total[r, :, :, cols] = jnp.zeros((PERTS, share, BLOCK), jnp.float32)

        out_copy(r, t).start()

    @pl.loop(0, leads)
    def _(lead):
        @pl.when(lead + 2 < leads)
        def _():
            chunks.fetch(lead + 2)

        both = jnp.logical_and(lead >= 1, lead <= REACH)

        @pl.when(both)
        def _():
            offset = REACH - lead
            chunks.add(lead, [(0, spot(0, offset)), (1, spot(1, offset + 1))])

        @pl.when(jnp.logical_not(both))
        def _():
            r = jnp.where(lead == 0, 0, 1)
            offset = jnp.where(lead == 0, REACH, 0)
            chunks.add(lead, [(r, spot(r, offset))])

        @pl.loop(lead, jnp.where(lead == REACH, BAND, jnp.minimum(lead + 1, REACH + 1)))
        def _(t):
            leave(0, t)

        @pl.loop(jnp.maximum(lead - 1, 0), jnp.where(lead == REACH + 1, BAND, lead))
        def _(t):
            leave(1, t)

    @pl.loop(0, BAND)
    def _(t):
        for r in range(2):
            out_copy(r, t).wait()


def chunk_scratch(slots, batches, cols, lists, dtype):
    most = 2 * slots * batches
    return [
        pltpu.SMEM((lists * most,), jnp.int32),
        pltpu.SMEM((lists,), jnp.int32),
        pltpu.VMEM((most, CUT, cols), dtype),
        pltpu.SemaphoreType.DMA((most,)),
        pltpu.SMEM((2,), jnp.float32),
    ]


def fock_own(facts, pot, picks, phi_all, share):
    slots, batches, points, cols = phi_all.shape
    far = pl.BlockSpec(memory_space=pl.ANY)
    whole = (2, PERTS, share, WIDE)
    dma = pltpu.SemaphoreType.DMA
    return pl.pallas_call(
        functools.partial(fock_kernel, batches, share),
        out_shape=jax.ShapeDtypeStruct(whole, jnp.float32),
        in_specs=[pl.BlockSpec(memory_space=pltpu.SMEM), far, far, far],
        out_specs=far,
        scratch_shapes=[
            pltpu.VMEM(whole, jnp.float32), pltpu.VMEM(pot.shape, pot.dtype), pltpu.VMEM(picks.shape, picks.dtype),
        ]
        + chunk_scratch(slots, batches, cols, REACH + 2, phi_all.dtype)
        + [dma((2,)), dma((2, BAND))],
        compiler_params=pltpu.CompilerParams(vmem_limit_bytes=56 << 20),
        cost_estimate=pl.CostEstimate(flops=20 * 10**9, bytes_accessed=20 * 10**6, transcendentals=0),
        name="fock_own",
    )(facts, pot, picks, phi_all)


def far_kernel(batches, facts_ref, pot_ref, picks_ref, phi_ref, out_ref, pot_v, picks_v, listed, counted, buf, sems, scale, in_sem):
    grid_pos = lax.axis_index("grid")
    core = lax.rem(grid_pos, 2)
    slot = jnp.where(core == 0, 4, 1)
    far_start = 4 * (grid_pos // 2) - 1
    own = pl.ds(slot * batches, batches)
    pot_copy = pltpu.make_async_copy(pot_ref.at[own], pot_v.at[own], in_sem.at[0])
    pot_copy.start()
    picks_copy = pltpu.make_async_copy(picks_ref, picks_v, in_sem.at[1])
    picks_copy.start()
    chunks = Chunks(batches, facts_ref, pot_v, lambda chunk, row: picks_v[chunk - 2 * batches * slot], phi_ref,
                    listed, counted, buf, sems, scale)
    counted[0] = 0

    @pl.loop(0, batches)
    def _(no):
        chunks.note(0, slot * batches + no, chunks.start(slot * batches + no) == far_start)

    chunks.fetch(0)
    out_ref[...] = jnp.zeros_like(out_ref)
    pot_copy.wait()
    chunks.set_scale(pot_v[own])
    picks_copy.wait()
    chunks.add(0, [(0, out_ref)])


def fock_far(facts, pot, far_picks, phi_all, share):
    slots, batches, points, cols = phi_all.shape
    smem = pl.BlockSpec(memory_space=pltpu.SMEM)
    far = pl.BlockSpec(memory_space=pl.ANY)
    vmem = pl.BlockSpec(memory_space=pltpu.VMEM)
    return pl.pallas_call(
        functools.partial(far_kernel, batches),
        out_shape=jax.ShapeDtypeStruct((PERTS, share, COLS), jnp.float32),
        in_specs=[smem, far, far, far],
        out_specs=vmem,
        scratch_shapes=[pltpu.VMEM(pot.shape, pot.dtype), pltpu.VMEM(far_picks.shape, far_picks.dtype)]
        + chunk_scratch(slots, batches, cols, 1, phi_all.dtype)
        + [pltpu.SemaphoreType.DMA((2,))],
        compiler_params=pltpu.CompilerParams(vmem_limit_bytes=56 << 20),
        cost_estimate=pl.CostEstimate(flops=10**9, bytes_accessed=2 * 10**6, transcendentals=0),
        name="fock_far",
    )(facts, pot, far_picks, phi_all)


def shards(density, basis_vals, kernel, starts, counts, pair_mask):
    grid_size, planes = lax.axis_size("grid"), lax.axis_size("basis")
    batches, share = basis_vals.shape[0], density.shape[2]
    grid_pos = lax.axis_index("grid")
    core = lax.rem(grid_pos, 2)
    phi_all, facts, pot, picks, far_picks = potentials(
        basis_vals, density, starts, counts, pair_mask.T, kernel, grid_size // 2, planes)
    pot = pot.reshape(SLOTS * batches, 2 * PERTS, POINTS // 2)
    picks = picks.reshape(2 * SLOTS * batches, 2, share, POINTS // 2)
    far_picks = far_picks.reshape(2 * batches, share, POINTS // 2)
    far = fock_far(facts, pot, far_picks, phi_all, share)
    route = [(i, (i + 1) % grid_size if i % 2 else (i - 1) % grid_size) for i in range(grid_size)]
    arrived = lax.ppermute(far, "grid", route)
    own = fock_own(facts, pot, picks, phi_all, share)
    mask_row = lax.dynamic_slice(pair_mask, (2 * grid_pos + core, core * REACH), (1, WINDOW))[0]
    keep = jnp.repeat(mask_row, BLOCK).astype(jnp.float32)
    place = (core, 0, 0, core * REACH * BLOCK)
    present = lax.dynamic_slice(own, place, (1, PERTS, share, COLS))
    return lax.dynamic_update_slice(own, present + (arrived * keep)[None], place)


def solution(mesh):
    placed = (
        P("grid", None, "basis", None),
        P("grid", None, None),
        P("grid", None),
        P("grid"),
        P("grid"),
        P(),
    )
    return jax.shard_map(
        shards,
        mesh=mesh,
        in_specs=placed,
        out_specs=P("grid", None, "basis", None),
        check_vma=False,
    )
```
